32 devices in a mesh: dp: 16 (over z, y, x), tensor: 2 (over core).
Axes of the slice: x: 2, y: 2, z: 4, core: 2. Of those that a mesh axis runs over, the one named last changes fastest.
Arguments:
- tokens: bfloat16 [16384, 1024], P(('dp', 'tensor')), may hold values from -6 to 6
- cotangent: bfloat16 [16384, 1024], P(('dp', 'tensor')), may hold values from -6 to 6
- species_ids: int32 [16], P('dp'), may hold values from 0 to 849, as said below
- species_counts: int32 [850], replicated, may hold values from 1000 to 15992
- norm1_gain: float32 [1024], replicated, may hold values from 0.1 to 1.9
- norm1_bias: float32 [1024], replicated, may hold values from -3 to 3
- w_query: bfloat16 [1024, 1024], P(None, 'tensor'), may hold values from -0.1875 to 0.1875
- w_key: bfloat16 [1024, 1024], P(None, 'tensor'), may hold values from -0.1875 to 0.1875
- w_value: bfloat16 [1024, 1024], P(None, 'tensor'), may hold values from -0.1875 to 0.1875
- w_out: bfloat16 [1024, 1024], P('tensor'), may hold values from -4 to 4
- norm2_gain: float32 [1024], replicated, may hold values from 0.1 to 1.9
- norm2_bias: float32 [1024], replicated, may hold values from -3 to 3
- w_gate: bfloat16 [1024, 4096], P(None, 'tensor'), may hold values from -0.1875 to 0.1875
- w_up: bfloat16 [1024, 4096], P(None, 'tensor'), may hold values from -0.1875 to 0.1875
- w_down: bfloat16 [4096, 1024], P('tensor'), may hold values from -0.09375 to 0.09375
Outputs:
- output: bfloat16 [16384, 1024], P(('dp', 'tensor'))
- input_grad: float32 [16384, 1024], P(('dp', 'tensor'))
- grad_norm1_gain: float32 [1024], replicated
- grad_norm1_bias: float32 [1024], replicated
- grad_query: float32 [1024, 1024], P(None, 'tensor')
- grad_key: float32 [1024, 1024], P(None, 'tensor')
- grad_value: float32 [1024, 1024], P(None, 'tensor')
- grad_out: float32 [1024, 1024], P('tensor')
- grad_norm2_gain: float32 [1024], replicated
- grad_norm2_bias: float32 [1024], replicated
- grad_gate: float32 [1024, 4096], P(None, 'tensor')
- grad_up: float32 [1024, 4096], P(None, 'tensor')
- grad_down: float32 [4096, 1024], P('tensor')
The draws below stay inside these ranges and needn't reach their ends.
Inputs may be any that keep to these rules, and one draw needn't show every extreme that they name: `species_ids`: each window's species, an index into species_counts; 0 and 849 are named in every draw.
All inputs are finite; a program needn't handle non-finite values.
Results may differ from the reference program's by a relative error of at most 0.02.
Values may be sent and summed in bfloat16 or wider, within the bound.
No kernel may reach another device: no remote copies, remote signals or barrier semaphores. Data moves between devices by JAX's collectives and lax.ppermute only.
A program may use at most 256 MiB of HBM per device.

```python
import jax
import jax.numpy as jnp
from jax import lax

D = 1024
HEADS = 16
HD = 64
FF = 4096
LEN = 1024
SPECIES = 850
WIN_DEV = 1
WINDOWS = 16
TOKENS = 16384
N_DP = 16


def draw_species_counts(key, part):
    base_count = jax.random.randint(jax.random.fold_in(key, 11), (SPECIES,), 1000, 2000)
    picked = jax.random.randint(jax.random.fold_in(key, 12), (2,), 0, SPECIES // 4)
    base_count = base_count.at[4 * picked[0] + 3].set(1999)
    base_count = base_count.at[4 * picked[1]].set(1000)
    levels = jnp.power(2, jnp.arange(SPECIES) % 4)
    return (base_count * levels).astype(jnp.int32)


def draw_species_ids(key, part):
    position = jnp.arange(WINDOWS) // WIN_DEV
    levels = 3 - 4 * position // N_DP
    picked = jax.random.randint(jax.random.fold_in(key, 21), (WINDOWS,), 0, SPECIES // 4)
    chosen = 4 * picked + levels
    chosen = chosen.at[N_DP // 2 * WIN_DEV].set(SPECIES - 1)
    chosen = chosen.at[WINDOWS - 1].set(0)
    return chosen.astype(jnp.int32)


def shard_levels(key, shape, split, least, high):
    gain, own = 1.0, jax.random.fold_in(key, 6)
    for axis_at, shards_of in split:
        steps = jnp.exp(jax.random.uniform(jax.random.fold_in(own, axis_at), (shards_of,), jnp.float32, least / len(split), high / len(split)))
        gain = gain * jnp.repeat(steps, shape[axis_at] // shards_of).reshape([-1 if axis == axis_at else 1 for axis in range(len(shape))])
    return gain


def gaussian(key, extent, spread, limit, shards=(), kind=jnp.bfloat16):
    entries = spread * jax.random.normal(key, extent, jnp.float32)
    if shards:
        entries = entries * shard_levels(key, extent, shards, -0.22, 0.18)
    return jnp.clip(entries, -limit, limit).astype(kind)


def setup_inputs(seed: int = 0) -> dict:
    key_of = jax.random.split(jax.random.key(seed), 16)
    tokens = gaussian(key_of[0], (TOKENS, D), 1.0, 6.0, ((0, 32),))
    cotangent = gaussian(key_of[1], (TOKENS, D), 1.0, 6.0, ((0, 32),))
    species_ids = draw_species_ids(jax.random.fold_in(key_of[15], 71), 0)
    species_counts = draw_species_counts(jax.random.fold_in(key_of[15], 71), 0)
    norm1_gain = jnp.clip(1.0 + 0.18 * jax.random.normal(key_of[4], (D,), jnp.float32), 0.1, 1.9)
    norm1_bias = gaussian(key_of[5], (D,), 0.5, 3.0, (), jnp.float32)
    w_query = gaussian(key_of[6], (D, D), D ** -0.5, 0.1875, ((1, 2),))
    w_key = gaussian(key_of[7], (D, D), D ** -0.5, 0.1875, ((1, 2),))
    w_value = gaussian(key_of[8], (D, D), D ** -0.5, 0.1875, ((1, 2),))
    w_out = gaussian(key_of[9], (D, D), (2 * D // LEN) ** -0.5, 4.0, ((0, 2),))
    norm2_gain = jnp.clip(1.0 + 0.18 * jax.random.normal(key_of[10], (D,), jnp.float32), 0.1, 1.9)
    norm2_bias = gaussian(key_of[11], (D,), 0.5, 3.0, (), jnp.float32)
    w_gate = gaussian(key_of[12], (D, FF), D ** -0.5, 0.1875, ((1, 2),))
    w_up = gaussian(key_of[13], (D, FF), D ** -0.5, 0.1875, ((1, 2),))
    w_down = gaussian(key_of[14], (FF, D), FF ** -0.5, 0.09375, ((0, 2),))
    return {"tokens": tokens, "cotangent": cotangent, "species_ids": species_ids, "species_counts": species_counts, "norm1_gain": norm1_gain, "norm1_bias": norm1_bias, "w_query": w_query, "w_key": w_key, "w_value": w_value, "w_out": w_out, "norm2_gain": norm2_gain, "norm2_bias": norm2_bias, "w_gate": w_gate, "w_up": w_up, "w_down": w_down}


@jax.custom_vjp
def low(v):
    return lax.optimization_barrier(v.astype(jnp.bfloat16)).astype(jnp.float32)

@jax.custom_vjp
def low_back(v):
    return v

def low_keep(v):
    return (low(v), None)

def low_pass(kept, grad):
    return (grad,)

def back_keep(v):
    return (v, None)

def back_low(kept, grad):
    return (low(grad),)
low.defvjp(low_keep, low_pass)
low_back.defvjp(back_keep, back_low)
precise = lax.Precision.HIGHEST
eps_norm = 1e-05

def dot_high(left_mat, right_mat):
    return jnp.dot(left_mat, right_mat, precision=precise)

def layer_norm(values, gain_vec, shift_vec):
    mean_val = lax.optimization_barrier(jnp.mean(values, axis=-1, keepdims=True))
    center = values - mean_val
    variance = lax.optimization_barrier(jnp.mean(center * center, axis=-1, keepdims=True))
    return center * lax.rsqrt(variance + eps_norm) * gain_vec + shift_vec

def rotary_tables():
    half_dim = HD // 2
    inv_freq = 1.0 / 10000.0 ** (jnp.arange(half_dim, dtype=jnp.float32) * 2.0 / HD)
    angles = jnp.arange(LEN, dtype=jnp.float32)[:, None] * inv_freq[None, :]
    angles = jnp.concatenate([angles, angles], axis=1)
    return (jnp.cos(angles), jnp.sin(angles))

def rotate_half(values):
    half_dim = values.shape[-1] // 2
    return jnp.concatenate([-values[..., half_dim:], values[..., :half_dim]], axis=-1)

def rotate(values, cos_tab, sin_tab):
    return values * cos_tab[:, None, :] + rotate_half(values) * sin_tab[:, None, :]

def window_attention(block_item):
    query, key_rot, value_low = block_item
    scores = low_back(jnp.einsum('qhd,khd->hqk', query, key_rot, precision=precise) * HD ** (-0.5))
    row_max = lax.optimization_barrier(jnp.max(scores, axis=-1, keepdims=True))
    exp_scores = jnp.exp(scores - row_max)
    probs = low(exp_scores / lax.optimization_barrier(jnp.sum(exp_scores, axis=-1, keepdims=True)))
    return jnp.einsum('hqk,khd->qhd', probs, value_low, precision=precise)

def block_forward(inputs, norm1_gain, norm1_bias, w_query, w_key, w_value, w_out, norm2_gain, norm2_bias, w_gate, w_up, w_down):
    row_total = inputs.shape[0]
    win_count = row_total // LEN
    cos_tab, sin_tab = rotary_tables()
    normed_in = low(layer_norm(inputs, norm1_gain, norm1_bias))

    def heads_of(values):
        return values.reshape(win_count, LEN, HEADS, HD)
    query = low(rotate(heads_of(low_back(dot_high(normed_in, w_query))), cos_tab, sin_tab))
    key_rot = low(rotate(heads_of(low_back(dot_high(normed_in, w_key))), cos_tab, sin_tab))
    value_low = heads_of(low(low_back(dot_high(normed_in, w_value))))
    context = lax.map(jax.checkpoint(window_attention), (query, key_rot, value_low))
    context = low(low_back(context.reshape(row_total, HEADS * HD)))
    mixed = inputs + low_back(dot_high(context, w_out))
    normed_mid = low(layer_norm(mixed, norm2_gain, norm2_bias))
    gate_pre = low_back(dot_high(normed_mid, w_gate))
    up_pre = low_back(dot_high(normed_mid, w_up))
    hidden = low(gate_pre * (1.0 / (1.0 + jnp.exp(-gate_pre))) * up_pre)
    return mixed + dot_high(hidden, w_down)

def reference(tokens, cotangent, species_ids, species_counts, norm1_gain, norm1_bias, w_query, w_key, w_value, w_out, norm2_gain, norm2_bias, w_gate, w_up, w_down):
    inverse = 1.0 / species_counts[species_ids].astype(jnp.float32)
    window_weight = WINDOWS * inverse / jnp.sum(inverse)
    row_weight = jnp.repeat(window_weight, LEN)
    scaled_grad = low(cotangent.astype(jnp.float32) * row_weight[:, None])
    params = tuple((weight_arg.astype(jnp.float32) for weight_arg in (norm1_gain, norm1_bias, w_query, w_key, w_value, w_out, norm2_gain, norm2_bias, w_gate, w_up, w_down)))
    per_step = 4 if WINDOWS % 4 == 0 else 1
    steps_count = WINDOWS // per_step
    input_steps = tokens.astype(jnp.float32).reshape(steps_count, per_step * LEN, D)
    grad_steps = scaled_grad.reshape(steps_count, per_step * LEN, D)

    def one_step(totals, inputs_pair):
        block_in, block_grad = inputs_pair
        result, pullback = jax.vjp(block_forward, block_in, *params)
        grads = pullback(block_grad)
        summed = tuple((running + update for running, update in zip(totals, grads[1:])))
        return (summed, (result, grads[0]))
    start_totals = tuple((jnp.zeros_like(weight_arg) for weight_arg in params))
    totals, (results, input_grads) = lax.scan(one_step, start_totals, (input_steps, grad_steps))
    return (results.reshape(TOKENS, D).astype(jnp.bfloat16), input_grads.reshape(TOKENS, D), totals[0], totals[1], totals[2], totals[3], totals[4], totals[5], totals[6], totals[7], totals[8], totals[9], totals[10])
```

```python
import functools
import math

import jax
import jax.numpy as jnp
from jax import lax
from jax.experimental import pallas as pl
from jax.experimental.pallas import tpu as pltpu
from jax.sharding import PartitionSpec as P

HD = 64
LEN = 1024
SPECIES = 850
LANES = 128

eps_norm = 1e-05
BF = jnp.bfloat16
F32 = jnp.float32
EXP_SCALE = HD ** (-0.5) * math.log2(math.e)
MIB = 1024 * 1024


def shape_of(dims, dtype):
    return jax.ShapeDtypeStruct(dims, dtype)


def dot_nn(left, right):
    return lax.dot_general(left, right, (((1,), (0,)), ((), ())), preferred_element_type=F32)


def dot_nt(left, right):
    return lax.dot_general(left, right, (((1,), (1,)), ((), ())), preferred_element_type=F32)


def dot_tn(left, right):
    return lax.dot_general(left, right, (((0,), (0,)), ((), ())), preferred_element_type=F32)


def row_norm(values):
    center = values - jnp.mean(values, axis=-1, keepdims=True)
    inv_std = lax.rsqrt(jnp.mean(center * center, axis=-1, keepdims=True) + eps_norm)
    return (center * inv_std, inv_std)


def norm_back(upstream, normed, inv_std, gain_vec):
    scaled_up = upstream * gain_vec
    mean_one = jnp.mean(scaled_up, axis=-1, keepdims=True)
    mean_two = jnp.mean(scaled_up * normed, axis=-1, keepdims=True)
    return inv_std * (scaled_up - mean_one - normed * mean_two)


def params(mib):
    return pltpu.CompilerParams(vmem_limit_bytes=mib * MIB)


def swap_halves(values):
    width = values.shape[1]
    lane = lax.broadcasted_iota(jnp.int32, values.shape, 1) % HD
    ahead = pltpu.roll(values, width - HD // 2, 1)
    behind = pltpu.roll(values, HD // 2, 1)
    return jnp.where(lane < HD // 2, ahead, behind)


def rope_tables(start):
    half_dim = HD // 2
    inv_freq = 1.0 / 10000.0 ** (jnp.arange(half_dim, dtype=F32) * 2.0 / HD)
    position = (start + jnp.arange(LEN, dtype=jnp.int32)) % LEN
    angles = position.astype(F32)[:, None] * inv_freq[None, :]
    cos_tab, sin_tab = jnp.cos(angles), jnp.sin(angles)
    return (
        jnp.concatenate([cos_tab] * 4, axis=1),
        jnp.concatenate([-sin_tab, sin_tab] * 2, axis=1),
    )


def project_kernel(own_ref, rest_ref, cos_ref, sin_ref, wq_ref, wk_ref, wv_ref, q_ref, k_ref, v_ref):
    own = own_ref.shape[0]
    for rows, x_ref in ((slice(0, own), own_ref), (slice(own, LEN), rest_ref)):
        x = x_ref[...]
        cos_tab, sin_tab = cos_ref[rows, :], sin_ref[rows, :]
        for w_ref, out_ref in ((wq_ref, q_ref), (wk_ref, k_ref)):
            lin = dot_nn(x, w_ref[...])
            for at in range(0, lin.shape[1], LANES):
                part = lin[:, at : at + LANES]
                turned = part * cos_tab + swap_halves(part) * sin_tab
                out_ref[rows, at : at + LANES] = turned.astype(BF)
        v_ref[rows, :] = dot_nn(x, wv_ref[...]).astype(BF)


def project(own, rest, cos_tab, sin_tab, w_query, w_key, w_value):
    cols = w_query.shape[1]
    block = min(256, cols)
    width = own.shape[1]
    whole = lambda a: pl.BlockSpec(a.shape, lambda i: (0, 0))
    w_spec = pl.BlockSpec((width, block), lambda i: (0, i))
    o_spec = pl.BlockSpec((LEN, block), lambda i: (0, i))
    return pl.pallas_call(
        project_kernel,
        grid=(cols // block,),
        in_specs=[whole(own), whole(rest), whole(cos_tab), whole(sin_tab), w_spec, w_spec, w_spec],
        out_specs=[o_spec] * 3,
        out_shape=[shape_of((LEN, cols), BF)] * 3,
        compiler_params=params(48),
        name="project",
    )(own, rest, cos_tab, sin_tab, w_query, w_key, w_value)


def head_only(values, head):
    lane = lax.broadcasted_iota(jnp.int32, values.shape, 1)
    return jnp.where(lane // HD == head, values, jnp.zeros_like(values))


def attend_kernel(q_ref, k_ref, v_ref, ctx_ref, lse_ref):
    k = k_ref[...]
    v_turned = v_ref[...].T
    parts = []
    for head in range(2):
        scores = dot_nt(k, head_only(q_ref[...], head))
        top = jnp.max(scores, axis=0, keepdims=True)
        exps = jnp.exp2((scores - top) * EXP_SCALE)
        total = jnp.sum(exps, axis=0, keepdims=True)
        mix = dot_nn(v_turned[head * HD : (head + 1) * HD, :], exps.astype(BF))
        parts.append(mix * (1.0 / total))
        lse_ref[0, head : head + 1, :] = top * EXP_SCALE + jnp.log2(total)
    ctx_ref[...] = jnp.concatenate(parts, axis=0).T.astype(BF)


def attend(query, key, value, first, count, tile):
    cols = query.shape[1]
    pairs = cols // LANES
    whole = pl.BlockSpec((LEN, LANES), lambda p, i: (0, p))
    return pl.pallas_call(
        attend_kernel,
        grid=(pairs, count // tile),
        in_specs=[pl.BlockSpec((tile, LANES), lambda p, i: (first // tile + i, p)), whole, whole],
        out_specs=[
            pl.BlockSpec((tile, LANES), lambda p, i: (i, p)),
            pl.BlockSpec((1, 2, tile), lambda p, i: (p, 0, i)),
        ],
        out_shape=[shape_of((count, cols), BF), shape_of((pairs, 2, count), F32)],
        compiler_params=params(48),
        name="attend",
    )(query, key, value)


def attend_back_kernel(
    tile, q_ref, k_ref, v_ref, d_ref, ctx_ref, lse_ref, cos_ref, sin_ref,
    dq_ref, dk_ref, dv_ref, dk_sum, dv_sum,
):
    scale = HD ** (-0.5)
    k, v = k_ref[...], v_ref[...]
    k_turned = k.T

    def unrotate(grads, rows):
        grads = grads * scale
        return (grads * cos_ref[rows, :] - swap_halves(grads) * sin_ref[rows, :]).astype(BF)

    dk_sum[...] = jnp.zeros_like(dk_sum)
    dv_sum[...] = jnp.zeros_like(dv_sum)

    def step(i, carry):
        at = pl.multiple_of(i * tile, tile)
        rows = pl.ds(at, tile)
        q, d = q_ref[rows, :], d_ref[rows, :]
        both = (d.astype(F32) * ctx_ref[rows, :].astype(F32)).T
        parts = []
        for head in range(2):
            q_head, d_head = head_only(q, head), head_only(d, head)
            delta = jnp.sum(both[head * HD : (head + 1) * HD, :], axis=0, keepdims=True)
            scores = dot_nt(k, q_head)
            probs = jnp.exp2(scores * EXP_SCALE - lse_ref[0, head : head + 1, rows])
            d_probs = dot_nt(v, d_head)
            d_scores = (probs * (d_probs - delta)).astype(BF)
            dv_sum[...] += dot_nn(probs.astype(BF), d_head)
            dk_sum[...] += dot_nn(d_scores, q_head)
            parts.append(dot_nn(k_turned[head * HD : (head + 1) * HD, :], d_scores))
        dq_ref[rows, :] = unrotate(jnp.concatenate(parts, axis=0).T, rows)
        return carry

    lax.fori_loop(0, LEN // tile, step, 0)
    everything = slice(0, LEN)
    dk_ref[...] = unrotate(dk_sum[...], everything)
    dv_ref[...] = dv_sum[...].astype(BF)


def attend_back(query, key, value, d_context, context, lse, cos_tab, sin_tab, tile=256):
    cols = query.shape[1]
    pairs = cols // LANES
    strip = pl.BlockSpec((LEN, LANES), lambda p: (0, p))
    table = pl.BlockSpec((LEN, LANES), lambda p: (0, 0))
    return pl.pallas_call(
        functools.partial(attend_back_kernel, tile),
        grid=(pairs,),
        in_specs=[strip] * 5 + [pl.BlockSpec((1, 2, LEN), lambda p: (p, 0, 0)), table, table],
        out_specs=[strip] * 3,
        out_shape=[shape_of((LEN, cols), BF)] * 3,
        scratch_shapes=[pltpu.VMEM((LEN, LANES), F32)] * 2,
        compiler_params=params(48),
        name="attend_back",
    )(query, key, value, d_context, context, lse, cos_tab, sin_tab)


def ff_kernel(
    n_pieces, slots_ref, nm_ref, nt_ref, sg_ref, wg_ref, wu_ref, wd_ref, *refs,
):
    hid_ref, dg_ref, du_ref, gd_ref, gg_ref, gu_ref, ht_ref = refs[-7:]
    width, block = wg_ref.shape
    tile = 256

    def forward(i, carry):
        rows = pl.ds(pl.multiple_of(i * tile, tile), tile)
        x = nm_ref[rows, :]
        gate = dot_nn(x, wg_ref[...])
        up = dot_nn(x, wu_ref[...])
        d_hidden = dot_nt(sg_ref[rows, :], wd_ref[...])
        sig = 1.0 / (1.0 + jnp.exp(-gate))
        silu = gate * sig
        hidden = (silu * up).astype(BF)
        hid_ref[rows, :] = hidden
        ht_ref[:, rows] = hidden.T
        dg_ref[rows, :] = (d_hidden * up * (sig * (1.0 + gate * (1.0 - sig)))).astype(BF)
        du_ref[rows, :] = (d_hidden * silu).astype(BF)
        return carry

    lax.fori_loop(0, LEN // tile, forward, 0)

    def weight_grad(which, left_ref, right_ref, out_ref):
        piece = out_ref.shape[0] // n_pieces
        step = max(tile, piece)
        per = step // piece

        def body(i, carry):
            rows = pl.ds(pl.multiple_of(i * step, step), step)
            grads = dot_nn(left_ref[rows, :], right_ref[...]).astype(BF)
            for j in range(per):
                at = pl.multiple_of(slots_ref[which, i * per + j] * piece, piece)
                out_ref[pl.ds(at, piece), :] = grads[j * piece : (j + 1) * piece, :]
            return carry

        lax.fori_loop(0, out_ref.shape[0] // step, body, 0)

    weight_grad(0, ht_ref, sg_ref, gd_ref)
    weight_grad(1, nt_ref, dg_ref, gg_ref)
    weight_grad(2, nt_ref, du_ref, gu_ref)


def feed_forward(index, block, n_pieces, slots, nm, nt, sg, w_gate, w_up, w_down, kept):
    width, units = w_gate.shape
    whole = pl.BlockSpec((LEN, width), lambda i, s: (0, 0))
    cols = pl.BlockSpec((width, block), lambda i, s: (0, index))
    kept_spec = pl.BlockSpec((LEN, block), lambda i, s: (0, index))
    grad = lambda dims: pl.BlockSpec(dims, lambda i, s: (0, 0))
    previous = list(kept) if kept is not None else []
    return pl.pallas_call(
        functools.partial(ff_kernel, n_pieces),
        grid_spec=pltpu.PrefetchScalarGridSpec(
            num_scalar_prefetch=1,
            grid=(1,),
            in_specs=[whole, pl.BlockSpec((width, LEN), lambda i, s: (0, 0)), whole, cols, cols,
                      pl.BlockSpec((block, width), lambda i, s: (index, 0))]
            + [pl.BlockSpec(memory_space=pl.ANY)] * len(previous),
            out_specs=[kept_spec] * 3 + [grad((block, width)), grad((width, block)), grad((width, block))],
            scratch_shapes=[pltpu.VMEM((block, LEN), BF)],
        ),
        out_shape=[shape_of((LEN, units), BF)] * 3
        + [shape_of((block, width), BF)] + [shape_of((width, block), BF)] * 2,
        input_output_aliases={7 + i: i for i in range(len(previous))},
        compiler_params=params(56),
        name="feed_forward",
    )(slots, nm, nt, sg, w_gate, w_up, w_down, *previous)


def orders_of(n_dp):
    bits = [1 << i for i in range(n_dp.bit_length() - 1)]
    if len(bits) < 4:
        return [bits] * 3
    a, b, c = bits[:3]
    return [[a, b, c] + bits[3:], [b, a, c] + bits[3:], [c, a, b] + bits[3:]]


def masks_of(order):
    size = 1 << len(order)
    masks = []
    for slot in range(size):
        mask = 0
        for level, bit in enumerate(order):
            if slot >> (len(order) - 1 - level) & 1:
                mask |= bit
        masks.append(mask)
    return masks


def slots_of(order, me):
    masks = masks_of(order)
    inverse = [0] * len(masks)
    for slot, mask in enumerate(masks):
        inverse[mask] = slot
    table = jnp.array(inverse, jnp.int32)
    return table[jnp.arange(len(masks), dtype=jnp.int32) ^ me]


def swap_dp(values, bit, n_dp):
    return lax.ppermute(values, "dp", [(i, i ^ bit) for i in range(n_dp)])


def sum_over_dp(values, order, n_dp):
    for bit in order:
        half = values.shape[0] // 2
        values = values[:half] + swap_dp(values[half:], bit, n_dp)
    for bit in order[::-1]:
        values = jnp.concatenate([values, swap_dp(values, bit, n_dp)], axis=0)
    return values


def place_kernel(pieces_ref, in_ref, *refs):
    refs[-1][...] = in_ref[...].astype(F32)


def place(summed, pieces, full_shape, block_index, base):
    n_pieces = pieces.shape[0]
    rows, cols = summed.shape
    piece = rows // n_pieces
    row_block, col_block = block_index
    given = [] if base is None else [base]
    return pl.pallas_call(
        place_kernel,
        grid_spec=pltpu.PrefetchScalarGridSpec(
            num_scalar_prefetch=1,
            grid=(n_pieces,),
            in_specs=[pl.BlockSpec((piece, cols), lambda i, s: (i, 0))]
            + [pl.BlockSpec(memory_space=pl.ANY)] * len(given),
            out_specs=pl.BlockSpec((piece, cols), lambda i, s: (row_block * n_pieces + s[i], col_block)),
        ),
        out_shape=shape_of(full_shape, F32),
        input_output_aliases={2: 0} if given else {},
        compiler_params=params(32),
        name="place",
    )(pieces, summed, *given)


def per_device(
    tokens,
    cotangent,
    species_ids,
    species_counts,
    norm1_gain,
    norm1_bias,
    w_query,
    w_key,
    w_value,
    w_out,
    norm2_gain,
    norm2_bias,
    w_gate,
    w_up,
    w_down,
):
    own, width = tokens.shape
    group = lax.axis_size("tensor")
    member = lax.axis_index("tensor")
    n_dp = lax.axis_size("dp")
    me = lax.axis_index("dp")
    rest = LEN - own
    units = w_gate.shape[1]
    block = min(512, units)
    hypercube = n_dp & (n_dp - 1) == 0

    def from_member(values, step):
        return lax.ppermute(values, "tensor", [((i + step) % group, i) for i in range(group)])

    def rest_rows(values):
        parts = [from_member(values, step) for step in range(1, group)]
        return parts[0] if group == 2 else jnp.concatenate(parts, axis=0)

    def to_owner(first, others):
        total = first
        for step in range(1, group):
            piece = others[(step - 1) * own : step * own].astype(BF)
            perm = [(i, (i + step) % group) for i in range(group)]
            total = total + lax.ppermute(piece, "tensor", perm).astype(F32)
        return total

    def rows_to_owner(partial):
        return to_owner(partial[:own], partial[own:])

    picked = species_ids[:, None] == jnp.arange(SPECIES, dtype=jnp.int32)[None, :]
    count = jnp.sum(jnp.where(picked, species_counts[None, :], 0), axis=1)
    inverse = jnp.broadcast_to(1.0 / count.astype(F32)[0], (1, LANES))
    inverse_sum = inverse
    if hypercube:
        for level in range(n_dp.bit_length() - 1):
            inverse_sum = inverse_sum + swap_dp(inverse_sum, 1 << level, n_dp)
    else:
        inverse_sum = lax.psum(inverse_sum, "dp")
    weight = (n_dp * inverse / inverse_sum)[:, :1]

    tok_own = tokens.astype(F32)
    normed1, inv1 = row_norm(tok_own)
    in_own = (normed1 * norm1_gain + norm1_bias).astype(BF)
    in_rest = rest_rows(in_own)
    cot_rest = rest_rows(cotangent)
    cos_tab, sin_tab = rope_tables(member * own)

    query, key, value = project(in_own, in_rest, cos_tab, sin_tab, w_query, w_key, w_value)
    ctx_rest, lse_rest = attend(query, key, value, own, rest, own)
    branch_rest = dot_nn(ctx_rest, w_out).astype(BF)
    ctx_own, lse_own = attend(query, key, value, 0, own, own)
    mixed = tok_own + to_owner(dot_nn(ctx_own, w_out), branch_rest)
    normed2, inv2 = row_norm(mixed)
    mid_own = (normed2 * norm2_gain + norm2_bias).astype(BF)
    mid_rest = rest_rows(mid_own)
    mid = jnp.concatenate([mid_own, mid_rest], axis=0)
    mid_turned = mid.T
    sg_own = (cotangent.astype(F32) * weight).astype(BF)
    sg = jnp.concatenate([sg_own, (cot_rest.astype(F32) * weight).astype(BF)], axis=0)

    orders = orders_of(n_dp) if hypercube else None
    masks = [jnp.array(masks_of(o), jnp.int32) ^ me for o in orders]
    slots = jnp.stack([slots_of(o, me) for o in orders])

    grads = []
    kept = None
    for index in range(units // block):
        *kept, g_down, g_gate, g_up = feed_forward(
            index, block, n_dp, slots, mid, mid_turned, sg, w_gate, w_up, w_down, kept
        )
        grads.append((g_down, g_gate, g_up))
    hidden, d_gate, d_up = kept

    summed = [[sum_over_dp(g, o, n_dp) for g, o in zip(trio, orders)] for trio in grads]

    d_mid = rows_to_owner(dot_nt(d_gate, w_gate) + dot_nt(d_up, w_up))
    gain2_sum = jnp.sum(d_mid * normed2, axis=0)
    bias2_sum = jnp.sum(d_mid, axis=0)
    d_mixed = sg_own.astype(F32) + norm_back(d_mid, normed2, inv2, norm2_gain)
    d_branch_own = d_mixed.astype(BF)
    d_branch = jnp.concatenate([d_branch_own, rest_rows(d_branch_own)], axis=0)
    context = jnp.concatenate([ctx_own, ctx_rest], axis=0)
    lse = jnp.concatenate([lse_own, lse_rest], axis=2)
    d_context = dot_nt(d_branch, w_out).astype(BF)
    d_query, d_key, d_value = attend_back(
        query, key, value, d_context, context, lse, cos_tab, sin_tab
    )
    normed_in = jnp.concatenate([in_own, in_rest], axis=0)
    grad_out = dot_tn(context, d_branch).astype(BF)
    late = [dot_tn(normed_in, d).astype(BF) for d in (d_query, d_key, d_value)]

    output = (mixed + rows_to_owner(dot_nn(hidden, w_down))).astype(BF)
    d_in = rows_to_owner(dot_nt(d_query, w_query) + dot_nt(d_key, w_key) + dot_nt(d_value, w_value))
    gain1_sum = jnp.sum(d_in * normed1, axis=0)
    bias1_sum = jnp.sum(d_in, axis=0)
    input_grad = d_mixed + norm_back(d_in, normed1, inv1, norm1_gain)

    vectors = jnp.stack([gain1_sum, bias1_sum, gain2_sum, bias2_sum])
    if hypercube:
        for level in range(n_dp.bit_length() - 1):
            vectors = vectors + swap_dp(vectors, 1 << level, n_dp)
        total = vectors
        for step in range(1, group):
            total = total + from_member(vectors, step)
        vectors = total
    else:
        vectors = lax.psum(vectors, ("dp", "tensor"))

    def small_sum(values, order_at):
        piece = values.shape[0] // n_dp
        if piece < 16:
            return lax.psum(values, "dp").astype(F32)
        order = orders[order_at]
        pieces = values.reshape(n_dp, piece, values.shape[1])
        rel = jnp.take(pieces, masks[order_at], axis=0).reshape(values.shape)
        return place(sum_over_dp(rel, order, n_dp), masks[order_at], values.shape, (0, 0), None)

    g_out = small_sum(grad_out, 2)
    g_query, g_key, g_value = (small_sum(g, at) for at, g in enumerate(late))
    g_down = g_gate = g_up = None
    for index, (s_down, s_gate, s_up) in enumerate(summed):
        g_down = place(s_down, masks[0], w_down.shape, (index, 0), g_down)
        g_gate = place(s_gate, masks[1], w_gate.shape, (0, index), g_gate)
        g_up = place(s_up, masks[2], w_up.shape, (0, index), g_up)
    return (
        output,
        input_grad,
        vectors[0],
        vectors[1],
        g_query,
        g_key,
        g_value,
        g_out,
        vectors[2],
        vectors[3],
        g_gate,
        g_up,
        g_down,
    )


def solution(mesh):
    split = P(("dp", "tensor"), None)
    cols = P(None, "tensor")
    rows = P("tensor", None)
    return jax.shard_map(
        per_device,
        mesh=mesh,
        in_specs=(split, split, P("dp"), P(), P(), P(), cols, cols, cols, rows, P(), P(), cols, cols, rows),
        out_specs=(split, split, P(), P(), cols, cols, cols, rows, P(), P(), cols, cols, rows),
        check_vma=False,
    )
```

```python
import functools
import math

import jax
import jax.numpy as jnp
from jax import lax
from jax.experimental import pallas as pl
from jax.experimental.pallas import tpu as pltpu
from jax.sharding import PartitionSpec as P

HD = 64
LEN = 1024
SPECIES = 850
LANES = 128

eps_norm = 1e-05
BF = jnp.bfloat16
F32 = jnp.float32
EXP_SCALE = HD ** (-0.5) * math.log2(math.e)
MIB = 1024 * 1024


def shape_of(dims, dtype):
    return jax.ShapeDtypeStruct(dims, dtype)


def dot_nn(left, right):
    return lax.dot_general(left, right, (((1,), (0,)), ((), ())), preferred_element_type=F32)


def dot_nt(left, right):
    return lax.dot_general(left, right, (((1,), (1,)), ((), ())), preferred_element_type=F32)


def dot_tn(left, right):
    return lax.dot_general(left, right, (((0,), (0,)), ((), ())), preferred_element_type=F32)


def row_norm(values):
    center = values - jnp.mean(values, axis=-1, keepdims=True)
    inv_std = lax.rsqrt(jnp.mean(center * center, axis=-1, keepdims=True) + eps_norm)
    return (center * inv_std, inv_std)


def norm_back(upstream, normed, inv_std, gain_vec):
    scaled_up = upstream * gain_vec
    mean_one = jnp.mean(scaled_up, axis=-1, keepdims=True)
    mean_two = jnp.mean(scaled_up * normed, axis=-1, keepdims=True)
    return inv_std * (scaled_up - mean_one - normed * mean_two)


def params(mib):
    return pltpu.CompilerParams(vmem_limit_bytes=mib * MIB)


def swap_halves(values):
    width = values.shape[1]
    lane = lax.broadcasted_iota(jnp.int32, values.shape, 1) % HD
    ahead = pltpu.roll(values, width - HD // 2, 1)
    behind = pltpu.roll(values, HD // 2, 1)
    return jnp.where(lane < HD // 2, ahead, behind)


def rope_tables(start):
    half_dim = HD // 2
    inv_freq = 1.0 / 10000.0 ** (jnp.arange(half_dim, dtype=F32) * 2.0 / HD)
    position = (start + jnp.arange(LEN, dtype=jnp.int32)) % LEN
    angles = position.astype(F32)[:, None] * inv_freq[None, :]
    cos_tab, sin_tab = jnp.cos(angles), jnp.sin(angles)
    return (
        jnp.concatenate([cos_tab] * 4, axis=1),
        jnp.concatenate([-sin_tab, sin_tab] * 2, axis=1),
    )


def project_kernel(own_ref, rest_ref, cos_ref, sin_ref, wq_ref, wk_ref, wv_ref, q_ref, k_ref, v_ref):
    own = own_ref.shape[0]
    for rows, x_ref in ((slice(0, own), own_ref), (slice(own, LEN), rest_ref)):
        x = x_ref[...]
        cos_tab, sin_tab = cos_ref[rows, :], sin_ref[rows, :]
        for w_ref, out_ref in ((wq_ref, q_ref), (wk_ref, k_ref)):
            lin = dot_nn(x, w_ref[...])
            for at in range(0, lin.shape[1], LANES):
                part = lin[:, at : at + LANES]
                turned = part * cos_tab + swap_halves(part) * sin_tab
                out_ref[rows, at : at + LANES] = turned.astype(BF)
        v_ref[rows, :] = dot_nn(x, wv_ref[...]).astype(BF)


def project(own, rest, cos_tab, sin_tab, w_query, w_key, w_value):
    cols = w_query.shape[1]
    block = min(256, cols)
    width = own.shape[1]
    whole = lambda a: pl.BlockSpec(a.shape, lambda i: (0, 0))
    w_spec = pl.BlockSpec((width, block), lambda i: (0, i))
    o_spec = pl.BlockSpec((LEN, block), lambda i: (0, i))
    return pl.pallas_call(
        project_kernel,
        grid=(cols // block,),
        in_specs=[whole(own), whole(rest), whole(cos_tab), whole(sin_tab), w_spec, w_spec, w_spec],
        out_specs=[o_spec] * 3,
        out_shape=[shape_of((LEN, cols), BF)] * 3,
        compiler_params=params(48),
        name="project",
    )(own, rest, cos_tab, sin_tab, w_query, w_key, w_value)


def head_only(values, head):
    lane = lax.broadcasted_iota(jnp.int32, values.shape, 1)
    return jnp.where(lane // HD == head, values, jnp.zeros_like(values))


def attend_kernel(q_ref, k_ref, v_ref, ctx_ref, lse_ref):
    k = k_ref[...]
    v_turned = v_ref[...].T
    parts = []
    for head in range(2):
        scores = dot_nt(k, head_only(q_ref[...], head))
        top = jnp.max(scores, axis=0, keepdims=True)
        exps = jnp.exp2((scores - top) * EXP_SCALE)
        total = jnp.sum(exps, axis=0, keepdims=True)
        mix = dot_nn(v_turned[head * HD : (head + 1) * HD, :], exps.astype(BF))
        parts.append(mix * (1.0 / total))
        lse_ref[0, head : head + 1, :] = top * EXP_SCALE + jnp.log2(total)
    ctx_ref[...] = jnp.concatenate(parts, axis=0).T.astype(BF)


def attend(query, key, value, first, count, tile):
    cols = query.shape[1]
    pairs = cols // LANES
    whole = pl.BlockSpec((LEN, LANES), lambda p, i: (0, p))
    return pl.pallas_call(
        attend_kernel,
        grid=(pairs, count // tile),
        in_specs=[pl.BlockSpec((tile, LANES), lambda p, i: (first // tile + i, p)), whole, whole],
        out_specs=[
            pl.BlockSpec((tile, LANES), lambda p, i: (i, p)),
            pl.BlockSpec((1, 2, tile), lambda p, i: (p, 0, i)),
        ],
        out_shape=[shape_of((count, cols), BF), shape_of((pairs, 2, count), F32)],
        compiler_params=params(48),
        name="attend",
    )(query, key, value)


def attend_back_kernel(
    tile, q_ref, k_ref, v_ref, d_ref, ctx_ref, lse_ref, cos_ref, sin_ref,
    dq_ref, dk_ref, dv_ref, dk_sum, dv_sum,
):
    scale = HD ** (-0.5)
    k, v = k_ref[...], v_ref[...]
    k_turned = k.T

    def unrotate(grads, rows):
        grads = grads * scale
        return (grads * cos_ref[rows, :] - swap_halves(grads) * sin_ref[rows, :]).astype(BF)

    dk_sum[...] = jnp.zeros_like(dk_sum)
    dv_sum[...] = jnp.zeros_like(dv_sum)

    def step(i, carry):
        at = pl.multiple_of(i * tile, tile)
        rows = pl.ds(at, tile)
        q, d = q_ref[rows, :], d_ref[rows, :]
        both = (d.astype(F32) * ctx_ref[rows, :].astype(F32)).T
        parts = []
        for head in range(2):
            q_head, d_head = head_only(q, head), head_only(d, head)
            delta = jnp.sum(both[head * HD : (head + 1) * HD, :], axis=0, keepdims=True)
            scores = dot_nt(k, q_head)
            probs = jnp.exp2(scores * EXP_SCALE - lse_ref[0, head : head + 1, rows])
            d_probs = dot_nt(v, d_head)
            d_scores = (probs * (d_probs - delta)).astype(BF)
            dv_sum[...] += dot_nn(probs.astype(BF), d_head)
            dk_sum[...] += dot_nn(d_scores, q_head)
            parts.append(dot_nn(k_turned[head * HD : (head + 1) * HD, :], d_scores))
        dq_ref[rows, :] = unrotate(jnp.concatenate(parts, axis=0).T, rows)
        return carry

    lax.fori_loop(0, LEN // tile, step, 0)
    everything = slice(0, LEN)
    dk_ref[...] = unrotate(dk_sum[...], everything)
    dv_ref[...] = dv_sum[...].astype(BF)


def attend_back(query, key, value, d_context, context, lse, cos_tab, sin_tab, at, cols, tile=256):
    pairs = cols // LANES
    first = at * pairs
    strip = pl.BlockSpec((LEN, LANES), lambda p: (0, first + p))
    result = pl.BlockSpec((LEN, LANES), lambda p: (0, p))
    table = pl.BlockSpec((LEN, LANES), lambda p: (0, 0))
    return pl.pallas_call(
        functools.partial(attend_back_kernel, tile),
        grid=(pairs,),
        in_specs=[strip] * 5 + [pl.BlockSpec((1, 2, LEN), lambda p: (first + p, 0, 0)), table, table],
        out_specs=[result] * 3,
        out_shape=[shape_of((LEN, cols), BF)] * 3,
        scratch_shapes=[pltpu.VMEM((LEN, LANES), F32)] * 2,
        compiler_params=params(48),
        name="attend_back",
    )(query, key, value, d_context, context, lse, cos_tab, sin_tab)


def ff_kernel(
    n_pieces, slots_ref, nm_ref, nt_ref, sg_ref, wg_ref, wu_ref, wd_ref, *refs,
):
    hid_ref, dg_ref, du_ref, gd_ref, ga_ref, gb_ref, ht_ref = refs[-7:]
    width, block = wg_ref.shape
    tile = 256

    def forward(i, carry):
        rows = pl.ds(pl.multiple_of(i * tile, tile), tile)
        x = nm_ref[rows, :]
        gate = dot_nn(x, wg_ref[...])
        up = dot_nn(x, wu_ref[...])
        d_hidden = dot_nt(sg_ref[rows, :], wd_ref[...])
        sig = 1.0 / (1.0 + jnp.exp(-gate))
        silu = gate * sig
        hidden = (silu * up).astype(BF)
        hid_ref[rows, :] = hidden
        ht_ref[:, rows] = hidden.T
        dg_ref[rows, :] = (d_hidden * up * (sig * (1.0 + gate * (1.0 - sig)))).astype(BF)
        du_ref[rows, :] = (d_hidden * silu).astype(BF)
        return carry

    lax.fori_loop(0, LEN // tile, forward, 0)

    def weight_grad(which, left_ref, first, count, right_refs, out_ref):
        piece = count // n_pieces
        step = max(tile, piece)
        per = step // piece

        def body(i, carry):
            rows = pl.ds(pl.multiple_of(first + i * step, step), step)
            left = left_ref[rows, :]
            at_lane = 0
            for right_ref in right_refs:
                grads = dot_nn(left, right_ref[...]).astype(BF)
                lanes = slice(at_lane, at_lane + grads.shape[1])
                for j in range(per):
                    at = pl.multiple_of(slots_ref[which, i * per + j] * piece, piece)
                    out_ref[pl.ds(at, piece), lanes] = grads[j * piece : (j + 1) * piece, :]
                at_lane = lanes.stop
            return carry

        lax.fori_loop(0, count // step, body, 0)

    half = width // 2
    weight_grad(0, ht_ref, 0, block, [sg_ref], gd_ref)
    weight_grad(1, nt_ref, 0, half, [dg_ref, du_ref], ga_ref)
    weight_grad(2, nt_ref, half, half, [dg_ref, du_ref], gb_ref)


def feed_forward(index, block, n_pieces, slots, nm, nt, sg, w_gate, w_up, w_down, kept):
    width, units = w_gate.shape
    whole = pl.BlockSpec((LEN, width), lambda i, s: (0, 0))
    cols = pl.BlockSpec((width, block), lambda i, s: (0, index))
    kept_spec = pl.BlockSpec((LEN, block), lambda i, s: (0, index))
    grad = lambda dims: pl.BlockSpec(dims, lambda i, s: (0, 0))
    chunks = [(block, width), (width // 2, 2 * block), (width // 2, 2 * block)]
    previous = list(kept) if kept is not None else []
    return pl.pallas_call(
        functools.partial(ff_kernel, n_pieces),
        grid_spec=pltpu.PrefetchScalarGridSpec(
            num_scalar_prefetch=1,
            grid=(1,),
            in_specs=[whole, pl.BlockSpec((width, LEN), lambda i, s: (0, 0)), whole, cols, cols,
                      pl.BlockSpec((block, width), lambda i, s: (index, 0))]
            + [pl.BlockSpec(memory_space=pl.ANY)] * len(previous),
            out_specs=[kept_spec] * 3 + [grad(dims) for dims in chunks],
            scratch_shapes=[pltpu.VMEM((block, LEN), BF)],
        ),
        out_shape=[shape_of((LEN, units), BF)] * 3
        + [shape_of(dims, BF) for dims in chunks],
        input_output_aliases={7 + i: i for i in range(len(previous))},
        compiler_params=params(56),
        name="feed_forward",
    )(slots, nm, nt, sg, w_gate, w_up, w_down, *previous)


def orders_of(n_dp):
    bits = [1 << i for i in range(n_dp.bit_length() - 1)]
    if len(bits) < 4:
        return [bits] * 4
    a, b, c = bits[:3]
    return [o + bits[3:] for o in ([a, b, c], [b, a, c], [c, a, b], [c, b, a])]


def masks_of(order):
    size = 1 << len(order)
    masks = []
    for slot in range(size):
        mask = 0
        for level, bit in enumerate(order):
            if slot >> (len(order) - 1 - level) & 1:
                mask |= bit
        masks.append(mask)
    return masks


def slots_of(orders, me):
    table = []
    for order in orders:
        inverse = [0] * (1 << len(order))
        for slot, mask in enumerate(masks_of(order)):
            inverse[mask] = slot
        table.append(inverse)
    size = len(table[0])
    here = jnp.arange(size, dtype=jnp.int32) ^ me
    match = here[:, None] == jnp.arange(size, dtype=jnp.int32)[None, :]
    return jnp.stack([jnp.sum(jnp.where(match, jnp.array(t, jnp.int32)[None, :], 0), axis=1) for t in table])


def swap_dp(values, bit, n_dp):
    return lax.ppermute(values, "dp", [(i, i ^ bit) for i in range(n_dp)])


class Chunk:
    def __init__(self, values, order, done):
        self.order, self.done = list(order), done
        self.current, self.rows = values, values.shape[0]
        self.at, self.last, self.parts = 0, -9, []

    @property
    def open(self):
        return self.at < 2 * len(self.order)

    @property
    def bit(self):
        return (self.order + self.order[::-1])[self.at]

    def next_rows(self):
        levels = len(self.order)
        return self.rows >> (self.at + 1 if self.at < levels else 2 * levels - self.at)

    def outgoing(self):
        if self.at < len(self.order):
            return [self.current[self.current.shape[0] // 2 :]]
        return self.parts

    def incoming(self, got):
        self.at += 1
        if self.at <= len(self.order):
            self.current = self.current[: self.current.shape[0] // 2] + got
            self.parts = [self.current]
        else:
            self.parts = self.parts + [got]


def in_rounds(work, chunks, n_dp, limit):
    placing = []
    wanted = next(work)
    before = None
    now = 0

    def finish(picks, got):
        for bit, members in picks.items():
            at = 0
            for chunk in members:
                rows = chunk.next_rows()
                chunk.incoming(got[bit][at : at + rows])
                at += rows
                if not chunk.open:
                    placing.append(chunk)

    while wanted is not None or before is not None or any(c.open for c in chunks):
        picks, loads = {}, {}
        for chunk in chunks:
            if not chunk.open or chunk.last > now - 2:
                continue
            bit, rows = chunk.bit, chunk.next_rows()
            if loads.get(bit, 0) and loads[bit] + rows > limit:
                continue
            loads[bit] = loads.get(bit, 0) + rows
            picks.setdefault(bit, []).append(chunk)
            chunk.last = now
        sends = {}
        for bit in sorted(picks):
            parts = [part for chunk in picks[bit] for part in chunk.outgoing()]
            sends[bit] = parts[0] if len(parts) == 1 else jnp.concatenate(parts, axis=0)
        ready = [jnp.concatenate(c.parts, axis=0) for c in placing]
        held = (before[1] if before else {}, sends, ready, wanted)
        got, tied_sends, ready, wanted = lax.optimization_barrier(held)
        taken = {bit: swap_dp(values, bit, n_dp) for bit, values in sends.items()}
        finished, placing = placing, []
        if before:
            finish(before[0], got)
        for chunk, values in zip(finished, ready):
            chunk.done(values)
        if wanted is not None:
            try:
                wanted = work.send(wanted)
            except StopIteration:
                wanted = None
        before = (picks, taken) if picks else None
        now += 1
        if not picks and placing:
            for chunk in placing:
                chunk.done(jnp.concatenate(chunk.parts, axis=0))
            placing = []


def place_kernel(slots_ref, which, n_pieces, folds, in_ref, *refs):
    outs = refs[-max(fold[2] for fold in folds) - 1 :]
    piece = in_ref.shape[0] // n_pieces
    for p in range(n_pieces):
        at = pl.multiple_of(slots_ref[which, p] * piece, piece)
        rows = in_ref[pl.ds(at, piece), :].astype(F32)
        for lane, end, out, row, col in folds:
            width = end - lane
            outs[out][row + p * piece : row + (p + 1) * piece, col : col + width] = rows[:, lane:end]


def place(values, slots, which, n_pieces, folds, blocks, bases):
    given = [base for base in bases if base is not None]
    index_map = lambda at: (lambda i, s: at)
    return pl.pallas_call(
        lambda s, i, *refs: place_kernel(s, which, n_pieces, folds, i, *refs),
        grid_spec=pltpu.PrefetchScalarGridSpec(
            num_scalar_prefetch=1,
            grid=(1,),
            in_specs=[pl.BlockSpec(values.shape, lambda i, s: (0, 0))]
            + [pl.BlockSpec(memory_space=pl.ANY)] * len(given),
            out_specs=[pl.BlockSpec(dims, index_map(at)) for _, dims, at in blocks],
        ),
        out_shape=[shape_of(full, F32) for full, _, _ in blocks],
        input_output_aliases={2 + i: i for i in range(len(given))},
        compiler_params=params(32),
        name="place",
    )(slots, values, *given)


def late_kernel(n_pieces, slots_ref, nt_ref, dq_ref, dk_ref, dv_ref, *out_refs):
    width = nt_ref.shape[0]
    cols = dq_ref.shape[1]
    rows = out_refs[0].shape[0]
    piece = rows // n_pieces

    def body(i, carry):
        left = nt_ref[pl.ds(pl.multiple_of(i * rows, rows), rows), :]
        for which, (d_ref, out_ref) in enumerate(zip((dq_ref, dk_ref, dv_ref), out_refs)):
            grads = dot_nn(left, d_ref[...]).astype(BF)
            for p in range(n_pieces):
                at = pl.multiple_of(slots_ref[which, p] * piece, piece)
                out_ref[pl.ds(at, piece), pl.ds(pl.multiple_of(i * cols, cols), cols)] = grads[
                    p * piece : (p + 1) * piece, :
                ]
        return carry

    lax.fori_loop(0, width // rows, body, 0)


def late_grads(slots, n_pieces, turned, d_query, d_key, d_value):
    width = turned.shape[0]
    cols = d_query.shape[1]
    rows = width * cols // 1024
    whole = lambda a: pl.BlockSpec(a.shape, lambda i, s: (0, 0))
    return pl.pallas_call(
        functools.partial(late_kernel, n_pieces),
        grid_spec=pltpu.PrefetchScalarGridSpec(
            num_scalar_prefetch=1,
            grid=(1,),
            in_specs=[whole(turned)] + [whole(d_query)] * 3,
            out_specs=[pl.BlockSpec((rows, 1024), lambda i, s: (0, 0))] * 3,
        ),
        out_shape=[shape_of((rows, 1024), BF)] * 3,
        compiler_params=params(48),
        name="late_grads",
    )(slots, turned, d_query, d_key, d_value)


def out_grad_kernel(n_pieces, slots_ref, ct_ref, d_ref, out_ref):
    rows = ct_ref.shape[0]
    piece = rows // n_pieces
    step = max(256, piece)
    per = step // piece

    def body(i, carry):
        left = ct_ref[pl.ds(pl.multiple_of(i * step, step), step), :]
        grads = dot_nn(left, d_ref[...]).astype(BF)
        for j in range(per):
            at = pl.multiple_of(slots_ref[3, i * per + j] * piece, piece)
            out_ref[pl.ds(at, piece), :] = grads[j * piece : (j + 1) * piece, :]
        return carry

    lax.fori_loop(0, rows // step, body, 0)


def out_grad(slots, n_pieces, turned, d_branch):
    whole = lambda a: pl.BlockSpec(a.shape, lambda i, s: (0, 0))
    return pl.pallas_call(
        functools.partial(out_grad_kernel, n_pieces),
        grid_spec=pltpu.PrefetchScalarGridSpec(
            num_scalar_prefetch=1,
            grid=(1,),
            in_specs=[whole(turned), whole(d_branch)],
            out_specs=pl.BlockSpec(turned.shape, lambda i, s: (0, 0)),
        ),
        out_shape=shape_of(turned.shape, BF),
        compiler_params=params(48),
        name="out_grad",
    )(slots, turned, d_branch)


def per_device(
    tokens,
    cotangent,
    species_ids,
    species_counts,
    norm1_gain,
    norm1_bias,
    w_query,
    w_key,
    w_value,
    w_out,
    norm2_gain,
    norm2_bias,
    w_gate,
    w_up,
    w_down,
):
    own, width = tokens.shape
    group = lax.axis_size("tensor")
    member = lax.axis_index("tensor")
    n_dp = lax.axis_size("dp")
    me = lax.axis_index("dp")
    rest = LEN - own
    units = w_gate.shape[1]
    block = min(512, units)
    head_cols = w_query.shape[1]
    own_out_rows = w_out.shape[0]

    def from_member(values, step):
        return lax.ppermute(values, "tensor", [((i + step) % group, i) for i in range(group)])

    def rest_rows(values):
        parts = [from_member(values, step) for step in range(1, group)]
        return parts[0] if group == 2 else jnp.concatenate(parts, axis=0)

    def to_owner(first, others):
        total = first
        for step in range(1, group):
            piece = others[(step - 1) * own : step * own].astype(BF)
            perm = [(i, (i + step) % group) for i in range(group)]
            total = total + lax.ppermute(piece, "tensor", perm).astype(F32)
        return total

    def rows_to_owner(partial):
        return to_owner(partial[:own], partial[own:])

    picked = species_ids[:, None] == jnp.arange(SPECIES, dtype=jnp.int32)[None, :]
    count = jnp.sum(jnp.where(picked, species_counts[None, :], 0), axis=1)
    inverse = jnp.broadcast_to(1.0 / count.astype(F32)[0], (1, LANES))
    inverse_sum = inverse
    for level in range(n_dp.bit_length() - 1):
        inverse_sum = inverse_sum + swap_dp(inverse_sum, 1 << level, n_dp)
    weight = (n_dp * inverse / inverse_sum)[:, :1]

    tok_own = tokens.astype(F32)
    normed1, inv1 = row_norm(tok_own)
    in_own = (normed1 * norm1_gain + norm1_bias).astype(BF)
    in_rest = rest_rows(in_own)
    cot_rest = rest_rows(cotangent)
    cos_tab, sin_tab = rope_tables(member * own)

    query, key, value = project(in_own, in_rest, cos_tab, sin_tab, w_query, w_key, w_value)
    ctx_rest, lse_rest = attend(query, key, value, own, rest, own)
    branch_rest = dot_nn(ctx_rest, w_out).astype(BF)
    ctx_own, lse_own = attend(query, key, value, 0, own, own)
    mixed = tok_own + to_owner(dot_nn(ctx_own, w_out), branch_rest)
    normed2, inv2 = row_norm(mixed)
    mid_own = (normed2 * norm2_gain + norm2_bias).astype(BF)
    mid_rest = rest_rows(mid_own)
    mid = jnp.concatenate([mid_own, mid_rest], axis=0)
    mid_turned = mid.T
    sg_own = (cotangent.astype(F32) * weight).astype(BF)
    sg = jnp.concatenate([sg_own, (cot_rest.astype(F32) * weight).astype(BF)], axis=0)

    orders = orders_of(n_dp)
    slots = slots_of(orders, me)
    chunks, found = [], {}
    late_fits = width * min(256, head_cols) // 1024 >= 16 * n_dp and own_out_rows >= 16 * n_dp

    def send_off(values, which, folds, blocks, names):
        def done(summed):
            bases = [found.get(name) for name in names]
            results = place(summed, slots, which, n_dp, folds, blocks, bases)
            found.update(zip(names, results))

        chunks.append(Chunk(values, orders[which], done))

    def work():
        kept = None
        gate_slots = slots
        for index in range(units // block):
            *kept, g_down, g_first, g_second = feed_forward(
                index, block, n_dp, gate_slots, mid, mid_turned, sg, w_gate, w_up, w_down, kept
            )
            send_off(
                g_down, 0, [(0, width, 0, 0, 0)], [(w_down.shape, (block, width), (index, 0))], ["down"]
            )
            for at, values in enumerate((g_first, g_second)):
                dims = (width // 2, block)
                folds = [(0, block, 0, 0, 0), (block, 2 * block, 1, 0, 0)]
                blocks = [(w.shape, dims, (at, index)) for w in (w_gate, w_up)]
                send_off(values, 1 + at, folds, blocks, ["gate", "up"])
            gate_slots, kept = yield (gate_slots, kept)
        hidden, d_gate, d_up = kept
        d_mid_part = dot_nt(d_gate, w_gate) + dot_nt(d_up, w_up)
        d_mid_part, hidden = yield (d_mid_part, hidden)
        d_mid = rows_to_owner(d_mid_part)
        out_part = dot_nn(hidden, w_down)
        d_mid, out_part = yield (d_mid, out_part)
        found["output"] = (mixed + rows_to_owner(out_part)).astype(BF)
        gain2_sum = jnp.sum(d_mid * normed2, axis=0)
        bias2_sum = jnp.sum(d_mid, axis=0)
        d_mixed = sg_own.astype(F32) + norm_back(d_mid, normed2, inv2, norm2_gain)
        d_branch_own = d_mixed.astype(BF)
        d_branch = jnp.concatenate([d_branch_own, rest_rows(d_branch_own)], axis=0)
        (d_branch,) = yield (d_branch,)
        context = jnp.concatenate([ctx_own, ctx_rest], axis=0)
        lse = jnp.concatenate([lse_own, lse_rest], axis=2)
        d_context = dot_nt(d_branch, w_out).astype(BF)
        normed_in = jnp.concatenate([in_own, in_rest], axis=0)
        in_turned = normed_in.T
        if late_fits:
            send_off(
                out_grad(slots, n_dp, context.T, d_branch), 3, [(0, width, 0, 0, 0)],
                [(w_out.shape, w_out.shape, (0, 0))], ["out"],
            )
        else:
            found["out"] = lax.psum(dot_tn(context, d_branch).astype(BF), "dp").astype(F32)
        cols = min(256, head_cols)
        d_in_part = 0.0
        for at in range(head_cols // cols):
            d_context, d_in_part = yield (d_context, d_in_part)
            strip = slice(at * cols, (at + 1) * cols)
            backs = attend_back(query, key, value, d_context, context, lse, cos_tab, sin_tab, at, cols)
            if late_fits:
                rows = width * cols // 1024
                folds = [(i * cols, (i + 1) * cols, 0, i * rows, 0) for i in range(width // rows)]
                late = late_grads(slots, n_dp, in_turned, *backs)
                for which, (name, values) in enumerate(zip(("query", "key", "value"), late)):
                    blocks = [(w_query.shape, (width, cols), (0, at))]
                    send_off(values, which, folds, blocks, [name])
            else:
                for name, d in zip(("query", "key", "value"), backs):
                    summed = lax.psum(dot_tn(normed_in, d).astype(BF), "dp").astype(F32)
                    found.setdefault(name, []).append(summed)
            for d, w in zip(backs, (w_query, w_key, w_value)):
                d_in_part = d_in_part + dot_nt(d, w[:, strip])
        (d_in_part,) = yield (d_in_part,)
        d_in = rows_to_owner(d_in_part)
        gain1_sum = jnp.sum(d_in * normed1, axis=0)
        bias1_sum = jnp.sum(d_in, axis=0)
        found["input"] = d_mixed + norm_back(d_in, normed1, inv1, norm1_gain)
        vectors = jnp.stack([gain1_sum, bias1_sum, gain2_sum, bias2_sum])
        total = vectors
        for step in range(1, group):
            total = total + from_member(vectors, step)
        for level in range(n_dp.bit_length() - 1):
            (total,) = yield (total,)
            total = total + swap_dp(total, 1 << level, n_dp)
        found["vectors"] = total

    in_rounds(work(), chunks, n_dp, 512)
    vectors = found["vectors"]
    return (
        found["output"],
        found["input"],
        vectors[0],
        vectors[1],
        *(found[n] if late_fits else jnp.concatenate(found[n], axis=1) for n in ("query", "key", "value")),
        found["out"],
        vectors[2],
        vectors[3],
        found["gate"],
        found["up"],
        found["down"],
    )


def solution(mesh):
    split = P(("dp", "tensor"), None)
    cols = P(None, "tensor")
    rows = P("tensor", None)
    return jax.shard_map(
        per_device,
        mesh=mesh,
        in_specs=(split, split, P("dp"), P(), P(), P(), cols, cols, cols, rows, P(), P(), cols, cols, rows),
        out_specs=(split, split, P(), P(), cols, cols, cols, rows, P(), P(), cols, cols, rows),
        check_vma=False,
    )
```

```python
import functools
import math

import jax
import jax.numpy as jnp
from jax import lax
from jax.experimental import pallas as pl
from jax.experimental.pallas import tpu as pltpu
from jax.sharding import PartitionSpec as P

HD = 64
LEN = 1024
SPECIES = 850
LANES = 128

eps_norm = 1e-05
BF = jnp.bfloat16
F32 = jnp.float32
EXP_SCALE = HD ** (-0.5) * math.log2(math.e)
MIB = 1024 * 1024


def shape_of(dims, dtype):
    return jax.ShapeDtypeStruct(dims, dtype)


def dot_nn(left, right):
    return lax.dot_general(left, right, (((1,), (0,)), ((), ())), preferred_element_type=F32)


def dot_nt(left, right):
    return lax.dot_general(left, right, (((1,), (1,)), ((), ())), preferred_element_type=F32)


def dot_tn(left, right):
    return lax.dot_general(left, right, (((0,), (0,)), ((), ())), preferred_element_type=F32)


def row_norm(values):
    center = values - jnp.mean(values, axis=-1, keepdims=True)
    inv_std = lax.rsqrt(jnp.mean(center * center, axis=-1, keepdims=True) + eps_norm)
    return (center * inv_std, inv_std)


def norm_back(upstream, normed, inv_std, gain_vec):
    scaled_up = upstream * gain_vec
    mean_one = jnp.mean(scaled_up, axis=-1, keepdims=True)
    mean_two = jnp.mean(scaled_up * normed, axis=-1, keepdims=True)
    return inv_std * (scaled_up - mean_one - normed * mean_two)


def params(mib):
    return pltpu.CompilerParams(vmem_limit_bytes=mib * MIB)


def swap_halves(values):
    width = values.shape[1]
    lane = lax.broadcasted_iota(jnp.int32, values.shape, 1) % HD
    ahead = pltpu.roll(values, width - HD // 2, 1)
    behind = pltpu.roll(values, HD // 2, 1)
    return jnp.where(lane < HD // 2, ahead, behind)


def rope_tables(start):
    half_dim = HD // 2
    inv_freq = 1.0 / 10000.0 ** (jnp.arange(half_dim, dtype=F32) * 2.0 / HD)
    position = (start + jnp.arange(LEN, dtype=jnp.int32)) % LEN
    angles = position.astype(F32)[:, None] * inv_freq[None, :]
    cos_tab, sin_tab = jnp.cos(angles), jnp.sin(angles)
    return (
        jnp.concatenate([cos_tab] * 4, axis=1),
        jnp.concatenate([-sin_tab, sin_tab] * 2, axis=1),
    )


def project_kernel(own_ref, rest_ref, cos_ref, sin_ref, wq_ref, wk_ref, wv_ref, q_ref, k_ref, v_ref):
    own = own_ref.shape[0]
    for rows, x_ref in ((slice(0, own), own_ref), (slice(own, LEN), rest_ref)):
        x = x_ref[...]
        cos_tab, sin_tab = cos_ref[rows, :], sin_ref[rows, :]
        for w_ref, out_ref in ((wq_ref, q_ref), (wk_ref, k_ref)):
            lin = dot_nn(x, w_ref[...])
            for at in range(0, lin.shape[1], LANES):
                part = lin[:, at : at + LANES]
                turned = part * cos_tab + swap_halves(part) * sin_tab
                out_ref[rows, at : at + LANES] = turned.astype(BF)
        v_ref[rows, :] = dot_nn(x, wv_ref[...]).astype(BF)


def project(own, rest, cos_tab, sin_tab, w_query, w_key, w_value):
    cols = w_query.shape[1]
    block = min(256, cols)
    width = own.shape[1]
    whole = lambda a: pl.BlockSpec(a.shape, lambda i: (0, 0))
    w_spec = pl.BlockSpec((width, block), lambda i: (0, i))
    o_spec = pl.BlockSpec((LEN, block), lambda i: (0, i))
    return pl.pallas_call(
        project_kernel,
        grid=(cols // block,),
        in_specs=[whole(own), whole(rest), whole(cos_tab), whole(sin_tab), w_spec, w_spec, w_spec],
        out_specs=[o_spec] * 3,
        out_shape=[shape_of((LEN, cols), BF)] * 3,
        compiler_params=params(28),
        name="project",
    )(own, rest, cos_tab, sin_tab, w_query, w_key, w_value)


def head_only(values, head):
    lane = lax.broadcasted_iota(jnp.int32, values.shape, 1)
    return jnp.where(lane // HD == head, values, jnp.zeros_like(values))


def attend_kernel(q_ref, k_ref, v_ref, ctx_ref, lse_ref):
    k = k_ref[...]
    v_turned = v_ref[...].T
    parts = []
    for head in range(2):
        scores = dot_nt(k, head_only(q_ref[...], head))
        top = jnp.max(scores, axis=0, keepdims=True)
        exps = jnp.exp2((scores - top) * EXP_SCALE)
        total = jnp.sum(exps, axis=0, keepdims=True)
        mix = dot_nn(v_turned[head * HD : (head + 1) * HD, :], exps.astype(BF))
        parts.append(mix * (1.0 / total))
        lse_ref[0, head : head + 1, :] = top * EXP_SCALE + jnp.log2(total)
    ctx_ref[...] = jnp.concatenate(parts, axis=0).T.astype(BF)


def attend(query, key, value, first, count, tile):
    cols = query.shape[1]
    pairs = cols // LANES
    whole = pl.BlockSpec((LEN, LANES), lambda p, i: (0, p))
    return pl.pallas_call(
        attend_kernel,
        grid=(pairs, count // tile),
        in_specs=[pl.BlockSpec((tile, LANES), lambda p, i: (first // tile + i, p)), whole, whole],
        out_specs=[
            pl.BlockSpec((tile, LANES), lambda p, i: (i, p)),
            pl.BlockSpec((1, 2, tile), lambda p, i: (p, 0, i)),
        ],
        out_shape=[shape_of((count, cols), BF), shape_of((pairs, 2, count), F32)],
        compiler_params=params(24),
        name="attend",
    )(query, key, value)


def attend_back_kernel(
    tile, q_ref, k_ref, v_ref, d_ref, delta_ref, lse_ref, cos_ref, sin_ref, *refs,
):
    dq_ref, dk_ref, dv_ref, dk_sum, dv_sum = refs[-5:]
    scale = HD ** (-0.5)
    k, v = k_ref[...], v_ref[...]
    k_turned = k.T

    def unrotate(grads, rows):
        grads = grads * scale
        return (grads * cos_ref[rows, :] - swap_halves(grads) * sin_ref[rows, :]).astype(BF)

    dk_sum[...] = jnp.zeros_like(dk_sum)
    dv_sum[...] = jnp.zeros_like(dv_sum)

    def step(i, carry):
        at = pl.multiple_of(i * tile, tile)
        rows = pl.ds(at, tile)
        q, d = q_ref[rows, :], d_ref[rows, :]
        parts = []
        for head in range(2):
            q_head, d_head = head_only(q, head), head_only(d, head)
            scores = dot_nt(k, q_head)
            probs = jnp.exp2(scores * EXP_SCALE - lse_ref[0, head : head + 1, rows])
            d_probs = dot_nt(v, d_head)
            d_scores = (probs * (d_probs - delta_ref[0, head : head + 1, rows])).astype(BF)
            dv_sum[...] += dot_nn(probs.astype(BF), d_head)
            dk_sum[...] += dot_nn(d_scores, q_head)
            parts.append(dot_nn(k_turned[head * HD : (head + 1) * HD, :], d_scores))
        dq_ref[rows, :] = unrotate(jnp.concatenate(parts, axis=0).T, rows)
        return carry

    lax.fori_loop(0, LEN // tile, step, 0)
    everything = slice(0, LEN)
    dk_ref[...] = unrotate(dk_sum[...], everything)
    dv_ref[...] = dv_sum[...].astype(BF)


def attend_back(query, key, value, d_context, delta, lse, cos_tab, sin_tab, first, pairs, given, tile=256):
    cols = query.shape[1]
    strip = pl.BlockSpec((LEN, LANES), lambda p: (0, first + p))
    table = pl.BlockSpec((LEN, LANES), lambda p: (0, 0))
    sums = pl.BlockSpec((1, 2, LEN), lambda p: (first + p, 0, 0))
    given = list(given)
    return pl.pallas_call(
        functools.partial(attend_back_kernel, tile),
        grid=(pairs,),
        in_specs=[strip] * 4 + [sums, sums, table, table] + [pl.BlockSpec(memory_space=pl.ANY)] * len(given),
        out_specs=[strip] * 3,
        out_shape=[shape_of((LEN, cols), BF)] * 3,
        scratch_shapes=[pltpu.VMEM((LEN, LANES), F32)] * 2,
        input_output_aliases={8 + i: i for i in range(len(given))},
        compiler_params=params(24),
        name="attend_back",
    )(query, key, value, d_context, delta, lse, cos_tab, sin_tab, *given)


def whole_of(array):
    return pl.BlockSpec(array.shape, lambda *_: (0,) * array.ndim)


def norm_in_kernel(tok_ref, gain_ref, bias_ref, out_ref):
    normed, _ = row_norm(tok_ref[...].astype(F32))
    out_ref[...] = (normed * gain_ref[...] + bias_ref[...]).astype(BF)


def norm_in(tokens, gain, bias):
    return pl.pallas_call(
        norm_in_kernel,
        out_shape=shape_of(tokens.shape, BF),
        compiler_params=params(16),
        name="norm_in",
    )(tokens, gain[None, :], bias[None, :])


def norm_mid_kernel(n_got, tok_ref, ctx_ref, w_ref, gain_ref, bias_ref, *refs):
    mixed_ref, mid_ref = refs[n_got:]
    mixed = tok_ref[...].astype(F32) + dot_nn(ctx_ref[...], w_ref[...])
    for got_ref in refs[:n_got]:
        mixed = mixed + got_ref[...].astype(F32)
    mixed_ref[...] = mixed
    normed, _ = row_norm(mixed)
    mid_ref[...] = (normed * gain_ref[...] + bias_ref[...]).astype(BF)


def norm_mid(tokens, ctx, w_out, gain, bias, got):
    return pl.pallas_call(
        functools.partial(norm_mid_kernel, len(got)),
        out_shape=[shape_of(tokens.shape, F32), shape_of(tokens.shape, BF)],
        compiler_params=params(24),
        name="norm_mid",
    )(tokens, ctx, w_out, gain[None, :], bias[None, :], *got)


def norm_back_kernel(n_got, kind, x_ref, base_ref, gain_ref, scale_ref, part_ref, *refs):
    upstream = part_ref[...]
    for got_ref in refs[:n_got]:
        upstream = upstream + got_ref[...].astype(F32)
    normed, inv_std = row_norm(x_ref[...].astype(F32))
    result = base_ref[...].astype(F32) + norm_back(upstream, normed, inv_std, gain_ref[...])
    sums_ref = refs[-1]
    sums_ref[0:1, :] = jnp.sum(upstream * normed, axis=0, keepdims=True)
    sums_ref[1:2, :] = jnp.sum(upstream, axis=0, keepdims=True)
    if kind == "mid":
        refs[n_got][...] = result
        refs[n_got + 1][...] = result.astype(BF)
    else:
        refs[n_got][...] = result * scale_ref[...]


def norm_backward(kind, values, base, gain, scale, part, got):
    rows, width = values.shape
    outs = [shape_of((rows, width), F32)]
    if kind == "mid":
        outs.append(shape_of((rows, width), BF))
    outs.append(shape_of((2, width), F32))
    own = pl.BlockSpec((rows, width), lambda i: (0, 0))
    vector = pl.BlockSpec((1, width), lambda i: (0, 0))
    return pl.pallas_call(
        functools.partial(norm_back_kernel, len(got), kind),
        grid=(1,),
        in_specs=[own, own, vector, pl.BlockSpec((1, 1), lambda i: (0, 0)), own] + [own] * len(got),
        out_specs=[pl.BlockSpec(o.shape, lambda i: (0, 0)) for o in outs],
        out_shape=outs,
        compiler_params=params(32),
        name="norm_back",
    )(values, base, gain[None, :], scale, part, *got)


def turn_kernel(n_pieces, slots_ref, own_ref, rest_ref, turned_ref, both_ref):
    at = 0
    for x_ref in (own_ref, rest_ref):
        count = x_ref.shape[0]
        both_ref[at : at + count, :] = x_ref[...]
        turned = x_ref[...].T
        half = turned.shape[0] // 2
        piece = half // n_pieces
        for which in (1, 2):
            first = (which - 1) * half
            for p in range(n_pieces):
                to = pl.multiple_of(first + slots_ref[which, p] * piece, piece)
                turned_ref[pl.ds(to, piece), at : at + count] = turned[
                    first + p * piece : first + (p + 1) * piece, :
                ]
        at += count


def turn(own, rest, slots, n_pieces):
    width = own.shape[1]
    return pl.pallas_call(
        functools.partial(turn_kernel, n_pieces),
        grid_spec=pltpu.PrefetchScalarGridSpec(
            num_scalar_prefetch=1,
            grid=(1,),
            in_specs=[whole_of(own), whole_of(rest)],
            out_specs=[pl.BlockSpec((width, LEN), lambda i, s: (0, 0)), pl.BlockSpec((LEN, width), lambda i, s: (0, 0))],
        ),
        out_shape=[shape_of((width, LEN), BF), shape_of((LEN, width), BF)],
        compiler_params=params(24),
        name="turn",
    )(slots, own, rest)


def ff_kernel(n_pieces, slots_ref, nm_ref, nt_ref, so_ref, sr_ref, wg_ref, wu_ref, wd_ref, *refs):
    hid_ref, dg_ref, du_ref, *grad_refs, ht_ref = refs[-10:]
    block = wg_ref.shape[1]
    own = so_ref.shape[0]
    tile = min(512, own)
    piece = block // n_pieces

    def forward(first, s_ref):
        def body(i, carry):
            here = pl.ds(pl.multiple_of(i * tile, tile), tile)
            rows = pl.ds(pl.multiple_of(first + i * tile, tile), tile)
            x = nm_ref[rows, :]
            gate = dot_nn(x, wg_ref[...])
            up = dot_nn(x, wu_ref[...])
            d_hidden = dot_nt(s_ref[here, :], wd_ref[...])
            sig = 1.0 / (1.0 + jnp.exp(-gate))
            silu = gate * sig
            hidden = (silu * up).astype(BF)
            hid_ref[rows, :] = hidden
            turned = hidden.T
            for p in range(n_pieces):
                to = pl.multiple_of(slots_ref[0, p] * piece, piece)
                ht_ref[pl.ds(to, piece), rows] = turned[p * piece : (p + 1) * piece, :]
            dg_ref[rows, :] = (d_hidden * up * (sig * (1.0 + gate * (1.0 - sig)))).astype(BF)
            du_ref[rows, :] = (d_hidden * silu).astype(BF)
            return carry

        lax.fori_loop(0, s_ref.shape[0] // tile, body, 0)

    forward(0, so_ref)
    forward(own, sr_ref)
    step = min(256, block // 2)
    for half in range(2):
        out_ref = grad_refs[half]
        for at in range(0, block // 2, step):
            rows = slice(half * block // 2 + at, half * block // 2 + at + step)
            down = dot_nn(ht_ref[rows, :own], so_ref[...]) + dot_nn(ht_ref[rows, own:], sr_ref[...])
            out_ref[at : at + step, :] = down.astype(BF)
    quarter = nt_ref.shape[0] // 4
    for at in range(4):
        left = nt_ref[at * quarter : (at + 1) * quarter, :]
        out_ref = grad_refs[2 + at]
        out_ref[:, :block] = dot_nn(left, dg_ref[...]).astype(BF)
        out_ref[:, block:] = dot_nn(left, du_ref[...]).astype(BF)


def feed_forward(index, block, n_pieces, slots, nm, nt, sg_own, sg_rest, w_gate, w_up, w_down, kept):
    width, units = w_gate.shape
    cols = pl.BlockSpec((width, block), lambda i, s: (0, index))
    kept_spec = pl.BlockSpec((LEN, block), lambda i, s: (0, index))
    grads = [(block // 2, width)] * 2 + [(width // 4, 2 * block)] * 4
    previous = list(kept) if kept is not None else []
    in_vmem = pl.BlockSpec(memory_space=pltpu.VMEM)
    return pl.pallas_call(
        functools.partial(ff_kernel, n_pieces),
        grid_spec=pltpu.PrefetchScalarGridSpec(
            num_scalar_prefetch=1,
            grid=(1,),
            in_specs=[in_vmem] * 4
            + [cols, cols, pl.BlockSpec((block, width), lambda i, s: (index, 0))]
            + [pl.BlockSpec(memory_space=pl.ANY)] * len(previous),
            out_specs=[kept_spec] * 3 + [pl.BlockSpec(dims, lambda i, s: (0, 0)) for dims in grads],
            scratch_shapes=[pltpu.VMEM((block, LEN), BF)],
        ),
        out_shape=[shape_of((LEN, units), BF)] * 3 + [shape_of(dims, BF) for dims in grads],
        input_output_aliases={8 + i: i for i in range(len(previous))},
        compiler_params=params(34),
        name="feed_forward",
    )(slots, nm, nt, sg_own, sg_rest, w_gate, w_up, w_down, *previous)


def orders_of(n_dp):
    bits = [1 << i for i in range(n_dp.bit_length() - 1)]
    if len(bits) < 4:
        return [bits] * 4
    a, b, c = bits[:3]
    return [o + bits[3:] for o in ([a, b, c], [b, a, c], [c, a, b], [c, b, a])]


def masks_of(order):
    size = 1 << len(order)
    masks = []
    for slot in range(size):
        mask = 0
        for level, bit in enumerate(order):
            if slot >> (len(order) - 1 - level) & 1:
                mask |= bit
        masks.append(mask)
    return masks


def slots_of(orders, me):
    table = []
    for order in orders:
        inverse = [0] * (1 << len(order))
        for slot, mask in enumerate(masks_of(order)):
            inverse[mask] = slot
        table.append(inverse)
    size = len(table[0])
    here = jnp.arange(size, dtype=jnp.int32) ^ me
    match = here[:, None] == jnp.arange(size, dtype=jnp.int32)[None, :]
    pieces = jnp.array([masks_of(order) for order in orders], jnp.int32) ^ me
    slots = jnp.stack([jnp.sum(jnp.where(match, jnp.array(t, jnp.int32)[None, :], 0), axis=1) for t in table])
    return (slots, pieces)


def swap_dp(values, bit, n_dp):
    return lax.ppermute(values, "dp", [(i, i ^ bit) for i in range(n_dp)])


class Part:
    def __init__(self, buffer, first, rows):
        self.buffer, self.first, self.rows = buffer, first, rows

    def value(self):
        if self.rows == self.buffer.shape[0]:
            return self.buffer
        return self.buffer[self.first : self.first + self.rows]


def phases_of(order):
    return [("halve", b) for b in order[:-1]] + [("swap", order[-1])] + [("double", b) for b in order[-2::-1]]


class Chunk:
    def __init__(self, keep, send, order, done):
        self.phases, self.done = phases_of(order), done
        self.keep, self.send = keep, send
        self.at, self.last, self.parts = 0, -9, []

    @property
    def open(self):
        return self.at < len(self.phases)

    @property
    def bit(self):
        return self.phases[self.at][1]

    def outgoing(self):
        if self.phases[self.at][0] == "double":
            return [part.value() for part in self.parts]
        return [self.send]

    def next_rows(self):
        if self.phases[self.at][0] == "double":
            return sum(part.rows for part in self.parts)
        return self.send.shape[0]

    def incoming(self, buffer, first):
        rows = self.next_rows()
        kind = self.phases[self.at][0]
        self.at += 1
        got = Part(buffer, first, rows)
        if kind == "double":
            self.parts = self.parts + [got]
            return
        total = self.keep + got.value()
        following = self.phases[self.at][0]
        if following == "halve":
            self.keep, self.send = total[: rows // 2], total[rows // 2 :]
        elif following == "swap":
            self.keep = self.send = total
        else:
            self.parts = [Part(total, 0, rows)]


def in_rounds(work, chunks, n_dp, limit):
    placing = []
    wanted = next(work)
    before = None
    now = 0

    def finish(picks, got):
        for bit, members in picks.items():
            at = 0
            for chunk in members:
                rows = chunk.next_rows()
                chunk.incoming(got[bit], at)
                at += rows
                if not chunk.open:
                    placing.append(chunk)

    while wanted is not None or before is not None or placing or any(c.open for c in chunks):
        picks, loads = {}, {}
        for chunk in chunks:
            if not chunk.open or chunk.last > now - 2:
                continue
            bit, rows = chunk.bit, chunk.next_rows()
            if loads.get(bit, 0) and loads[bit] + rows > limit:
                continue
            loads[bit] = loads.get(bit, 0) + rows
            picks.setdefault(bit, []).append(chunk)
            chunk.last = now
        sends = {}
        for bit in sorted(picks):
            picks[bit].sort(key=lambda c: -c.next_rows())
            parts = [part for chunk in picks[bit] for part in chunk.outgoing()]
            sends[bit] = parts[0] if len(parts) == 1 else jnp.concatenate(parts, axis=0)
        buffers = [c.parts[-1].buffer for c in placing]
        held = (before[1] if before else {}, sends, buffers, wanted)
        got, _, buffers, wanted = lax.optimization_barrier(held)
        taken = {bit: swap_dp(values, bit, n_dp) for bit, values in sends.items()}
        finished, placing = placing, []
        if before:
            finish(before[0], got)
        for chunk, buffer in zip(finished, buffers):
            chunk.parts[-1].buffer = buffer
            chunk.done(chunk.parts)
        if wanted is not None:
            try:
                wanted = work.send(wanted)
            except StopIteration:
                wanted = None
        before = (picks, taken) if picks else None
        now += 1


def place_kernel(slots_ref, scale_ref, which, n_pieces, folds, n_outs, counts, *refs):
    outs = refs[-n_outs:]
    piece = refs[0].shape[0] // counts[0]
    scale = scale_ref[0]
    slot = 0
    for part_ref, count in zip(refs, counts):
        for j in range(count):
            rows = part_ref[j * piece : (j + 1) * piece, :].astype(F32) * scale
            place_at = slots_ref[which, slot]
            for lane, end, out, row, col in folds:
                to = pl.multiple_of(row + place_at * piece, piece)
                outs[out][pl.ds(to, piece), col : col + end - lane] = rows[:, lane:end]
            slot += 1


def place(parts, pieces, scale, which, folds, blocks, bases):
    given = [base for base in bases if base is not None]
    n_pieces = pieces.shape[1]
    least = min(part.rows for part in parts)
    rows_all = sum(part.rows for part in parts)
    piece = rows_all // n_pieces
    counts = [part.rows // piece for part in parts]
    index_map = lambda at: (lambda i, *_: at)
    return pl.pallas_call(
        lambda s, k, *refs: place_kernel(s, k, which, n_pieces, folds, len(blocks), counts, *refs),
        grid_spec=pltpu.PrefetchScalarGridSpec(
            num_scalar_prefetch=2,
            grid=(1,),
            in_specs=[pl.BlockSpec((p.rows, 1024), index_map((p.first // p.rows, 0))) for p in parts]
            + [pl.BlockSpec(memory_space=pl.ANY)] * len(given),
            out_specs=[pl.BlockSpec(dims, index_map(at)) for _, dims, at in blocks],
        ),
        out_shape=[shape_of(full, F32) for full, _, _ in blocks],
        input_output_aliases={2 + len(parts) + i: i for i in range(len(given))},
        compiler_params=params(16),
        name="place",
    )(pieces, scale, *[part.buffer for part in parts], *given)


def late_kernel(n_pieces, slots_ref, own_ref, rest_ref, dq_ref, dk_ref, dv_ref, *refs):
    out_refs, all_ref = refs[:-1], refs[-1]
    own, width = own_ref.shape
    cols = dq_ref.shape[1]
    rows = all_ref.shape[0]
    piece = rows // n_pieces
    for which, d_ref in enumerate((dq_ref, dk_ref, dv_ref)):
        for i in range(width // rows):
            lanes = slice(i * rows, (i + 1) * rows)
            grads = dot_tn(own_ref[:, lanes], d_ref[:own, :]) + dot_tn(rest_ref[:, lanes], d_ref[own:, :])
            all_ref[:, i * cols : (i + 1) * cols] = grads.astype(BF)
        to_slots(n_pieces, slots_ref, which, piece, all_ref, out_refs[2 * which], out_refs[2 * which + 1])


def to_slots(n_pieces, pieces_ref, which, piece, all_ref, keep_ref, send_ref):
    for slot in range(n_pieces):
        at = pl.multiple_of(pieces_ref[which, slot] * piece, piece)
        out_ref = keep_ref if slot < n_pieces // 2 else send_ref
        to = slot % (n_pieces // 2) * piece
        out_ref[to : to + piece, :] = all_ref[pl.ds(at, piece), :]


def late_grads(pieces, n_pieces, own, rest, backs, at, cols):
    width = own.shape[1]
    rows = width * cols // 1024
    strip = pl.BlockSpec((LEN, cols), lambda i, s: (0, at))
    return pl.pallas_call(
        functools.partial(late_kernel, n_pieces),
        grid_spec=pltpu.PrefetchScalarGridSpec(
            num_scalar_prefetch=1,
            grid=(1,),
            in_specs=[whole_of(own), whole_of(rest)] + [strip] * 3,
            out_specs=[pl.BlockSpec((rows // 2, 1024), lambda i, s: (0, 0))] * 6,
            scratch_shapes=[pltpu.VMEM((rows, 1024), BF)],
        ),
        out_shape=[shape_of((rows // 2, 1024), BF)] * 6,
        compiler_params=params(24),
        name="late_grads",
    )(pieces, own, rest, *backs)


def out_back_kernel(n_pieces, pieces_ref, do_ref, dr_ref, co_ref, cr_ref, w_ref, dc_ref, delta_ref, keep_ref, send_ref, all_ref):
    own = do_ref.shape[0]
    at = 0
    for d_ref, c_ref in ((do_ref, co_ref), (dr_ref, cr_ref)):
        count = d_ref.shape[0]
        d_context = dot_nt(d_ref[...], w_ref[...]).astype(BF)
        dc_ref[at : at + count, :] = d_context
        both = (d_context.astype(F32) * c_ref[...].astype(F32)).T
        for head in range(both.shape[0] // HD):
            sums = jnp.sum(both[head * HD : (head + 1) * HD, :], axis=0, keepdims=True)
            delta_ref[head // 2, head % 2 : head % 2 + 1, at : at + count] = sums
        at += count
    rows = all_ref.shape[0]
    step = min(256, rows)
    for first in range(0, rows, step):
        lanes = slice(first, first + step)
        grads = dot_tn(co_ref[:, lanes], do_ref[...]) + dot_tn(cr_ref[:, lanes], dr_ref[...])
        all_ref[lanes, :] = grads.astype(BF)
    if rows % (16 * n_pieces) == 0:
        to_slots(n_pieces, pieces_ref, 3, rows // n_pieces, all_ref, keep_ref, send_ref)
    else:
        keep_ref[...] = all_ref[: rows // 2, :]
        send_ref[...] = all_ref[rows // 2 :, :]


def out_back(pieces, n_pieces, d_own, d_rest, ctx_own, ctx_rest, w_out):
    cols, width = w_out.shape
    pairs = cols // LANES
    outs = [shape_of((LEN, cols), BF), shape_of((pairs, 2, LEN), F32)] + [shape_of((cols // 2, width), BF)] * 2
    arrays = (d_own, d_rest, ctx_own, ctx_rest, w_out)
    return pl.pallas_call(
        functools.partial(out_back_kernel, n_pieces),
        grid_spec=pltpu.PrefetchScalarGridSpec(
            num_scalar_prefetch=1,
            grid=(1,),
            in_specs=[whole_of(a) for a in arrays],
            out_specs=[whole_of(o) for o in outs],
            scratch_shapes=[pltpu.VMEM((cols, width), BF)],
        ),
        out_shape=outs,
        compiler_params=params(32),
        name="out_back",
    )(pieces, *arrays)


def per_device(
    tokens,
    cotangent,
    species_ids,
    species_counts,
    norm1_gain,
    norm1_bias,
    w_query,
    w_key,
    w_value,
    w_out,
    norm2_gain,
    norm2_bias,
    w_gate,
    w_up,
    w_down,
):
    own, width = tokens.shape
    group = lax.axis_size("tensor")
    member = lax.axis_index("tensor")
    n_dp = lax.axis_size("dp")
    me = lax.axis_index("dp")
    rest = LEN - own
    units = w_gate.shape[1]
    block = min(512, units)
    head_cols = w_query.shape[1]
    pairs = head_cols // LANES
    orders = orders_of(n_dp)
    n_pieces = n_dp // 2
    slots, pieces = slots_of([order[:-1] for order in orders], me % n_pieces)

    def from_member(values, step):
        return lax.ppermute(values, "tensor", [((i + step) % group, i) for i in range(group)])

    def rest_rows(values):
        parts = [from_member(values, step) for step in range(1, group)]
        return parts[0] if group == 2 else jnp.concatenate(parts, axis=0)

    def from_others(others):
        got = []
        for step in range(1, group):
            perm = [(i, (i + step) % group) for i in range(group)]
            got.append(lax.ppermute(others[(step - 1) * own : step * own], "tensor", perm))
        return got

    picked = species_ids[:, None] == jnp.arange(SPECIES, dtype=jnp.int32)[None, :]
    count = jnp.sum(jnp.where(picked, species_counts[None, :], 0), axis=1)
    inverse = 1000.0 / count.astype(F32)[0]
    sg_own = (cotangent.astype(F32) * inverse).astype(BF)

    in_own = norm_in(tokens, norm1_gain, norm1_bias)
    in_rest = rest_rows(in_own)
    sg_rest = rest_rows(sg_own)
    cos_tab, sin_tab = rope_tables(member * own)

    query, key, value = project(in_own, in_rest, cos_tab, sin_tab, w_query, w_key, w_value)
    ctx_rest, lse_rest = attend(query, key, value, own, rest, own)
    branch_rest = dot_nn(ctx_rest, w_out).astype(BF)
    got_branch = from_others(branch_rest)
    ctx_own, lse_own = attend(query, key, value, 0, own, own)
    mixed, mid_own = norm_mid(tokens, ctx_own, w_out, norm2_gain, norm2_bias, got_branch)
    mid_rest = rest_rows(mid_own)
    mid_turned, mid = turn(mid_own, mid_rest, slots, n_pieces)

    chunks, found = [], {}
    late_cols = min(256, head_cols)
    late_fits = width * late_cols // 1024 >= 16 * n_pieces and w_out.shape[0] % (16 * n_pieces) == 0

    def send_off(keep, send, which, folds, blocks, names):
        def done(parts):
            bases = [found.get(name) for name in names]
            results = place(parts, pieces, found["scale"], which, folds, blocks, bases)
            found.update(zip(names, results))

        chunks.append(Chunk(keep, send, orders[which], done))

    def work():
        kept = None
        gate_slots = slots
        total = jnp.broadcast_to(inverse, (1, LANES))
        for index in range(units // block):
            *kept, down_keep, down_send, a_keep, a_send, b_keep, b_send = feed_forward(
                index, block, n_pieces, gate_slots, mid, mid_turned, sg_own, sg_rest, w_gate, w_up, w_down, kept
            )
            send_off(
                down_keep, down_send, 0, [(0, width, 0, 0, 0)],
                [(w_down.shape, (block, width), (index, 0))], ["down"],
            )
            for at, (keep, send) in enumerate(((a_keep, a_send), (b_keep, b_send))):
                folds = [(0, block, 0, 0, 0), (block, 2 * block, 1, 0, 0)]
                blocks = [(w.shape, (width // 2, block), (at, index)) for w in (w_gate, w_up)]
                send_off(keep, send, 1 + at, folds, blocks, ["gate", "up"])
            if index < n_dp.bit_length() - 1:
                total = total + swap_dp(total, 1 << index, n_dp)
            gate_slots, kept, total = yield (gate_slots, kept, total)
        for level in range(units // block, n_dp.bit_length() - 1):
            total = total + swap_dp(total, 1 << level, n_dp)
        scale = n_dp / total[:, :1]
        found["scale"] = scale[0]
        hidden, d_gate, d_up = kept
        d_mid_part = dot_nt(d_gate, w_gate) + dot_nt(d_up, w_up)
        d_mid_part, hidden = yield (d_mid_part, hidden)
        got = from_others(d_mid_part[own:].astype(BF))
        out_part = dot_nn(hidden, w_down)
        got, out_part = yield (got, out_part)
        got_out = from_others(out_part[own:].astype(BF))
        d_mixed, d_branch_own, sums2 = norm_backward(
            "mid", mixed, sg_own, norm2_gain, scale, d_mid_part, got
        )
        d_branch_rest = rest_rows(d_branch_own)
        lse = jnp.concatenate([lse_own, lse_rest], axis=2)
        d_branch_rest, got_out = yield (d_branch_rest, got_out)
        output = mixed + out_part[:own]
        for part in got_out:
            output = output + part.astype(F32)
        found["output"] = output.astype(BF)
        d_context, delta, out_keep, out_send = out_back(
            pieces, n_pieces, d_branch_own, d_branch_rest, ctx_own, ctx_rest, w_out
        )
        if late_fits:
            send_off(
                out_keep, out_send, 3, [(0, width, 0, 0, 0)],
                [(w_out.shape, w_out.shape, (0, 0))], ["out"],
            )
        else:
            grad = jnp.concatenate([out_keep, out_send], axis=0)
            found["out"] = lax.psum(grad, "dp").astype(F32) * scale
        backs = ()
        for at in range(head_cols // late_cols):
            d_context, backs = yield (d_context, backs)
            per = late_cols // LANES
            backs = attend_back(
                query, key, value, d_context, delta, lse, cos_tab, sin_tab, at * per, per, backs
            )
            if late_fits:
                rows = width * late_cols // 1024
                folds = [(i * late_cols, (i + 1) * late_cols, 0, i * rows, 0) for i in range(width // rows)]
                late = late_grads(pieces, n_pieces, in_own, in_rest, backs, at, late_cols)
                for which, name in enumerate(("query", "key", "value")):
                    blocks = [(w_query.shape, (width, late_cols), (0, at))]
                    send_off(late[2 * which], late[2 * which + 1], which, folds, blocks, [name])
        if not late_fits:
            for name, d in zip(("query", "key", "value"), backs):
                grad = dot_tn(in_own, d[:own]) + dot_tn(in_rest, d[own:])
                found[name] = lax.psum(grad.astype(BF), "dp").astype(F32) * scale
        (backs,) = yield (backs,)
        d_in_part = sum(dot_nt(d, w) for d, w in zip(backs, (w_query, w_key, w_value)))
        got = from_others(d_in_part[own:].astype(BF))
        (got,) = yield (got,)
        found["input"], sums1 = norm_backward("in", tokens, d_mixed, norm1_gain, scale, d_in_part, got)
        vectors = jnp.concatenate([sums1, sums2], axis=0)
        total = vectors
        for step in range(1, group):
            total = total + from_member(vectors, step)
        for level in range(n_dp.bit_length() - 1):
            (total,) = yield (total,)
            total = total + swap_dp(total, 1 << level, n_dp)
        found["vectors"] = total * scale

    in_rounds(work(), chunks, n_dp, 512)
    vectors = found["vectors"]
    return (
        found["output"],
        found["input"],
        vectors[0],
        vectors[1],
        found["query"],
        found["key"],
        found["value"],
        found["out"],
        vectors[2],
        vectors[3],
        found["gate"],
        found["up"],
        found["down"],
    )


def solution(mesh):
    split = P(("dp", "tensor"), None)
    cols = P(None, "tensor")
    rows = P("tensor", None)
    return jax.shard_map(
        per_device,
        mesh=mesh,
        in_specs=(split, split, P("dp"), P(), P(), P(), cols, cols, cols, rows, P(), P(), cols, cols, rows),
        out_specs=(split, split, P(), P(), cols, cols, cols, rows, P(), P(), cols, cols, rows),
        check_vma=False,
    )
```

```python
import functools
import math

import jax
import jax.numpy as jnp
from jax import lax
from jax.experimental import pallas as pl
from jax.experimental.pallas import tpu as pltpu
from jax.sharding import PartitionSpec as P

HD = 64
LEN = 1024
SPECIES = 850
LANES = 128

eps_norm = 1e-05
BF = jnp.bfloat16
F32 = jnp.float32
EXP_SCALE = HD ** (-0.5) * math.log2(math.e)
MIB = 1024 * 1024
WIDE_ORDERS = (2, 4)
DOWN_ORDERS = (0, 0, 0, 0)
OUT_ORDER = 2
LATE_ORDERS = ((0, 2, 4), (0, 2, 4))
EARLY = (0, 0, 0, 0, 0, 0, 1, 0, 0, 1, 0, 0, 0, 0, 0, 0, 0, 0, 0, 0, 0, 0, 0, 1, 0, 1, 1, 0, 0, 0)
LIMITS = (256, 640, 768, 320, 64, 256, 128, 192, 512, 384, 320, 320, 320, 512, 384, 320, 448, 512, 768, 448, 448, 384, 512, 384, 320, 64, 192, 768, 768, 320)
RANKS = (1, 3, 1, 0, 1, 0, 2, 2, 2, 2, 2, 3, 1, 1, 3, 3, 1, 1, 3, 0, 0, 3, 3, 3, 1, 3, 1, 3, 3, 2)


def shape_of(dims, dtype):
    return jax.ShapeDtypeStruct(dims, dtype)


def dot_nn(left, right):
    return lax.dot_general(left, right, (((1,), (0,)), ((), ())), preferred_element_type=F32)


def dot_nt(left, right):
    return lax.dot_general(left, right, (((1,), (1,)), ((), ())), preferred_element_type=F32)


def dot_tn(left, right):
    return lax.dot_general(left, right, (((0,), (0,)), ((), ())), preferred_element_type=F32)


def row_norm(values):
    center = values - jnp.mean(values, axis=-1, keepdims=True)
    inv_std = lax.rsqrt(jnp.mean(center * center, axis=-1, keepdims=True) + eps_norm)
    return (center * inv_std, inv_std)


def norm_back(upstream, normed, inv_std, gain_vec):
    scaled_up = upstream * gain_vec
    mean_one = jnp.mean(scaled_up, axis=-1, keepdims=True)
    mean_two = jnp.mean(scaled_up * normed, axis=-1, keepdims=True)
    return inv_std * (scaled_up - mean_one - normed * mean_two)


def params(mib):
    return pltpu.CompilerParams(vmem_limit_bytes=mib * MIB)


def swap_halves(values):
    width = values.shape[1]
    lane = lax.broadcasted_iota(jnp.int32, values.shape, 1) % HD
    ahead = pltpu.roll(values, width - HD // 2, 1)
    behind = pltpu.roll(values, HD // 2, 1)
    return jnp.where(lane < HD // 2, ahead, behind)


def rope_tables(start):
    half_dim = HD // 2
    inv_freq = 1.0 / 10000.0 ** (jnp.arange(half_dim, dtype=F32) * 2.0 / HD)
    position = (start + jnp.arange(LEN, dtype=jnp.int32)) % LEN
    angles = position.astype(F32)[:, None] * inv_freq[None, :]
    cos_tab, sin_tab = jnp.cos(angles), jnp.sin(angles)
    return (
        jnp.concatenate([cos_tab] * 4, axis=1),
        jnp.concatenate([-sin_tab, sin_tab] * 2, axis=1),
    )


def project_kernel(own_ref, rest_ref, cos_ref, sin_ref, wq_ref, wk_ref, wv_ref, q_ref, k_ref, v_ref):
    own = own_ref.shape[0]
    for rows, x_ref in ((slice(0, own), own_ref), (slice(own, LEN), rest_ref)):
        x = x_ref[...]
        cos_tab, sin_tab = cos_ref[rows, :], sin_ref[rows, :]
        for w_ref, out_ref in ((wq_ref, q_ref), (wk_ref, k_ref)):
            lin = dot_nn(x, w_ref[...])
            for at in range(0, lin.shape[1], LANES):
                part = lin[:, at : at + LANES]
                turned = part * cos_tab + swap_halves(part) * sin_tab
                out_ref[rows, at : at + LANES] = turned.astype(BF)
        v_ref[rows, :] = dot_nn(x, wv_ref[...]).astype(BF)


def project(own, rest, cos_tab, sin_tab, w_query, w_key, w_value):
    cols = w_query.shape[1]
    block = min(256, cols)
    width = own.shape[1]
    whole = lambda a: pl.BlockSpec(a.shape, lambda i: (0, 0))
    w_spec = pl.BlockSpec((width, block), lambda i: (0, i))
    o_spec = pl.BlockSpec((LEN, block), lambda i: (0, i))
    return pl.pallas_call(
        project_kernel,
        grid=(cols // block,),
        in_specs=[whole(own), whole(rest), whole(cos_tab), whole(sin_tab), w_spec, w_spec, w_spec],
        out_specs=[o_spec] * 3,
        out_shape=[shape_of((LEN, cols), BF)] * 3,
        compiler_params=params(28),
        name="project",
    )(own, rest, cos_tab, sin_tab, w_query, w_key, w_value)


def head_only(values, head):
    lane = lax.broadcasted_iota(jnp.int32, values.shape, 1)
    return jnp.where(lane // HD == head, values, jnp.zeros_like(values))


def attend_kernel(q_ref, k_ref, v_ref, ctx_ref, lse_ref):
    k = k_ref[...]
    v_turned = v_ref[...].T
    parts = []
    for head in range(2):
        scores = dot_nt(k, head_only(q_ref[...], head))
        top = jnp.max(scores, axis=0, keepdims=True)
        exps = jnp.exp2((scores - top) * EXP_SCALE)
        total = jnp.sum(exps, axis=0, keepdims=True)
        mix = dot_nn(v_turned[head * HD : (head + 1) * HD, :], exps.astype(BF))
        parts.append(mix * (1.0 / total))
        lse_ref[0, head : head + 1, :] = top * EXP_SCALE + jnp.log2(total)
    ctx_ref[...] = jnp.concatenate(parts, axis=0).T.astype(BF)


def attend(query, key, value, first, count, tile):
    cols = query.shape[1]
    pairs = cols // LANES
    whole = pl.BlockSpec((LEN, LANES), lambda p, i: (0, p))
    return pl.pallas_call(
        attend_kernel,
        grid=(pairs, count // tile),
        in_specs=[pl.BlockSpec((tile, LANES), lambda p, i: (first // tile + i, p)), whole, whole],
        out_specs=[
            pl.BlockSpec((tile, LANES), lambda p, i: (i, p)),
            pl.BlockSpec((1, 2, tile), lambda p, i: (p, 0, i)),
        ],
        out_shape=[shape_of((count, cols), BF), shape_of((pairs, 2, count), F32)],
        compiler_params=params(24),
        name="attend",
    )(query, key, value)


def attend_back_kernel(
    tile, q_ref, k_ref, v_ref, d_ref, delta_ref, lse_ref, cos_ref, sin_ref, *refs,
):
    dq_ref, dk_ref, dv_ref, dk_sum, dv_sum = refs[-5:]
    scale = HD ** (-0.5)
    k, v = k_ref[...], v_ref[...]
    k_turned = k.T

    def unrotate(grads, rows):
        grads = grads * scale
        return (grads * cos_ref[rows, :] - swap_halves(grads) * sin_ref[rows, :]).astype(BF)

    dk_sum[...] = jnp.zeros_like(dk_sum)
    dv_sum[...] = jnp.zeros_like(dv_sum)

    def step(i, carry):
        at = pl.multiple_of(i * tile, tile)
        rows = pl.ds(at, tile)
        q, d = q_ref[rows, :], d_ref[rows, :]
        parts = []
        for head in range(2):
            q_head, d_head = head_only(q, head), head_only(d, head)
            scores = dot_nt(k, q_head)
            probs = jnp.exp2(scores * EXP_SCALE - lse_ref[0, head : head + 1, rows])
            d_probs = dot_nt(v, d_head)
            d_scores = (probs * (d_probs - delta_ref[0, head : head + 1, rows])).astype(BF)
            dv_sum[...] += dot_nn(probs.astype(BF), d_head)
            dk_sum[...] += dot_nn(d_scores, q_head)
            parts.append(dot_nn(k_turned[head * HD : (head + 1) * HD, :], d_scores))
        dq_ref[rows, :] = unrotate(jnp.concatenate(parts, axis=0).T, rows)
        return carry

    lax.fori_loop(0, LEN // tile, step, 0)
    everything = slice(0, LEN)
    dk_ref[...] = unrotate(dk_sum[...], everything)
    dv_ref[...] = dv_sum[...].astype(BF)


def attend_back(query, key, value, d_context, delta, lse, cos_tab, sin_tab, first, pairs, given, tile=256):
    cols = query.shape[1]
    strip = pl.BlockSpec((LEN, LANES), lambda p: (0, first + p))
    table = pl.BlockSpec((LEN, LANES), lambda p: (0, 0))
    sums = pl.BlockSpec((1, 2, LEN), lambda p: (first + p, 0, 0))
    given = list(given)
    return pl.pallas_call(
        functools.partial(attend_back_kernel, tile),
        grid=(pairs,),
        in_specs=[strip] * 4 + [sums, sums, table, table] + [pl.BlockSpec(memory_space=pl.ANY)] * len(given),
        out_specs=[strip] * 3,
        out_shape=[shape_of((LEN, cols), BF)] * 3,
        scratch_shapes=[pltpu.VMEM((LEN, LANES), F32)] * 2,
        input_output_aliases={8 + i: i for i in range(len(given))},
        compiler_params=params(24),
        name="attend_back",
    )(query, key, value, d_context, delta, lse, cos_tab, sin_tab, *given)


def whole_of(array):
    return pl.BlockSpec(array.shape, lambda *_: (0,) * array.ndim)


def norm_in_kernel(tok_ref, gain_ref, bias_ref, out_ref):
    normed, _ = row_norm(tok_ref[...].astype(F32))
    out_ref[...] = (normed * gain_ref[...] + bias_ref[...]).astype(BF)


def norm_in(tokens, gain, bias):
    return pl.pallas_call(
        norm_in_kernel,
        out_shape=shape_of(tokens.shape, BF),
        compiler_params=params(16),
        name="norm_in",
    )(tokens, gain[None, :], bias[None, :])


def norm_mid_kernel(n_got, tok_ref, ctx_ref, w_ref, gain_ref, bias_ref, *refs):
    mixed_ref, mid_ref = refs[n_got:]
    mixed = tok_ref[...].astype(F32) + dot_nn(ctx_ref[...], w_ref[...])
    for got_ref in refs[:n_got]:
        mixed = mixed + got_ref[...].astype(F32)
    mixed_ref[...] = mixed
    normed, _ = row_norm(mixed)
    mid_ref[...] = (normed * gain_ref[...] + bias_ref[...]).astype(BF)


def norm_mid(tokens, ctx, w_out, gain, bias, got):
    return pl.pallas_call(
        functools.partial(norm_mid_kernel, len(got)),
        out_shape=[shape_of(tokens.shape, F32), shape_of(tokens.shape, BF)],
        compiler_params=params(24),
        name="norm_mid",
    )(tokens, ctx, w_out, gain[None, :], bias[None, :], *got)


def norm_back_kernel(n_got, kind, x_ref, base_ref, gain_ref, scale_ref, part_ref, *refs):
    upstream = part_ref[...]
    for got_ref in refs[:n_got]:
        upstream = upstream + got_ref[...].astype(F32)
    normed, inv_std = row_norm(x_ref[...].astype(F32))
    result = base_ref[...].astype(F32) + norm_back(upstream, normed, inv_std, gain_ref[...])
    sums_ref = refs[-1]
    sums_ref[0:1, :] = jnp.sum(upstream * normed, axis=0, keepdims=True)
    sums_ref[1:2, :] = jnp.sum(upstream, axis=0, keepdims=True)
    if kind == "mid":
        refs[n_got][...] = result
        refs[n_got + 1][...] = result.astype(BF)
    else:
        refs[n_got][...] = result * scale_ref[...]


def norm_backward(kind, values, base, gain, scale, part, got):
    rows, width = values.shape
    outs = [shape_of((rows, width), F32)]
    if kind == "mid":
        outs.append(shape_of((rows, width), BF))
    outs.append(shape_of((2, width), F32))
    own = pl.BlockSpec((rows, width), lambda i: (0, 0))
    vector = pl.BlockSpec((1, width), lambda i: (0, 0))
    return pl.pallas_call(
        functools.partial(norm_back_kernel, len(got), kind),
        grid=(1,),
        in_specs=[own, own, vector, pl.BlockSpec((1, 1), lambda i: (0, 0)), own] + [own] * len(got),
        out_specs=[pl.BlockSpec(o.shape, lambda i: (0, 0)) for o in outs],
        out_shape=outs,
        compiler_params=params(32),
        name="norm_back",
    )(values, base, gain[None, :], scale, part, *got)


def turn_kernel(n_pieces, slots_ref, own_ref, rest_ref, turned_ref, both_ref):
    at = 0
    for x_ref in (own_ref, rest_ref):
        count = x_ref.shape[0]
        both_ref[at : at + count, :] = x_ref[...]
        turned = x_ref[...].T
        half = turned.shape[0] // 2
        piece = half // n_pieces
        for first, which in zip((0, half), WIDE_ORDERS):
            for p in range(n_pieces):
                to = pl.multiple_of(first + slots_ref[which, p] * piece, piece)
                turned_ref[pl.ds(to, piece), at : at + count] = turned[
                    first + p * piece : first + (p + 1) * piece, :
                ]
        at += count


def turn(own, rest, slots, n_pieces):
    width = own.shape[1]
    return pl.pallas_call(
        functools.partial(turn_kernel, n_pieces),
        grid_spec=pltpu.PrefetchScalarGridSpec(
            num_scalar_prefetch=1,
            grid=(1,),
            in_specs=[whole_of(own), whole_of(rest)],
            out_specs=[pl.BlockSpec((width, LEN), lambda i, s: (0, 0)), pl.BlockSpec((LEN, width), lambda i, s: (0, 0))],
        ),
        out_shape=[shape_of((width, LEN), BF), shape_of((LEN, width), BF)],
        compiler_params=params(24),
        name="turn",
    )(slots, own, rest)


def ff_kernel(n_pieces, down_order, slots_ref, nm_ref, nt_ref, so_ref, sr_ref, wg_ref, wu_ref, wd_ref, *refs):
    hid_ref, dg_ref, du_ref, *grad_refs, ht_ref = refs[-10:]
    block = wg_ref.shape[1]
    own = so_ref.shape[0]
    tile = min(512, own)
    piece = block // n_pieces

    def forward(first, s_ref):
        def body(i, carry):
            here = pl.ds(pl.multiple_of(i * tile, tile), tile)
            rows = pl.ds(pl.multiple_of(first + i * tile, tile), tile)
            x = nm_ref[rows, :]
            gate = dot_nn(x, wg_ref[...])
            up = dot_nn(x, wu_ref[...])
            d_hidden = dot_nt(s_ref[here, :], wd_ref[...])
            sig = 1.0 / (1.0 + jnp.exp(-gate))
            silu = gate * sig
            hidden = (silu * up).astype(BF)
            hid_ref[rows, :] = hidden
            turned = hidden.T
            for p in range(n_pieces):
                to = pl.multiple_of(slots_ref[down_order, p] * piece, piece)
                ht_ref[pl.ds(to, piece), rows] = turned[p * piece : (p + 1) * piece, :]
            dg_ref[rows, :] = (d_hidden * up * (sig * (1.0 + gate * (1.0 - sig)))).astype(BF)
            du_ref[rows, :] = (d_hidden * silu).astype(BF)
            return carry

        lax.fori_loop(0, s_ref.shape[0] // tile, body, 0)

    forward(0, so_ref)
    forward(own, sr_ref)
    step = min(256, block // 2)
    for half in range(2):
        out_ref = grad_refs[half]
        for at in range(0, block // 2, step):
            rows = slice(half * block // 2 + at, half * block // 2 + at + step)
            down = dot_nn(ht_ref[rows, :own], so_ref[...]) + dot_nn(ht_ref[rows, own:], sr_ref[...])
            out_ref[at : at + step, :] = down.astype(BF)
    quarter = nt_ref.shape[0] // 4
    for at in range(4):
        left = nt_ref[at * quarter : (at + 1) * quarter, :]
        out_ref = grad_refs[2 + at]
        out_ref[:, :block] = dot_nn(left, dg_ref[...]).astype(BF)
        out_ref[:, block:] = dot_nn(left, du_ref[...]).astype(BF)


def d_mid_kernel(dg_ref, du_ref, wg_ref, wu_ref, own_ref, rest_ref, sum_ref):
    step = pl.program_id(0)
    own = own_ref.shape[0]
    tile = min(512, own)
    for at in range(0, LEN, tile):
        rows = slice(at, at + tile)
        part = dot_nt(dg_ref[rows, :], wg_ref[...]) + dot_nt(du_ref[rows, :], wu_ref[...])

        @pl.when(step == 0)
        def _():
            sum_ref[rows, :] = part

        @pl.when(step > 0)
        def _():
            sum_ref[rows, :] += part

    @pl.when(step == pl.num_programs(0) - 1)
    def _():
        own_ref[...] = sum_ref[:own, :]
        rest_ref[...] = sum_ref[own:, :].astype(BF)


def d_mid_parts(d_gate, d_up, w_gate, w_up, own):
    width, units = w_gate.shape
    block = min(512, units)
    d_spec = pl.BlockSpec((LEN, block), lambda i: (0, i))
    w_spec = pl.BlockSpec((width, block), lambda i: (0, i))
    return pl.pallas_call(
        d_mid_kernel,
        grid=(units // block,),
        in_specs=[d_spec, d_spec, w_spec, w_spec],
        out_specs=[pl.BlockSpec((own, width), lambda i: (0, 0)), pl.BlockSpec((LEN - own, width), lambda i: (0, 0))],
        out_shape=[shape_of((own, width), F32), shape_of((LEN - own, width), BF)],
        scratch_shapes=[pltpu.VMEM((LEN, width), F32)],
        compiler_params=params(30),
        name="d_mid",
    )(d_gate, d_up, w_gate, w_up)


def feed_forward(index, block, n_pieces, down_order, slots, nm, nt, sg_own, sg_rest, w_gate, w_up, w_down, kept):
    width, units = w_gate.shape
    cols = pl.BlockSpec((width, block), lambda i, s: (0, index))
    kept_spec = pl.BlockSpec((LEN, block), lambda i, s: (0, index))
    grads = [(block // 2, width)] * 2 + [(width // 4, 2 * block)] * 4
    previous = list(kept) if kept is not None else []
    in_vmem = pl.BlockSpec(memory_space=pltpu.VMEM)
    return pl.pallas_call(
        functools.partial(ff_kernel, n_pieces, down_order),
        grid_spec=pltpu.PrefetchScalarGridSpec(
            num_scalar_prefetch=1,
            grid=(1,),
            in_specs=[in_vmem] * 4
            + [cols, cols, pl.BlockSpec((block, width), lambda i, s: (index, 0))]
            + [pl.BlockSpec(memory_space=pl.ANY)] * len(previous),
            out_specs=[kept_spec] * 3 + [pl.BlockSpec(dims, lambda i, s: (0, 0)) for dims in grads],
            scratch_shapes=[pltpu.VMEM((block, LEN), BF)],
        ),
        out_shape=[shape_of((LEN, units), BF)] * 3 + [shape_of(dims, BF) for dims in grads],
        input_output_aliases={8 + i: i for i in range(len(previous))},
        compiler_params=params(34),
        name="feed_forward",
    )(slots, nm, nt, sg_own, sg_rest, w_gate, w_up, w_down, *previous)


def orders_of(n_dp):
    bits = [1 << i for i in range(n_dp.bit_length() - 1)]
    if len(bits) < 4:
        return [bits] * 6
    x, y, z = bits[:3]
    return [o + bits[3:] for o in ([x, y, z], [x, z, y], [y, x, z], [y, z, x], [z, x, y], [z, y, x])]


def masks_of(order):
    size = 1 << len(order)
    masks = []
    for slot in range(size):
        mask = 0
        for level, bit in enumerate(order):
            if slot >> (len(order) - 1 - level) & 1:
                mask |= bit
        masks.append(mask)
    return masks


def slots_of(orders, me):
    table = []
    for order in orders:
        inverse = [0] * (1 << len(order))
        for slot, mask in enumerate(masks_of(order)):
            inverse[mask] = slot
        table.append(inverse)
    size = len(table[0])
    here = jnp.arange(size, dtype=jnp.int32) ^ me
    match = here[:, None] == jnp.arange(size, dtype=jnp.int32)[None, :]
    pieces = jnp.array([masks_of(order) for order in orders], jnp.int32) ^ me
    slots = jnp.stack([jnp.sum(jnp.where(match, jnp.array(t, jnp.int32)[None, :], 0), axis=1) for t in table])
    return (slots, pieces)


def swap_dp(values, bit, n_dp):
    return lax.ppermute(values, "dp", [(i, i ^ bit) for i in range(n_dp)])


class Part:
    def __init__(self, buffer, first, rows):
        self.buffer, self.first, self.rows = buffer, first, rows

    def value(self):
        if self.rows == self.buffer.shape[0]:
            return self.buffer
        return self.buffer[self.first : self.first + self.rows]


def phases_of(order):
    return [("halve", b) for b in order[:-1]] + [("swap", order[-1])] + [("double", b) for b in order[-2::-1]]


class Chunk:
    def __init__(self, keep, send, order, target):
        self.phases, self.target = phases_of(order), target
        self.keep, self.send = keep, send
        self.at, self.parts = 0, []

    @property
    def open(self):
        return self.at < len(self.phases)

    @property
    def left(self):
        return len(self.phases) - self.at

    @property
    def bit(self):
        return self.phases[self.at][1]

    def outgoing(self):
        if self.phases[self.at][0] == "double":
            return [part.value() for part in self.parts]
        return [self.send]

    def next_rows(self):
        if self.phases[self.at][0] == "double":
            return sum(part.rows for part in self.parts)
        return self.send.shape[0]

    def incoming(self, buffer, first):
        rows = self.next_rows()
        kind = self.phases[self.at][0]
        self.at += 1
        got = Part(buffer, first, rows)
        if kind == "double":
            self.parts = self.parts + [got]
            return
        total = self.keep + got.value()
        following = self.phases[self.at][0]
        if following == "halve":
            self.keep, self.send = total[: rows // 2], total[rows // 2 :]
        elif following == "swap":
            self.keep = self.send = total
        else:
            self.parts = [Part(total, 0, rows)]


def in_rounds(work, chunks, n_dp, found, place):
    placing, recent = [], set()
    wanted = next(work)
    before = ({}, {})
    now = 1

    def finish(picks, got):
        for bit, members in picks.items():
            at = 0
            for chunk in members:
                rows = chunk.next_rows()
                chunk.incoming(got[bit], at)
                at += rows
                if not chunk.open:
                    placing.append(chunk)

    while wanted is not None or before[0] or placing or any(c.open for c in chunks):
        early, limit, rank = (row[min(now, len(row) - 1)] for row in (EARLY, LIMITS, RANKS))
        if early and before[0]:
            got, wanted = lax.optimization_barrier((before[1], wanted))
            finish(before[0], got)
            before = ({}, {})
        picks, loads = {}, {}
        busy = [chunk for members in before[0].values() for chunk in members]
        free = [chunk for chunk in chunks if chunk.open and chunk not in busy]
        free.sort(key=lambda c: (0, -c.left, -c.next_rows(), c.next_rows())[rank])
        for chunk in free:
            bit, rows = chunk.bit, chunk.next_rows()
            if loads.get(bit, 0) and loads[bit] + rows > limit:
                continue
            loads[bit] = loads.get(bit, 0) + rows
            picks.setdefault(bit, []).append(chunk)
        sends = {}
        for bit in sorted(picks):
            picks[bit].sort(key=lambda c: -c.next_rows())
            parts = [part for chunk in picks[bit] for part in chunk.outgoing()]
            sends[bit] = parts[0] if len(parts) == 1 else jnp.concatenate(parts, axis=0)
        buffers = [c.parts[-1].buffer for c in placing]
        placed = {name: found[name] for name in recent}
        held = (before[1], sends, buffers, placed, wanted)
        got, _, buffers, placed, wanted = lax.optimization_barrier(held)
        found.update(placed)
        recent = set()
        taken = {bit: swap_dp(values, bit, n_dp) for bit, values in sends.items()}
        finished, placing = placing, []
        finish(before[0], got)
        for chunk, buffer in zip(finished, buffers):
            chunk.parts[-1].buffer = buffer
        while finished:
            recent.update(place(finished[:4]))
            finished = finished[4:]
        if wanted is not None:
            try:
                wanted = work.send(wanted)
            except StopIteration:
                wanted = None
        before = (picks, taken)
        now += 1


def place_kernel(plans, n_outs, n_given, slots_ref, scale_ref, *refs):
    outs, wide_ref, sems = refs[-n_outs - 2 : -2], refs[-2], refs[-1]
    scale = scale_ref[0]
    copies = []
    at_ref = done_rows = 0
    for which, counts, folds in plans:
        slot = 0
        for count in counts:
            part_ref = refs[at_ref]
            at_ref += 1
            piece = part_ref.shape[0] // count
            for j in range(count):
                here = slice(done_rows, done_rows + piece)
                done_rows += piece
                wide_ref[here, :] = part_ref[j * piece : (j + 1) * piece, :].astype(F32) * scale
                place_at = slots_ref[which, slot]
                for lane, end, out, row, col in folds:
                    to = pl.multiple_of(row + place_at * piece, piece)
                    copy = pltpu.make_async_copy(
                        wide_ref.at[here, lane:end],
                        outs[out].at[pl.ds(to, piece), col : col + end - lane],
                        sems.at[len(copies)],
                    )
                    copy.start()
                    copies.append(copy)
                slot += 1
    for copy in copies:
        copy.wait()


def place(chunks, pieces, scale, found):
    names, plans, parts = {}, [], []
    n_pieces = pieces.shape[1]
    for chunk in chunks:
        which, folds, shapes = chunk.target
        for name, dims in shapes:
            names.setdefault(name, dims)
        order = list(names)
        mine = [order.index(name) for name, _ in shapes]
        piece = sum(part.rows for part in chunk.parts) // n_pieces
        counts = tuple(part.rows // piece for part in chunk.parts)
        plans.append((which, counts, tuple((l, e, mine[o], r, c) for l, e, o, r, c in folds)))
        parts += chunk.parts
    given = [name for name in names if name in found]
    at = {name: i for i, name in enumerate(names)}
    index_map = lambda block: (lambda i, *_: block)
    anywhere = pl.BlockSpec(memory_space=pl.ANY)
    rows_all = sum(part.rows for part in parts)
    results = pl.pallas_call(
        lambda s, k, *refs: place_kernel(plans, len(names), len(given), s, k, *refs),
        grid_spec=pltpu.PrefetchScalarGridSpec(
            num_scalar_prefetch=2,
            grid=(1,),
            in_specs=[pl.BlockSpec((p.rows, 1024), index_map((p.first // p.rows, 0))) for p in parts]
            + [anywhere] * len(given),
            out_specs=[anywhere] * len(names),
            scratch_shapes=[
                pltpu.VMEM((rows_all, 1024), F32),
                pltpu.SemaphoreType.DMA((n_pieces * sum(len(plan[2]) for plan in plans),)),
            ],
        ),
        out_shape=[shape_of(dims, F32) for dims in names.values()],
        input_output_aliases={2 + len(parts) + i: at[name] for i, name in enumerate(given)},
        compiler_params=params(4 + 8 * rows_all * 1024 // MIB),
        name="place",
    )(pieces, scale, *[part.buffer for part in parts], *[found[name] for name in given])
    found.update(zip(names, results))
    return list(names)


def late_kernel(n_pieces, table, slots_ref, own_ref, rest_ref, dq_ref, dk_ref, dv_ref, *refs):
    out_refs, all_ref = refs[:-1], refs[-1]
    own, width = own_ref.shape
    cols = dq_ref.shape[1]
    rows = all_ref.shape[0]
    piece = rows // n_pieces
    for which, d_ref in enumerate((dq_ref, dk_ref, dv_ref)):
        for i in range(width // rows):
            lanes = slice(i * rows, (i + 1) * rows)
            grads = dot_tn(own_ref[:, lanes], d_ref[:own, :]) + dot_tn(rest_ref[:, lanes], d_ref[own:, :])
            all_ref[:, i * cols : (i + 1) * cols] = grads.astype(BF)
        to_slots(n_pieces, slots_ref, table[which], piece, all_ref, out_refs[2 * which], out_refs[2 * which + 1])


def to_slots(n_pieces, pieces_ref, which, piece, all_ref, keep_ref, send_ref):
    for slot in range(n_pieces):
        at = pl.multiple_of(pieces_ref[which, slot] * piece, piece)
        out_ref = keep_ref if slot < n_pieces // 2 else send_ref
        to = slot % (n_pieces // 2) * piece
        out_ref[to : to + piece, :] = all_ref[pl.ds(at, piece), :]


def late_grads(pieces, n_pieces, table, own, rest, backs, at, cols):
    width = own.shape[1]
    rows = width * cols // 1024
    strip = pl.BlockSpec((LEN, cols), lambda i, s: (0, at))
    return pl.pallas_call(
        functools.partial(late_kernel, n_pieces, table),
        grid_spec=pltpu.PrefetchScalarGridSpec(
            num_scalar_prefetch=1,
            grid=(1,),
            in_specs=[whole_of(own), whole_of(rest)] + [strip] * 3,
            out_specs=[pl.BlockSpec((rows // 2, 1024), lambda i, s: (0, 0))] * 6,
            scratch_shapes=[pltpu.VMEM((rows, 1024), BF)],
        ),
        out_shape=[shape_of((rows // 2, 1024), BF)] * 6,
        compiler_params=params(24),
        name="late_grads",
    )(pieces, own, rest, *backs)


def out_back_kernel(n_pieces, pieces_ref, do_ref, dr_ref, co_ref, cr_ref, w_ref, dc_ref, delta_ref, keep_ref, send_ref, all_ref):
    own = do_ref.shape[0]
    at = 0
    for d_ref, c_ref in ((do_ref, co_ref), (dr_ref, cr_ref)):
        count = d_ref.shape[0]
        d_context = dot_nt(d_ref[...], w_ref[...]).astype(BF)
        dc_ref[at : at + count, :] = d_context
        both = (d_context.astype(F32) * c_ref[...].astype(F32)).T
        for head in range(both.shape[0] // HD):
            sums = jnp.sum(both[head * HD : (head + 1) * HD, :], axis=0, keepdims=True)
            delta_ref[head // 2, head % 2 : head % 2 + 1, at : at + count] = sums
        at += count
    rows = all_ref.shape[0]
    step = min(256, rows)
    for first in range(0, rows, step):
        lanes = slice(first, first + step)
        grads = dot_tn(co_ref[:, lanes], do_ref[...]) + dot_tn(cr_ref[:, lanes], dr_ref[...])
        all_ref[lanes, :] = grads.astype(BF)
    if rows % (16 * n_pieces) == 0:
        to_slots(n_pieces, pieces_ref, OUT_ORDER, rows // n_pieces, all_ref, keep_ref, send_ref)
    else:
        keep_ref[...] = all_ref[: rows // 2, :]
        send_ref[...] = all_ref[rows // 2 :, :]


def out_back(pieces, n_pieces, d_own, d_rest, ctx_own, ctx_rest, w_out):
    cols, width = w_out.shape
    pairs = cols // LANES
    outs = [shape_of((LEN, cols), BF), shape_of((pairs, 2, LEN), F32)] + [shape_of((cols // 2, width), BF)] * 2
    arrays = (d_own, d_rest, ctx_own, ctx_rest, w_out)
    return pl.pallas_call(
        functools.partial(out_back_kernel, n_pieces),
        grid_spec=pltpu.PrefetchScalarGridSpec(
            num_scalar_prefetch=1,
            grid=(1,),
            in_specs=[whole_of(a) for a in arrays],
            out_specs=[whole_of(o) for o in outs],
            scratch_shapes=[pltpu.VMEM((cols, width), BF)],
        ),
        out_shape=outs,
        compiler_params=params(32),
        name="out_back",
    )(pieces, *arrays)


def per_device(
    tokens,
    cotangent,
    species_ids,
    species_counts,
    norm1_gain,
    norm1_bias,
    w_query,
    w_key,
    w_value,
    w_out,
    norm2_gain,
    norm2_bias,
    w_gate,
    w_up,
    w_down,
):
    own, width = tokens.shape
    group = lax.axis_size("tensor")
    member = lax.axis_index("tensor")
    n_dp = lax.axis_size("dp")
    me = lax.axis_index("dp")
    rest = LEN - own
    units = w_gate.shape[1]
    block = min(512, units)
    head_cols = w_query.shape[1]
    pairs = head_cols // LANES
    orders = orders_of(n_dp)
    n_pieces = n_dp // 2
    slots, pieces = slots_of([order[:-1] for order in orders], me % n_pieces)

    def from_member(values, step):
        return lax.ppermute(values, "tensor", [((i + step) % group, i) for i in range(group)])

    def rest_rows(values):
        parts = [from_member(values, step) for step in range(1, group)]
        return parts[0] if group == 2 else jnp.concatenate(parts, axis=0)

    def from_others(others):
        got = []
        for step in range(1, group):
            perm = [(i, (i + step) % group) for i in range(group)]
            got.append(lax.ppermute(others[(step - 1) * own : step * own], "tensor", perm))
        return got

    picked = species_ids[:, None] == jnp.arange(SPECIES, dtype=jnp.int32)[None, :]
    count = jnp.sum(jnp.where(picked, species_counts[None, :], 0), axis=1)
    inverse = 1000.0 / count.astype(F32)[0]
    sg_own = (cotangent.astype(F32) * inverse).astype(BF)

    in_own = norm_in(tokens, norm1_gain, norm1_bias)
    in_rest = rest_rows(in_own)
    sg_rest = rest_rows(sg_own)
    cos_tab, sin_tab = rope_tables(member * own)

    share = jnp.broadcast_to(inverse, (1, LANES))
    levels = [1 << level for level in range(n_dp.bit_length() - 1)]

    def hop(values):
        nonlocal share
        if levels:
            share = share + swap_dp(share, levels.pop(0), n_dp)
        values, share = lax.optimization_barrier((values, share))
        return values

    query, key, value = project(in_own, in_rest, cos_tab, sin_tab, w_query, w_key, w_value)
    query = hop(query)
    ctx_rest, lse_rest = attend(query, key, value, own, rest, own)
    branch_rest = hop(dot_nn(ctx_rest, w_out).astype(BF))
    got_branch = from_others(branch_rest)
    ctx_own, lse_own = attend(query, key, value, 0, own, own)
    ctx_own = hop(ctx_own)
    mixed, mid_own = norm_mid(tokens, ctx_own, w_out, norm2_gain, norm2_bias, got_branch)
    mid_rest = rest_rows(mid_own)
    mid_turned, mid = turn(mid_own, mid_rest, slots, n_pieces)
    while levels:
        mid = hop(mid)
    scale = n_dp / share[:, :1]

    chunks, found = [], {"scale": scale[0]}
    late_cols = min(256, head_cols)
    late_fits = width * late_cols // 1024 >= 16 * n_pieces and w_out.shape[0] % (16 * n_pieces) == 0

    def send_off(keep, send, which, folds, shapes):
        chunks.append(Chunk(keep, send, orders[which], (which, folds, shapes)))

    def work():
        kept = None
        gate_slots = slots
        for index in range(units // block):
            down_order = DOWN_ORDERS[index % len(DOWN_ORDERS)]
            *kept, down_keep, down_send, a_keep, a_send, b_keep, b_send = feed_forward(
                index, block, n_pieces, down_order, gate_slots, mid, mid_turned, sg_own, sg_rest, w_gate, w_up, w_down, kept
            )
            folds = [(0, width, 0, index * block, 0)]
            send_off(down_keep, down_send, down_order, folds, [("down", w_down.shape)])
            for at, (keep, send) in enumerate(((a_keep, a_send), (b_keep, b_send))):
                row, col = at * width // 2, index * block
                folds = [(0, block, 0, row, col), (block, 2 * block, 1, row, col)]
                send_off(keep, send, WIDE_ORDERS[at], folds, [("gate", w_gate.shape), ("up", w_up.shape)])
            gate_slots, kept = yield (gate_slots, kept)
        hidden, d_gate, d_up = kept
        d_mid_part, d_mid_rest = d_mid_parts(d_gate, d_up, w_gate, w_up, own)
        d_mid_part, d_mid_rest, hidden = yield (d_mid_part, d_mid_rest, hidden)
        got = from_others(d_mid_rest)
        out_part = dot_nn(hidden, w_down)
        got, out_part = yield (got, out_part)
        got_out = from_others(out_part[own:].astype(BF))
        d_mixed, d_branch_own, sums2 = norm_backward(
            "mid", mixed, sg_own, norm2_gain, scale, d_mid_part, got
        )
        d_branch_rest = rest_rows(d_branch_own)
        lse = jnp.concatenate([lse_own, lse_rest], axis=2)
        d_branch_rest, got_out = yield (d_branch_rest, got_out)
        output = mixed + out_part[:own]
        for part in got_out:
            output = output + part.astype(F32)
        found["output"] = output.astype(BF)
        d_context, delta, out_keep, out_send = out_back(
            pieces, n_pieces, d_branch_own, d_branch_rest, ctx_own, ctx_rest, w_out
        )
        if late_fits:
            send_off(out_keep, out_send, OUT_ORDER, [(0, width, 0, 0, 0)], [("out", w_out.shape)])
        else:
            grad = jnp.concatenate([out_keep, out_send], axis=0)
            found["out"] = lax.psum(grad, "dp").astype(F32) * scale
        backs = ()
        for at in range(head_cols // late_cols):
            d_context, backs = yield (d_context, backs)
            per = late_cols // LANES
            backs = attend_back(
                query, key, value, d_context, delta, lse, cos_tab, sin_tab, at * per, per, backs
            )
            if late_fits:
                rows = width * late_cols // 1024
                lanes = [i * late_cols for i in range(width // rows + 1)]
                folds = [(lanes[i], lanes[i + 1], 0, i * rows, at * late_cols) for i in range(width // rows)]
                late_orders = LATE_ORDERS[at % len(LATE_ORDERS)]
                late = late_grads(pieces, n_pieces, late_orders, in_own, in_rest, backs, at, late_cols)
                for which, name in enumerate(("query", "key", "value")):
                    send_off(late[2 * which], late[2 * which + 1], late_orders[which], folds, [(name, w_query.shape)])
        if not late_fits:
            for name, d in zip(("query", "key", "value"), backs):
                grad = dot_tn(in_own, d[:own]) + dot_tn(in_rest, d[own:])
                found[name] = lax.psum(grad.astype(BF), "dp").astype(F32) * scale
        (backs,) = yield (backs,)
        d_in_part = sum(dot_nt(d, w) for d, w in zip(backs, (w_query, w_key, w_value)))
        got = from_others(d_in_part[own:].astype(BF))
        (got,) = yield (got,)
        found["input"], sums1 = norm_backward("in", tokens, d_mixed, norm1_gain, scale, d_in_part, got)
        vectors = jnp.concatenate([sums1, sums2], axis=0)
        total = vectors
        for step in range(1, group):
            total = total + from_member(vectors, step)
        for level in range(n_dp.bit_length() - 1):
            (total,) = yield (total,)
            other = swap_dp(total, 1 << level, n_dp)
            yield ()
            total = total + other
        found["vectors"] = total * scale

    in_rounds(work(), chunks, n_dp, found, lambda done: place(done, pieces, found["scale"], found))
    vectors = found["vectors"]
    return (
        found["output"],
        found["input"],
        vectors[0],
        vectors[1],
        found["query"],
        found["key"],
        found["value"],
        found["out"],
        vectors[2],
        vectors[3],
        found["gate"],
        found["up"],
        found["down"],
    )


def solution(mesh):
    split = P(("dp", "tensor"), None)
    cols = P(None, "tensor")
    rows = P("tensor", None)
    return jax.shard_map(
        per_device,
        mesh=mesh,
        in_specs=(split, split, P("dp"), P(), P(), P(), cols, cols, cols, rows, P(), P(), cols, cols, rows),
        out_specs=(split, split, P(), P(), cols, cols, cols, rows, P(), P(), cols, cols, rows),
        check_vma=False,
    )
```

```python
import functools
import math

import jax
import jax.numpy as jnp
from jax import lax
from jax.experimental import pallas as pl
from jax.experimental.pallas import tpu as pltpu
from jax.sharding import PartitionSpec as P

HD = 64
LEN = 1024
SPECIES = 850
LANES = 128

eps_norm = 1e-05
BF = jnp.bfloat16
F32 = jnp.float32
EXP_SCALE = HD ** (-0.5) * math.log2(math.e)
MIB = 1024 * 1024
WIDE_ORDERS = (2, 4)
DOWN_ORDERS = (0, 0, 0, 0)
OUT_ORDER = 2
LATE_ORDERS = ((0, 2, 4), (0, 2, 4))
EARLY = (1, 1, 1, 1, 1, 1, 1, 1, 1, 1, 1, 1, 0, 0, 0, 0, 0, 0, 0, 0, 0, 0, 0, 0, 0, 0, 0, 0, 0, 0)
LIMITS = (384, 384, 384, 384, 384, 384, 384, 384, 384, 384, 384, 384, 384, 384, 384, 384, 384, 384, 384, 384, 384, 384, 384, 384, 384, 384, 384, 384, 384, 384)
RANKS = (0, 0, 0, 0, 0, 0, 0, 1, 1, 1, 1, 1, 1, 1, 1, 1, 1, 1, 1, 1, 1, 1, 1, 1, 1, 1, 1, 1, 1, 1)


def shape_of(dims, dtype):
    return jax.ShapeDtypeStruct(dims, dtype)


def dot_nn(left, right):
    return lax.dot_general(left, right, (((1,), (0,)), ((), ())), preferred_element_type=F32)


def dot_nt(left, right):
    return lax.dot_general(left, right, (((1,), (1,)), ((), ())), preferred_element_type=F32)


def dot_tn(left, right):
    return lax.dot_general(left, right, (((0,), (0,)), ((), ())), preferred_element_type=F32)


def row_norm(values):
    center = values - jnp.mean(values, axis=-1, keepdims=True)
    inv_std = lax.rsqrt(jnp.mean(center * center, axis=-1, keepdims=True) + eps_norm)
    return (center * inv_std, inv_std)


def norm_back(upstream, normed, inv_std, gain_vec):
    scaled_up = upstream * gain_vec
    mean_one = jnp.mean(scaled_up, axis=-1, keepdims=True)
    mean_two = jnp.mean(scaled_up * normed, axis=-1, keepdims=True)
    return inv_std * (scaled_up - mean_one - normed * mean_two)


def params(mib):
    return pltpu.CompilerParams(vmem_limit_bytes=mib * MIB)


def swap_halves(values):
    width = values.shape[1]
    lane = lax.broadcasted_iota(jnp.int32, values.shape, 1) % HD
    ahead = pltpu.roll(values, width - HD // 2, 1)
    behind = pltpu.roll(values, HD // 2, 1)
    return jnp.where(lane < HD // 2, ahead, behind)


def rope_tables(start):
    half_dim = HD // 2
    inv_freq = 1.0 / 10000.0 ** (jnp.arange(half_dim, dtype=F32) * 2.0 / HD)
    position = (start + jnp.arange(LEN, dtype=jnp.int32)) % LEN
    angles = position.astype(F32)[:, None] * inv_freq[None, :]
    cos_tab, sin_tab = jnp.cos(angles), jnp.sin(angles)
    return (
        jnp.concatenate([cos_tab] * 4, axis=1),
        jnp.concatenate([-sin_tab, sin_tab] * 2, axis=1),
    )


def project_kernel(own_ref, rest_ref, cos_ref, sin_ref, wq_ref, wk_ref, wv_ref, q_ref, k_ref, v_ref):
    own = own_ref.shape[0]
    for rows, x_ref in ((slice(0, own), own_ref), (slice(own, LEN), rest_ref)):
        x = x_ref[...]
        cos_tab, sin_tab = cos_ref[rows, :], sin_ref[rows, :]
        for w_ref, out_ref in ((wq_ref, q_ref), (wk_ref, k_ref)):
            lin = dot_nn(x, w_ref[...])
            for at in range(0, lin.shape[1], LANES):
                part = lin[:, at : at + LANES]
                turned = part * cos_tab + swap_halves(part) * sin_tab
                out_ref[rows, at : at + LANES] = turned.astype(BF)
        v_ref[rows, :] = dot_nn(x, wv_ref[...]).astype(BF)


def project(own, rest, cos_tab, sin_tab, w_query, w_key, w_value):
    cols = w_query.shape[1]
    block = min(256, cols)
    width = own.shape[1]
    whole = lambda a: pl.BlockSpec(a.shape, lambda i: (0, 0))
    w_spec = pl.BlockSpec((width, block), lambda i: (0, i))
    o_spec = pl.BlockSpec((LEN, block), lambda i: (0, i))
    return pl.pallas_call(
        project_kernel,
        grid=(cols // block,),
        in_specs=[whole(own), whole(rest), whole(cos_tab), whole(sin_tab), w_spec, w_spec, w_spec],
        out_specs=[o_spec] * 3,
        out_shape=[shape_of((LEN, cols), BF)] * 3,
        compiler_params=params(28),
        name="project",
    )(own, rest, cos_tab, sin_tab, w_query, w_key, w_value)


def head_only(values, head):
    lane = lax.broadcasted_iota(jnp.int32, values.shape, 1)
    return jnp.where(lane // HD == head, values, jnp.zeros_like(values))


def attend_kernel(q_ref, k_ref, v_ref, ctx_ref, lse_ref):
    k = k_ref[...]
    v_turned = v_ref[...].T
    parts = []
    for head in range(2):
        scores = dot_nt(k, head_only(q_ref[...], head))
        top = jnp.max(scores, axis=0, keepdims=True)
        exps = jnp.exp2((scores - top) * EXP_SCALE)
        total = jnp.sum(exps, axis=0, keepdims=True)
        mix = dot_nn(v_turned[head * HD : (head + 1) * HD, :], exps.astype(BF))
        parts.append(mix * (1.0 / total))
        lse_ref[0, head : head + 1, :] = top * EXP_SCALE + jnp.log2(total)
    ctx_ref[...] = jnp.concatenate(parts, axis=0).T.astype(BF)


def attend(query, key, value, first, count, tile):
    cols = query.shape[1]
    pairs = cols // LANES
    whole = pl.BlockSpec((LEN, LANES), lambda p, i: (0, p))
    return pl.pallas_call(
        attend_kernel,
        grid=(pairs, count // tile),
        in_specs=[pl.BlockSpec((tile, LANES), lambda p, i: (first // tile + i, p)), whole, whole],
        out_specs=[
            pl.BlockSpec((tile, LANES), lambda p, i: (i, p)),
            pl.BlockSpec((1, 2, tile), lambda p, i: (p, 0, i)),
        ],
        out_shape=[shape_of((count, cols), BF), shape_of((pairs, 2, count), F32)],
        compiler_params=params(24),
        name="attend",
    )(query, key, value)


def attend_back_kernel(
    tile, q_ref, k_ref, v_ref, d_ref, delta_ref, lse_ref, cos_ref, sin_ref, *refs,
):
    dq_ref, dk_ref, dv_ref, dk_sum, dv_sum = refs[-5:]
    scale = HD ** (-0.5)
    k, v = k_ref[...], v_ref[...]
    k_turned = k.T

    def unrotate(grads, rows):
        grads = grads * scale
        return (grads * cos_ref[rows, :] - swap_halves(grads) * sin_ref[rows, :]).astype(BF)

    dk_sum[...] = jnp.zeros_like(dk_sum)
    dv_sum[...] = jnp.zeros_like(dv_sum)

    def step(i, carry):
        at = pl.multiple_of(i * tile, tile)
        rows = pl.ds(at, tile)
        q, d = q_ref[rows, :], d_ref[rows, :]
        parts = []
        for head in range(2):
            q_head, d_head = head_only(q, head), head_only(d, head)
            scores = dot_nt(k, q_head)
            probs = jnp.exp2(scores * EXP_SCALE - lse_ref[0, head : head + 1, rows])
            d_probs = dot_nt(v, d_head)
            d_scores = (probs * (d_probs - delta_ref[0, head : head + 1, rows])).astype(BF)
            dv_sum[...] += dot_nn(probs.astype(BF), d_head)
            dk_sum[...] += dot_nn(d_scores, q_head)
            parts.append(dot_nn(k_turned[head * HD : (head + 1) * HD, :], d_scores))
        dq_ref[rows, :] = unrotate(jnp.concatenate(parts, axis=0).T, rows)
        return carry

    lax.fori_loop(0, LEN // tile, step, 0)
    everything = slice(0, LEN)
    dk_ref[...] = unrotate(dk_sum[...], everything)
    dv_ref[...] = dv_sum[...].astype(BF)


def attend_back(query, key, value, d_context, delta, lse, cos_tab, sin_tab, first, pairs, given, tile=256):
    cols = query.shape[1]
    strip = pl.BlockSpec((LEN, LANES), lambda p: (0, first + p))
    table = pl.BlockSpec((LEN, LANES), lambda p: (0, 0))
    sums = pl.BlockSpec((1, 2, LEN), lambda p: (first + p, 0, 0))
    given = list(given)
    return pl.pallas_call(
        functools.partial(attend_back_kernel, tile),
        grid=(pairs,),
        in_specs=[strip] * 4 + [sums, sums, table, table] + [pl.BlockSpec(memory_space=pl.ANY)] * len(given),
        out_specs=[strip] * 3,
        out_shape=[shape_of((LEN, cols), BF)] * 3,
        scratch_shapes=[pltpu.VMEM((LEN, LANES), F32)] * 2,
        input_output_aliases={8 + i: i for i in range(len(given))},
        compiler_params=params(24),
        name="attend_back",
    )(query, key, value, d_context, delta, lse, cos_tab, sin_tab, *given)


def whole_of(array):
    return pl.BlockSpec(array.shape, lambda *_: (0,) * array.ndim)


def norm_in_kernel(tok_ref, gain_ref, bias_ref, out_ref):
    normed, _ = row_norm(tok_ref[...].astype(F32))
    out_ref[...] = (normed * gain_ref[...] + bias_ref[...]).astype(BF)


def norm_in(tokens, gain, bias):
    return pl.pallas_call(
        norm_in_kernel,
        out_shape=shape_of(tokens.shape, BF),
        compiler_params=params(16),
        name="norm_in",
    )(tokens, gain[None, :], bias[None, :])


def norm_mid_kernel(n_got, tok_ref, ctx_ref, w_ref, gain_ref, bias_ref, *refs):
    mixed_ref, mid_ref = refs[n_got:]
    mixed = tok_ref[...].astype(F32) + dot_nn(ctx_ref[...], w_ref[...])
    for got_ref in refs[:n_got]:
        mixed = mixed + got_ref[...].astype(F32)
    mixed_ref[...] = mixed
    normed, _ = row_norm(mixed)
    mid_ref[...] = (normed * gain_ref[...] + bias_ref[...]).astype(BF)


def norm_mid(tokens, ctx, w_out, gain, bias, got):
    return pl.pallas_call(
        functools.partial(norm_mid_kernel, len(got)),
        out_shape=[shape_of(tokens.shape, F32), shape_of(tokens.shape, BF)],
        compiler_params=params(24),
        name="norm_mid",
    )(tokens, ctx, w_out, gain[None, :], bias[None, :], *got)


def norm_back_kernel(n_got, kind, x_ref, base_ref, gain_ref, scale_ref, part_ref, *refs):
    upstream = part_ref[...]
    for got_ref in refs[:n_got]:
        upstream = upstream + got_ref[...].astype(F32)
    normed, inv_std = row_norm(x_ref[...].astype(F32))
    result = base_ref[...].astype(F32) + norm_back(upstream, normed, inv_std, gain_ref[...])
    sums_ref = refs[-1]
    sums_ref[0:1, :] = jnp.sum(upstream * normed, axis=0, keepdims=True)
    sums_ref[1:2, :] = jnp.sum(upstream, axis=0, keepdims=True)
    if kind == "mid":
        refs[n_got][...] = result
        refs[n_got + 1][...] = result.astype(BF)
    else:
        refs[n_got][...] = result * scale_ref[...]


def norm_backward(kind, values, base, gain, scale, part, got):
    rows, width = values.shape
    outs = [shape_of((rows, width), F32)]
    if kind == "mid":
        outs.append(shape_of((rows, width), BF))
    outs.append(shape_of((2, width), F32))
    own = pl.BlockSpec((rows, width), lambda i: (0, 0))
    vector = pl.BlockSpec((1, width), lambda i: (0, 0))
    return pl.pallas_call(
        functools.partial(norm_back_kernel, len(got), kind),
        grid=(1,),
        in_specs=[own, own, vector, pl.BlockSpec((1, 1), lambda i: (0, 0)), own] + [own] * len(got),
        out_specs=[pl.BlockSpec(o.shape, lambda i: (0, 0)) for o in outs],
        out_shape=outs,
        compiler_params=params(32),
        name="norm_back",
    )(values, base, gain[None, :], scale, part, *got)


def turn_kernel(n_pieces, slots_ref, own_ref, rest_ref, turned_ref, both_ref):
    at = 0
    for x_ref in (own_ref, rest_ref):
        count = x_ref.shape[0]
        both_ref[at : at + count, :] = x_ref[...]
        turned = x_ref[...].T
        half = turned.shape[0] // 2
        piece = half // n_pieces
        for first, which in zip((0, half), WIDE_ORDERS):
            for p in range(n_pieces):
                to = pl.multiple_of(first + slots_ref[which, p] * piece, piece)
                turned_ref[pl.ds(to, piece), at : at + count] = turned[
                    first + p * piece : first + (p + 1) * piece, :
                ]
        at += count


def turn(own, rest, slots, n_pieces):
    width = own.shape[1]
    return pl.pallas_call(
        functools.partial(turn_kernel, n_pieces),
        grid_spec=pltpu.PrefetchScalarGridSpec(
            num_scalar_prefetch=1,
            grid=(1,),
            in_specs=[whole_of(own), whole_of(rest)],
            out_specs=[pl.BlockSpec((width, LEN), lambda i, s: (0, 0)), pl.BlockSpec((LEN, width), lambda i, s: (0, 0))],
        ),
        out_shape=[shape_of((width, LEN), BF), shape_of((LEN, width), BF)],
        compiler_params=params(24),
        name="turn",
    )(slots, own, rest)


def ff_kernel(n_pieces, down_order, slots_ref, nm_ref, nt_ref, so_ref, sr_ref, wg_ref, wu_ref, wd_ref, *refs):
    hid_ref, dg_ref, du_ref, *grad_refs, ht_ref = refs[-10:]
    block = wg_ref.shape[1]
    own = so_ref.shape[0]
    tile = min(512, own)
    piece = block // n_pieces

    def forward(first, s_ref):
        def body(i, carry):
            here = pl.ds(pl.multiple_of(i * tile, tile), tile)
            rows = pl.ds(pl.multiple_of(first + i * tile, tile), tile)
            x = nm_ref[rows, :]
            gate = dot_nn(x, wg_ref[...])
            up = dot_nn(x, wu_ref[...])
            d_hidden = dot_nt(s_ref[here, :], wd_ref[...])
            sig = 1.0 / (1.0 + jnp.exp(-gate))
            silu = gate * sig
            hidden = (silu * up).astype(BF)
            hid_ref[rows, :] = hidden
            turned = hidden.T
            for p in range(n_pieces):
                to = pl.multiple_of(slots_ref[down_order, p] * piece, piece)
                ht_ref[pl.ds(to, piece), rows] = turned[p * piece : (p + 1) * piece, :]
            dg_ref[rows, :] = (d_hidden * up * (sig * (1.0 + gate * (1.0 - sig)))).astype(BF)
            du_ref[rows, :] = (d_hidden * silu).astype(BF)
            return carry

        lax.fori_loop(0, s_ref.shape[0] // tile, body, 0)

    forward(0, so_ref)
    forward(own, sr_ref)
    step = min(256, block // 2)
    for half in range(2):
        out_ref = grad_refs[half]
        for at in range(0, block // 2, step):
            rows = slice(half * block // 2 + at, half * block // 2 + at + step)
            down = dot_nn(ht_ref[rows, :own], so_ref[...]) + dot_nn(ht_ref[rows, own:], sr_ref[...])
            out_ref[at : at + step, :] = down.astype(BF)
    quarter = nt_ref.shape[0] // 4
    for at in range(4):
        left = nt_ref[at * quarter : (at + 1) * quarter, :]
        out_ref = grad_refs[2 + at]
        out_ref[:, :block] = dot_nn(left, dg_ref[...]).astype(BF)
        out_ref[:, block:] = dot_nn(left, du_ref[...]).astype(BF)


def d_mid_kernel(dg_ref, du_ref, wg_ref, wu_ref, own_ref, rest_ref, sum_ref):
    step = pl.program_id(0)
    own = own_ref.shape[0]
    tile = min(512, own)
    for at in range(0, LEN, tile):
        rows = slice(at, at + tile)
        part = dot_nt(dg_ref[rows, :], wg_ref[...]) + dot_nt(du_ref[rows, :], wu_ref[...])

        @pl.when(step == 0)
        def _():
            sum_ref[rows, :] = part

        @pl.when(step > 0)
        def _():
            sum_ref[rows, :] += part

    @pl.when(step == pl.num_programs(0) - 1)
    def _():
        own_ref[...] = sum_ref[:own, :]
        rest_ref[...] = sum_ref[own:, :].astype(BF)


def d_mid_parts(d_gate, d_up, w_gate, w_up, own):
    width, units = w_gate.shape
    block = min(512, units)
    d_spec = pl.BlockSpec((LEN, block), lambda i: (0, i))
    w_spec = pl.BlockSpec((width, block), lambda i: (0, i))
    return pl.pallas_call(
        d_mid_kernel,
        grid=(units // block,),
        in_specs=[d_spec, d_spec, w_spec, w_spec],
        out_specs=[pl.BlockSpec((own, width), lambda i: (0, 0)), pl.BlockSpec((LEN - own, width), lambda i: (0, 0))],
        out_shape=[shape_of((own, width), F32), shape_of((LEN - own, width), BF)],
        scratch_shapes=[pltpu.VMEM((LEN, width), F32)],
        compiler_params=params(30),
        name="d_mid",
    )(d_gate, d_up, w_gate, w_up)


def feed_forward(index, block, n_pieces, down_order, slots, nm, nt, sg_own, sg_rest, w_gate, w_up, w_down, kept):
    width, units = w_gate.shape
    cols = pl.BlockSpec((width, block), lambda i, s: (0, index))
    kept_spec = pl.BlockSpec((LEN, block), lambda i, s: (0, index))
    grads = [(block // 2, width)] * 2 + [(width // 4, 2 * block)] * 4
    previous = list(kept) if kept is not None else []
    in_vmem = pl.BlockSpec(memory_space=pltpu.VMEM)
    return pl.pallas_call(
        functools.partial(ff_kernel, n_pieces, down_order),
        grid_spec=pltpu.PrefetchScalarGridSpec(
            num_scalar_prefetch=1,
            grid=(1,),
            in_specs=[in_vmem] * 4
            + [cols, cols, pl.BlockSpec((block, width), lambda i, s: (index, 0))]
            + [pl.BlockSpec(memory_space=pl.ANY)] * len(previous),
            out_specs=[kept_spec] * 3 + [pl.BlockSpec(dims, lambda i, s: (0, 0)) for dims in grads],
            scratch_shapes=[pltpu.VMEM((block, LEN), BF)],
        ),
        out_shape=[shape_of((LEN, units), BF)] * 3 + [shape_of(dims, BF) for dims in grads],
        input_output_aliases={8 + i: i for i in range(len(previous))},
        compiler_params=params(34),
        name="feed_forward",
    )(slots, nm, nt, sg_own, sg_rest, w_gate, w_up, w_down, *previous)


def orders_of(n_dp):
    bits = [1 << i for i in range(n_dp.bit_length() - 1)]
    if len(bits) < 4:
        return [bits] * 6
    x, y, z = bits[:3]
    return [o + bits[3:] for o in ([x, y, z], [x, z, y], [y, x, z], [y, z, x], [z, x, y], [z, y, x])]


def masks_of(order):
    size = 1 << len(order)
    masks = []
    for slot in range(size):
        mask = 0
        for level, bit in enumerate(order):
            if slot >> (len(order) - 1 - level) & 1:
                mask |= bit
        masks.append(mask)
    return masks


def slots_of(orders, me):
    table = []
    for order in orders:
        inverse = [0] * (1 << len(order))
        for slot, mask in enumerate(masks_of(order)):
            inverse[mask] = slot
        table.append(inverse)
    size = len(table[0])
    here = jnp.arange(size, dtype=jnp.int32) ^ me
    match = here[:, None] == jnp.arange(size, dtype=jnp.int32)[None, :]
    pieces = jnp.array([masks_of(order) for order in orders], jnp.int32) ^ me
    slots = jnp.stack([jnp.sum(jnp.where(match, jnp.array(t, jnp.int32)[None, :], 0), axis=1) for t in table])
    return (slots, pieces)


def swap_dp(values, bit, n_dp):
    return lax.ppermute(values, "dp", [(i, i ^ bit) for i in range(n_dp)])


class Part:
    def __init__(self, buffer, first, rows):
        self.buffer, self.first, self.rows = buffer, first, rows

    def value(self):
        if self.rows == self.buffer.shape[0]:
            return self.buffer
        return self.buffer[self.first : self.first + self.rows]


def phases_of(order):
    return [("halve", b) for b in order[:-1]] + [("swap", order[-1])] + [("double", b) for b in order[-2::-1]]


class Chunk:
    def __init__(self, keep, send, order, target):
        self.phases, self.target = phases_of(order), target
        self.keep, self.send = keep, send
        self.at, self.parts = 0, []

    @property
    def open(self):
        return self.at < len(self.phases)

    @property
    def left(self):
        return len(self.phases) - self.at

    @property
    def bit(self):
        return self.phases[self.at][1]

    def outgoing(self):
        if self.phases[self.at][0] == "double":
            return [part.value() for part in self.parts]
        return [self.send]

    def next_rows(self):
        if self.phases[self.at][0] == "double":
            return sum(part.rows for part in self.parts)
        return self.send.shape[0]

    def incoming(self, buffer, first):
        rows = self.next_rows()
        kind = self.phases[self.at][0]
        self.at += 1
        got = Part(buffer, first, rows)
        if kind == "double":
            self.parts = self.parts + [got]
            return
        total = self.keep + got.value()
        following = self.phases[self.at][0]
        if following == "halve":
            self.keep, self.send = total[: rows // 2], total[rows // 2 :]
        elif following == "swap":
            self.keep = self.send = total
        else:
            self.parts = [Part(total, 0, rows)]


def in_rounds(work, chunks, n_dp, found, place):
    placing, recent = [], set()
    wanted = next(work)
    before = ({}, {})
    now = 1

    def finish(picks, got):
        for bit, members in picks.items():
            at = 0
            for chunk in members:
                rows = chunk.next_rows()
                chunk.incoming(got[bit], at)
                at += rows
                if not chunk.open:
                    placing.append(chunk)

    while wanted is not None or before[0] or placing or any(c.open for c in chunks):
        early, limit, rank = (row[min(now, len(row) - 1)] for row in (EARLY, LIMITS, RANKS))
        if early and before[0]:
            got, wanted = lax.optimization_barrier((before[1], wanted))
            finish(before[0], got)
            before = ({}, {})
        picks, loads = {}, {}
        busy = [chunk for members in before[0].values() for chunk in members]
        free = [chunk for chunk in chunks if chunk.open and chunk not in busy]
        free.sort(key=lambda c: (0, -c.left, -c.next_rows(), c.next_rows())[rank])
        for chunk in free:
            bit, rows = chunk.bit, chunk.next_rows()
            cost = rows * (2 if bit == n_dp // 2 else 1)
            if loads.get(bit, 0) and loads[bit] + cost > limit:
                continue
            loads[bit] = loads.get(bit, 0) + cost
            picks.setdefault(bit, []).append(chunk)
        sends = {}
        for bit in sorted(picks):
            picks[bit].sort(key=lambda c: -c.next_rows())
            parts = [part for chunk in picks[bit] for part in chunk.outgoing()]
            sends[bit] = parts[0] if len(parts) == 1 else jnp.concatenate(parts, axis=0)
        buffers = [c.parts[-1].buffer for c in placing]
        placed = {name: found[name] for name in recent}
        held = (before[1], sends, buffers, placed, wanted)
        got, _, buffers, placed, wanted = lax.optimization_barrier(held)
        found.update(placed)
        recent = set()
        taken = {bit: swap_dp(values, bit, n_dp) for bit, values in sends.items()}
        finished, placing = placing, []
        finish(before[0], got)
        for chunk, buffer in zip(finished, buffers):
            chunk.parts[-1].buffer = buffer
        while finished:
            recent.update(place(finished[:4]))
            finished = finished[4:]
        if wanted is not None:
            try:
                wanted = work.send(wanted)
            except StopIteration:
                wanted = None
        before = (picks, taken)
        now += 1


def place_kernel(plans, n_outs, n_given, slots_ref, scale_ref, *refs):
    outs, wide_ref, sems = refs[-n_outs - 2 : -2], refs[-2], refs[-1]
    scale = scale_ref[0]
    copies = []
    at_ref = done_rows = 0
    for which, counts, folds in plans:
        slot = 0
        for count in counts:
            part_ref = refs[at_ref]
            at_ref += 1
            piece = part_ref.shape[0] // count
            for j in range(count):
                here = slice(done_rows, done_rows + piece)
                done_rows += piece
                wide_ref[here, :] = part_ref[j * piece : (j + 1) * piece, :].astype(F32) * scale
                place_at = slots_ref[which, slot]
                for lane, end, out, row, col in folds:
                    to = pl.multiple_of(row + place_at * piece, piece)
                    copy = pltpu.make_async_copy(
                        wide_ref.at[here, lane:end],
                        outs[out].at[pl.ds(to, piece), col : col + end - lane],
                        sems.at[len(copies)],
                    )
                    copy.start()
                    copies.append(copy)
                slot += 1
    for copy in copies:
        copy.wait()


def place(chunks, pieces, scale, found):
    names, plans, parts = {}, [], []
    n_pieces = pieces.shape[1]
    for chunk in chunks:
        which, folds, shapes = chunk.target
        for name, dims in shapes:
            names.setdefault(name, dims)
        order = list(names)
        mine = [order.index(name) for name, _ in shapes]
        piece = sum(part.rows for part in chunk.parts) // n_pieces
        counts = tuple(part.rows // piece for part in chunk.parts)
        plans.append((which, counts, tuple((l, e, mine[o], r, c) for l, e, o, r, c in folds)))
        parts += chunk.parts
    given = [name for name in names if name in found]
    at = {name: i for i, name in enumerate(names)}
    index_map = lambda block: (lambda i, *_: block)
    anywhere = pl.BlockSpec(memory_space=pl.ANY)
    rows_all = sum(part.rows for part in parts)
    results = pl.pallas_call(
        lambda s, k, *refs: place_kernel(plans, len(names), len(given), s, k, *refs),
        grid_spec=pltpu.PrefetchScalarGridSpec(
            num_scalar_prefetch=2,
            grid=(1,),
            in_specs=[pl.BlockSpec((p.rows, 1024), index_map((p.first // p.rows, 0))) for p in parts]
            + [anywhere] * len(given),
            out_specs=[anywhere] * len(names),
            scratch_shapes=[
                pltpu.VMEM((rows_all, 1024), F32),
                pltpu.SemaphoreType.DMA((n_pieces * sum(len(plan[2]) for plan in plans),)),
            ],
        ),
        out_shape=[shape_of(dims, F32) for dims in names.values()],
        input_output_aliases={2 + len(parts) + i: at[name] for i, name in enumerate(given)},
        compiler_params=params(4 + 8 * rows_all * 1024 // MIB),
        name="place",
    )(pieces, scale, *[part.buffer for part in parts], *[found[name] for name in given])
    found.update(zip(names, results))
    return list(names)


def late_kernel(n_pieces, table, slots_ref, own_ref, rest_ref, dq_ref, dk_ref, dv_ref, *refs):
    out_refs, all_ref = refs[:-1], refs[-1]
    own, width = own_ref.shape
    cols = dq_ref.shape[1]
    rows = all_ref.shape[0]
    piece = rows // n_pieces
    for which, d_ref in enumerate((dq_ref, dk_ref, dv_ref)):
        for i in range(width // rows):
            lanes = slice(i * rows, (i + 1) * rows)
            grads = dot_tn(own_ref[:, lanes], d_ref[:own, :]) + dot_tn(rest_ref[:, lanes], d_ref[own:, :])
            all_ref[:, i * cols : (i + 1) * cols] = grads.astype(BF)
        to_slots(n_pieces, slots_ref, table[which], piece, all_ref, out_refs[2 * which], out_refs[2 * which + 1])


def to_slots(n_pieces, pieces_ref, which, piece, all_ref, keep_ref, send_ref):
    for slot in range(n_pieces):
        at = pl.multiple_of(pieces_ref[which, slot] * piece, piece)
        out_ref = keep_ref if slot < n_pieces // 2 else send_ref
        to = slot % (n_pieces // 2) * piece
        out_ref[to : to + piece, :] = all_ref[pl.ds(at, piece), :]


def late_grads(pieces, n_pieces, table, own, rest, backs, at, cols):
    width = own.shape[1]
    rows = width * cols // 1024
    strip = pl.BlockSpec((LEN, cols), lambda i, s: (0, at))
    return pl.pallas_call(
        functools.partial(late_kernel, n_pieces, table),
        grid_spec=pltpu.PrefetchScalarGridSpec(
            num_scalar_prefetch=1,
            grid=(1,),
            in_specs=[whole_of(own), whole_of(rest)] + [strip] * 3,
            out_specs=[pl.BlockSpec((rows // 2, 1024), lambda i, s: (0, 0))] * 6,
            scratch_shapes=[pltpu.VMEM((rows, 1024), BF)],
        ),
        out_shape=[shape_of((rows // 2, 1024), BF)] * 6,
        compiler_params=params(24),
        name="late_grads",
    )(pieces, own, rest, *backs)


def out_back_kernel(n_pieces, pieces_ref, do_ref, dr_ref, co_ref, cr_ref, w_ref, dc_ref, delta_ref, keep_ref, send_ref, all_ref):
    own = do_ref.shape[0]
    at = 0
    for d_ref, c_ref in ((do_ref, co_ref), (dr_ref, cr_ref)):
        count = d_ref.shape[0]
        d_context = dot_nt(d_ref[...], w_ref[...]).astype(BF)
        dc_ref[at : at + count, :] = d_context
        both = (d_context.astype(F32) * c_ref[...].astype(F32)).T
        for head in range(both.shape[0] // HD):
            sums = jnp.sum(both[head * HD : (head + 1) * HD, :], axis=0, keepdims=True)
            delta_ref[head // 2, head % 2 : head % 2 + 1, at : at + count] = sums
        at += count
    rows = all_ref.shape[0]
    step = min(256, rows)
    for first in range(0, rows, step):
        lanes = slice(first, first + step)
        grads = dot_tn(co_ref[:, lanes], do_ref[...]) + dot_tn(cr_ref[:, lanes], dr_ref[...])
        all_ref[lanes, :] = grads.astype(BF)
    if rows % (16 * n_pieces) == 0:
        to_slots(n_pieces, pieces_ref, OUT_ORDER, rows // n_pieces, all_ref, keep_ref, send_ref)
    else:
        keep_ref[...] = all_ref[: rows // 2, :]
        send_ref[...] = all_ref[rows // 2 :, :]


def out_back(pieces, n_pieces, d_own, d_rest, ctx_own, ctx_rest, w_out):
    cols, width = w_out.shape
    pairs = cols // LANES
    outs = [shape_of((LEN, cols), BF), shape_of((pairs, 2, LEN), F32)] + [shape_of((cols // 2, width), BF)] * 2
    arrays = (d_own, d_rest, ctx_own, ctx_rest, w_out)
    return pl.pallas_call(
        functools.partial(out_back_kernel, n_pieces),
        grid_spec=pltpu.PrefetchScalarGridSpec(
            num_scalar_prefetch=1,
            grid=(1,),
            in_specs=[whole_of(a) for a in arrays],
            out_specs=[whole_of(o) for o in outs],
            scratch_shapes=[pltpu.VMEM((cols, width), BF)],
        ),
        out_shape=outs,
        compiler_params=params(32),
        name="out_back",
    )(pieces, *arrays)


def per_device(
    tokens,
    cotangent,
    species_ids,
    species_counts,
    norm1_gain,
    norm1_bias,
    w_query,
    w_key,
    w_value,
    w_out,
    norm2_gain,
    norm2_bias,
    w_gate,
    w_up,
    w_down,
):
    own, width = tokens.shape
    group = lax.axis_size("tensor")
    member = lax.axis_index("tensor")
    n_dp = lax.axis_size("dp")
    me = lax.axis_index("dp")
    rest = LEN - own
    units = w_gate.shape[1]
    block = min(512, units)
    head_cols = w_query.shape[1]
    pairs = head_cols // LANES
    orders = orders_of(n_dp)
    n_pieces = n_dp // 2
    slots, pieces = slots_of([order[:-1] for order in orders], me % n_pieces)

    def from_member(values, step):
        return lax.ppermute(values, "tensor", [((i + step) % group, i) for i in range(group)])

    def rest_rows(values):
        parts = [from_member(values, step) for step in range(1, group)]
        return parts[0] if group == 2 else jnp.concatenate(parts, axis=0)

    def from_others(others):
        got = []
        for step in range(1, group):
            perm = [(i, (i + step) % group) for i in range(group)]
            got.append(lax.ppermute(others[(step - 1) * own : step * own], "tensor", perm))
        return got

    picked = species_ids[:, None] == jnp.arange(SPECIES, dtype=jnp.int32)[None, :]
    count = jnp.sum(jnp.where(picked, species_counts[None, :], 0), axis=1)
    inverse = 1000.0 / count.astype(F32)[0]
    sg_own = (cotangent.astype(F32) * inverse).astype(BF)

    in_own = norm_in(tokens, norm1_gain, norm1_bias)
    in_rest = rest_rows(in_own)
    sg_rest = rest_rows(sg_own)
    cos_tab, sin_tab = rope_tables(member * own)

    share = jnp.broadcast_to(inverse, (1, LANES))
    levels = [1 << level for level in range(n_dp.bit_length() - 1)]

    def hop(values):
        nonlocal share
        if levels:
            share = share + swap_dp(share, levels.pop(0), n_dp)
        values, share = lax.optimization_barrier((values, share))
        return values

    query, key, value = project(in_own, in_rest, cos_tab, sin_tab, w_query, w_key, w_value)
    query = hop(query)
    ctx_rest, lse_rest = attend(query, key, value, own, rest, own)
    branch_rest = hop(dot_nn(ctx_rest, w_out).astype(BF))
    got_branch = from_others(branch_rest)
    ctx_own, lse_own = attend(query, key, value, 0, own, own)
    ctx_own = hop(ctx_own)
    mixed, mid_own = norm_mid(tokens, ctx_own, w_out, norm2_gain, norm2_bias, got_branch)
    mid_rest = rest_rows(mid_own)
    mid_turned, mid = turn(mid_own, mid_rest, slots, n_pieces)
    while levels:
        mid = hop(mid)
    scale = n_dp / share[:, :1]

    chunks, found = [], {"scale": scale[0]}
    late_cols = min(256, head_cols)
    late_fits = width * late_cols // 1024 >= 16 * n_pieces and w_out.shape[0] % (16 * n_pieces) == 0

    def send_off(keep, send, which, folds, shapes):
        chunks.append(Chunk(keep, send, orders[which], (which, folds, shapes)))

    def work():
        kept = None
        gate_slots = slots
        for index in range(units // block):
            down_order = DOWN_ORDERS[index % len(DOWN_ORDERS)]
            *kept, down_keep, down_send, a_keep, a_send, b_keep, b_send = feed_forward(
                index, block, n_pieces, down_order, gate_slots, mid, mid_turned, sg_own, sg_rest, w_gate, w_up, w_down, kept
            )
            folds = [(0, width, 0, index * block, 0)]
            send_off(down_keep, down_send, down_order, folds, [("down", w_down.shape)])
            for at, (keep, send) in enumerate(((a_keep, a_send), (b_keep, b_send))):
                row, col = at * width // 2, index * block
                folds = [(0, block, 0, row, col), (block, 2 * block, 1, row, col)]
                send_off(keep, send, WIDE_ORDERS[at], folds, [("gate", w_gate.shape), ("up", w_up.shape)])
            gate_slots, kept = yield (gate_slots, kept)
        hidden, d_gate, d_up = kept
        d_mid_part, d_mid_rest = d_mid_parts(d_gate, d_up, w_gate, w_up, own)
        d_mid_part, d_mid_rest, hidden = yield (d_mid_part, d_mid_rest, hidden)
        got = from_others(d_mid_rest)
        out_part = dot_nn(hidden, w_down)
        got_out = from_others(out_part[own:].astype(BF))
        got, out_part = lax.optimization_barrier((got, out_part))
        d_mixed, d_branch_own, sums2 = norm_backward(
            "mid", mixed, sg_own, norm2_gain, scale, d_mid_part, got
        )
        d_branch_rest = rest_rows(d_branch_own)
        lse = jnp.concatenate([lse_own, lse_rest], axis=2)
        output = mixed + out_part[:own]
        for part in got_out:
            output = output + part.astype(F32)
        output = output.astype(BF)
        d_branch_rest, found["output"] = lax.optimization_barrier((d_branch_rest, output))
        d_context, delta, out_keep, out_send = out_back(
            pieces, n_pieces, d_branch_own, d_branch_rest, ctx_own, ctx_rest, w_out
        )
        if late_fits:
            send_off(out_keep, out_send, OUT_ORDER, [(0, width, 0, 0, 0)], [("out", w_out.shape)])
        else:
            grad = jnp.concatenate([out_keep, out_send], axis=0)
            found["out"] = lax.psum(grad, "dp").astype(F32) * scale
        backs = ()
        for at in range(head_cols // late_cols):
            d_context, *backs = yield (d_context, *backs)
            per = late_cols // LANES
            backs = attend_back(
                query, key, value, d_context, delta, lse, cos_tab, sin_tab, at * per, per, backs
            )
            if late_fits:
                rows = width * late_cols // 1024
                lanes = [i * late_cols for i in range(width // rows + 1)]
                folds = [(lanes[i], lanes[i + 1], 0, i * rows, at * late_cols) for i in range(width // rows)]
                late_orders = LATE_ORDERS[at % len(LATE_ORDERS)]
                late = late_grads(pieces, n_pieces, late_orders, in_own, in_rest, backs, at, late_cols)
                for which, name in enumerate(("query", "key", "value")):
                    target = [(name, w_query.shape)]
                    send_off(late[2 * which], late[2 * which + 1], late_orders[which], folds, target)
        if not late_fits:
            for name, d in zip(("query", "key", "value"), backs):
                grad = dot_tn(in_own, d[:own]) + dot_tn(in_rest, d[own:])
                found[name] = lax.psum(grad.astype(BF), "dp").astype(F32) * scale
        backs = yield (*backs,)
        d_in_part = sum(dot_nt(d, w) for d, w in zip(backs, (w_query, w_key, w_value)))
        got = from_others(d_in_part[own:].astype(BF))
        found["input"], sums1 = norm_backward("in", tokens, d_mixed, norm1_gain, scale, d_in_part, got)
        vectors = jnp.concatenate([sums1, sums2], axis=0)
        total = vectors
        for step in range(1, group):
            total = total + from_member(vectors, step)
        for level in range(n_dp.bit_length() - 1):
            (total,) = yield (total,)
            total = total + swap_dp(total, 1 << level, n_dp)
        found["vectors"] = total * scale

    in_rounds(work(), chunks, n_dp, found, lambda done: place(done, pieces, found["scale"], found))
    vectors = found["vectors"]
    return (
        found["output"],
        found["input"],
        vectors[0],
        vectors[1],
        found["query"],
        found["key"],
        found["value"],
        found["out"],
        vectors[2],
        vectors[3],
        found["gate"],
        found["up"],
        found["down"],
    )


def solution(mesh):
    split = P(("dp", "tensor"), None)
    cols = P(None, "tensor")
    rows = P("tensor", None)
    return jax.shard_map(
        per_device,
        mesh=mesh,
        in_specs=(split, split, P("dp"), P(), P(), P(), cols, cols, cols, rows, P(), P(), cols, cols, rows),
        out_specs=(split, split, P(), P(), cols, cols, cols, rows, P(), P(), cols, cols, rows),
        check_vma=False,
    )
```

```python
import functools
import math

import jax
import jax.numpy as jnp
from jax import lax
from jax.experimental import pallas as pl
from jax.experimental.pallas import tpu as pltpu
from jax.sharding import PartitionSpec as P

HD = 64
LEN = 1024
SPECIES = 850
LANES = 128

eps_norm = 1e-05
BF = jnp.bfloat16
F32 = jnp.float32
EXP_SCALE = HD ** (-0.5) * math.log2(math.e)
MIB = 1024 * 1024
BACK_TILE = 512
WIDE_ORDERS = (2, 4)
DOWN_ORDERS = (0, 0, 0, 0)
OUT_ORDER = 2
LATE_ORDERS = ((0, 2, 4), (0, 2, 4))
EARLY = (1, 1, 1, 1, 1, 1, 1, 1, 1, 1, 1, 0, 0, 0, 0, 0, 0, 0, 0, 0, 0, 0, 0, 0, 0, 0, 0, 0, 0, 0)
LIMITS = (384, 384, 384, 384, 384, 384, 384, 384, 384, 384, 384, 384, 384, 384, 384, 384, 384, 384, 384, 384, 384, 384, 384, 384, 384, 384, 384, 384, 384, 384)
RANKS = (0, 0, 0, 0, 0, 0, 0, 1, 1, 1, 1, 1, 1, 1, 1, 1, 1, 1, 1, 1, 1, 1, 1, 1, 1, 1, 1, 1, 1, 1)


def shape_of(dims, dtype):
    return jax.ShapeDtypeStruct(dims, dtype)


def dot_nn(left, right):
    return lax.dot_general(left, right, (((1,), (0,)), ((), ())), preferred_element_type=F32)


def dot_nt(left, right):
    return lax.dot_general(left, right, (((1,), (1,)), ((), ())), preferred_element_type=F32)


def dot_tn(left, right):
    return lax.dot_general(left, right, (((0,), (0,)), ((), ())), preferred_element_type=F32)


def row_norm(values):
    center = values - jnp.mean(values, axis=-1, keepdims=True)
    inv_std = lax.rsqrt(jnp.mean(center * center, axis=-1, keepdims=True) + eps_norm)
    return (center * inv_std, inv_std)


def norm_back(upstream, normed, inv_std, gain_vec):
    scaled_up = upstream * gain_vec
    mean_one = jnp.mean(scaled_up, axis=-1, keepdims=True)
    mean_two = jnp.mean(scaled_up * normed, axis=-1, keepdims=True)
    return inv_std * (scaled_up - mean_one - normed * mean_two)


def params(mib):
    return pltpu.CompilerParams(vmem_limit_bytes=mib * MIB)


def swap_halves(values):
    width = values.shape[1]
    lane = lax.broadcasted_iota(jnp.int32, values.shape, 1) % HD
    ahead = pltpu.roll(values, width - HD // 2, 1)
    behind = pltpu.roll(values, HD // 2, 1)
    return jnp.where(lane < HD // 2, ahead, behind)


def rope_tables(start):
    half_dim = HD // 2
    inv_freq = 1.0 / 10000.0 ** (jnp.arange(half_dim, dtype=F32) * 2.0 / HD)
    position = (start + jnp.arange(LEN, dtype=jnp.int32)) % LEN
    angles = position.astype(F32)[:, None] * inv_freq[None, :]
    cos_tab, sin_tab = jnp.cos(angles), jnp.sin(angles)
    return (
        jnp.concatenate([cos_tab] * 4, axis=1),
        jnp.concatenate([-sin_tab, sin_tab] * 2, axis=1),
    )


def project_kernel(own_ref, rest_ref, cos_ref, sin_ref, wq_ref, wk_ref, wv_ref, q_ref, k_ref, v_ref):
    own = own_ref.shape[0]
    for rows, x_ref in ((slice(0, own), own_ref), (slice(own, LEN), rest_ref)):
        x = x_ref[...]
        cos_tab, sin_tab = cos_ref[rows, :], sin_ref[rows, :]
        for w_ref, out_ref, factor in ((wq_ref, q_ref, EXP_SCALE), (wk_ref, k_ref, 1.0)):
            lin = dot_nn(x, w_ref[...]) * factor
            for at in range(0, lin.shape[1], LANES):
                part = lin[:, at : at + LANES]
                turned = part * cos_tab + swap_halves(part) * sin_tab
                out_ref[rows, at : at + LANES] = turned.astype(BF)
        v_ref[rows, :] = dot_nn(x, wv_ref[...]).astype(BF)


def project(own, rest, cos_tab, sin_tab, w_query, w_key, w_value):
    cols = w_query.shape[1]
    block = min(256, cols)
    width = own.shape[1]
    whole = lambda a: pl.BlockSpec(a.shape, lambda i: (0, 0))
    w_spec = pl.BlockSpec((width, block), lambda i: (0, i))
    o_spec = pl.BlockSpec((LEN, block), lambda i: (0, i))
    return pl.pallas_call(
        project_kernel,
        grid=(cols // block,),
        in_specs=[whole(own), whole(rest), whole(cos_tab), whole(sin_tab), w_spec, w_spec, w_spec],
        out_specs=[o_spec] * 3,
        out_shape=[shape_of((LEN, cols), BF)] * 3,
        compiler_params=params(28),
        name="project",
    )(own, rest, cos_tab, sin_tab, w_query, w_key, w_value)


def head_only(values, head):
    lane = lax.broadcasted_iota(jnp.int32, values.shape, 1)
    return jnp.where(lane // HD == head, values, jnp.zeros_like(values))


def attend_kernel(q_ref, k_ref, v_ref, ctx_ref, lse_ref):
    k = k_ref[...]
    v_turned = v_ref[...].T
    parts = []
    for head in range(2):
        scores = dot_nt(k, head_only(q_ref[...], head))
        top = jnp.max(scores, axis=0, keepdims=True)
        exps = jnp.exp2(scores - top)
        total = jnp.sum(exps, axis=0, keepdims=True)
        mix = dot_nn(v_turned[head * HD : (head + 1) * HD, :], exps.astype(BF))
        parts.append(mix * (1.0 / total))
        lse_ref[0, head : head + 1, :] = top + jnp.log2(total)
    ctx_ref[...] = jnp.concatenate(parts, axis=0).T.astype(BF)


def attend(query, key, value, first, count, tile):
    cols = query.shape[1]
    pairs = cols // LANES
    whole = pl.BlockSpec((LEN, LANES), lambda p, i: (0, p))
    return pl.pallas_call(
        attend_kernel,
        grid=(pairs, count // tile),
        in_specs=[pl.BlockSpec((tile, LANES), lambda p, i: (first // tile + i, p)), whole, whole],
        out_specs=[
            pl.BlockSpec((tile, LANES), lambda p, i: (i, p)),
            pl.BlockSpec((1, 2, tile), lambda p, i: (p, 0, i)),
        ],
        out_shape=[shape_of((count, cols), BF), shape_of((pairs, 2, count), F32)],
        compiler_params=params(24),
        name="attend",
    )(query, key, value)


def attend_back_kernel(
    tile, q_ref, k_ref, v_ref, d_ref, delta_ref, lse_ref, cos_ref, sin_ref, *refs,
):
    dq_ref, dk_ref, dv_ref, dk_sum, dv_sum = refs[-5:]
    k, v = k_ref[...], v_ref[...]
    k_turned = k.T

    def unrotate(grads, rows, scale):
        grads = grads * scale
        return (grads * cos_ref[rows, :] - swap_halves(grads) * sin_ref[rows, :]).astype(BF)

    dk_sum[...] = jnp.zeros_like(dk_sum)
    dv_sum[...] = jnp.zeros_like(dv_sum)

    def step(i, carry):
        at = pl.multiple_of(i * tile, tile)
        rows = pl.ds(at, tile)
        q, d = q_ref[rows, :], d_ref[rows, :]
        parts = []
        for head in range(2):
            q_head, d_head = head_only(q, head), head_only(d, head)
            scores = dot_nt(k, q_head)
            probs = jnp.exp2(scores - lse_ref[0, head : head + 1, rows])
            d_probs = dot_nt(v, d_head)
            d_scores = (probs * (d_probs - delta_ref[0, head : head + 1, rows])).astype(BF)
            dv_sum[...] += dot_nn(probs.astype(BF), d_head)
            dk_sum[...] += dot_nn(d_scores, q_head)
            parts.append(dot_nn(k_turned[head * HD : (head + 1) * HD, :], d_scores))
        dq_ref[rows, :] = unrotate(jnp.concatenate(parts, axis=0).T, rows, HD ** (-0.5))
        return carry

    lax.fori_loop(0, LEN // tile, step, 0)
    everything = slice(0, LEN)
    dk_ref[...] = unrotate(dk_sum[...], everything, HD ** (-0.5) / EXP_SCALE)
    dv_ref[...] = dv_sum[...].astype(BF)


def attend_back(query, key, value, d_context, delta, lse, cos_tab, sin_tab, first, pairs, given):
    cols = query.shape[1]
    strip = pl.BlockSpec((LEN, LANES), lambda p: (0, first + p))
    table = pl.BlockSpec((LEN, LANES), lambda p: (0, 0))
    sums = pl.BlockSpec((1, 2, LEN), lambda p: (first + p, 0, 0))
    given = list(given)
    return pl.pallas_call(
        functools.partial(attend_back_kernel, BACK_TILE),
        grid=(pairs,),
        in_specs=[strip] * 4 + [sums, sums, table, table] + [pl.BlockSpec(memory_space=pl.ANY)] * len(given),
        out_specs=[strip] * 3,
        out_shape=[shape_of((LEN, cols), BF)] * 3,
        scratch_shapes=[pltpu.VMEM((LEN, LANES), F32)] * 2,
        input_output_aliases={8 + i: i for i in range(len(given))},
        compiler_params=params(24),
        name="attend_back",
    )(query, key, value, d_context, delta, lse, cos_tab, sin_tab, *given)


def whole_of(array):
    return pl.BlockSpec(array.shape, lambda *_: (0,) * array.ndim)


def norm_in_kernel(tok_ref, gain_ref, bias_ref, out_ref):
    normed, _ = row_norm(tok_ref[...].astype(F32))
    out_ref[...] = (normed * gain_ref[...] + bias_ref[...]).astype(BF)


def norm_in(tokens, gain, bias):
    return pl.pallas_call(
        norm_in_kernel,
        out_shape=shape_of(tokens.shape, BF),
        compiler_params=params(16),
        name="norm_in",
    )(tokens, gain[None, :], bias[None, :])


def norm_mid_kernel(n_got, tok_ref, ctx_ref, w_ref, gain_ref, bias_ref, *refs):
    mixed_ref, mid_ref = refs[n_got:]
    mixed = tok_ref[...].astype(F32) + dot_nn(ctx_ref[...], w_ref[...])
    for got_ref in refs[:n_got]:
        mixed = mixed + got_ref[...].astype(F32)
    mixed_ref[...] = mixed
    normed, _ = row_norm(mixed)
    mid_ref[...] = (normed * gain_ref[...] + bias_ref[...]).astype(BF)


def norm_mid(tokens, ctx, w_out, gain, bias, got):
    return pl.pallas_call(
        functools.partial(norm_mid_kernel, len(got)),
        out_shape=[shape_of(tokens.shape, F32), shape_of(tokens.shape, BF)],
        compiler_params=params(24),
        name="norm_mid",
    )(tokens, ctx, w_out, gain[None, :], bias[None, :], *got)


def norm_back_kernel(n_got, kind, x_ref, base_ref, gain_ref, scale_ref, part_ref, *refs):
    upstream = part_ref[...]
    for got_ref in refs[:n_got]:
        upstream = upstream + got_ref[...].astype(F32)
    normed, inv_std = row_norm(x_ref[...].astype(F32))
    result = base_ref[...].astype(F32) + norm_back(upstream, normed, inv_std, gain_ref[...])
    sums_ref = refs[-1]
    sums_ref[0:1, :] = jnp.sum(upstream * normed, axis=0, keepdims=True)
    sums_ref[1:2, :] = jnp.sum(upstream, axis=0, keepdims=True)
    if kind == "mid":
        refs[n_got][...] = result
        refs[n_got + 1][...] = result.astype(BF)
    else:
        refs[n_got][...] = result * scale_ref[...]


def norm_backward(kind, values, base, gain, scale, part, got):
    rows, width = values.shape
    outs = [shape_of((rows, width), F32)]
    if kind == "mid":
        outs.append(shape_of((rows, width), BF))
    outs.append(shape_of((2, width), F32))
    own = pl.BlockSpec((rows, width), lambda i: (0, 0))
    vector = pl.BlockSpec((1, width), lambda i: (0, 0))
    return pl.pallas_call(
        functools.partial(norm_back_kernel, len(got), kind),
        grid=(1,),
        in_specs=[own, own, vector, pl.BlockSpec((1, 1), lambda i: (0, 0)), own] + [own] * len(got),
        out_specs=[pl.BlockSpec(o.shape, lambda i: (0, 0)) for o in outs],
        out_shape=outs,
        compiler_params=params(32),
        name="norm_back",
    )(values, base, gain[None, :], scale, part, *got)


def turn_kernel(n_pieces, slots_ref, own_ref, rest_ref, turned_ref, both_ref):
    at = 0
    for x_ref in (own_ref, rest_ref):
        count = x_ref.shape[0]
        both_ref[at : at + count, :] = x_ref[...]
        turned = x_ref[...].T
        half = turned.shape[0] // 2
        piece = half // n_pieces
        for first, which in zip((0, half), WIDE_ORDERS):
            for p in range(n_pieces):
                to = pl.multiple_of(first + slots_ref[which, p] * piece, piece)
                turned_ref[pl.ds(to, piece), at : at + count] = turned[
                    first + p * piece : first + (p + 1) * piece, :
                ]
        at += count


def turn(own, rest, slots, n_pieces):
    width = own.shape[1]
    return pl.pallas_call(
        functools.partial(turn_kernel, n_pieces),
        grid_spec=pltpu.PrefetchScalarGridSpec(
            num_scalar_prefetch=1,
            grid=(1,),
            in_specs=[whole_of(own), whole_of(rest)],
            out_specs=[pl.BlockSpec((width, LEN), lambda i, s: (0, 0)), pl.BlockSpec((LEN, width), lambda i, s: (0, 0))],
        ),
        out_shape=[shape_of((width, LEN), BF), shape_of((LEN, width), BF)],
        compiler_params=params(24),
        name="turn",
    )(slots, own, rest)


def ff_kernel(n_pieces, down_order, slots_ref, nm_ref, nt_ref, so_ref, sr_ref, wg_ref, wu_ref, wd_ref, *refs):
    hid_ref, dg_ref, du_ref, *grad_refs, ht_ref = refs[-10:]
    block = wg_ref.shape[1]
    own = so_ref.shape[0]
    tile = min(512, own)
    piece = block // n_pieces

    def forward(first, s_ref):
        def body(i, carry):
            here = pl.ds(pl.multiple_of(i * tile, tile), tile)
            rows = pl.ds(pl.multiple_of(first + i * tile, tile), tile)
            x = nm_ref[rows, :]
            gate = dot_nn(x, wg_ref[...])
            up = dot_nn(x, wu_ref[...])
            d_hidden = dot_nt(s_ref[here, :], wd_ref[...])
            sig = 1.0 / (1.0 + jnp.exp(-gate))
            silu = gate * sig
            hidden = (silu * up).astype(BF)
            hid_ref[rows, :] = hidden
            turned = hidden.T
            for p in range(n_pieces):
                to = pl.multiple_of(slots_ref[down_order, p] * piece, piece)
                ht_ref[pl.ds(to, piece), rows] = turned[p * piece : (p + 1) * piece, :]
            dg_ref[rows, :] = (d_hidden * up * (sig * (1.0 + gate * (1.0 - sig)))).astype(BF)
            du_ref[rows, :] = (d_hidden * silu).astype(BF)
            return carry

        lax.fori_loop(0, s_ref.shape[0] // tile, body, 0)

    forward(0, so_ref)
    forward(own, sr_ref)
    step = min(256, block // 2)
    for half in range(2):
        out_ref = grad_refs[half]
        for at in range(0, block // 2, step):
            rows = slice(half * block // 2 + at, half * block // 2 + at + step)
            down = dot_nn(ht_ref[rows, :own], so_ref[...]) + dot_nn(ht_ref[rows, own:], sr_ref[...])
            out_ref[at : at + step, :] = down.astype(BF)
    quarter = nt_ref.shape[0] // 4
    for at in range(4):
        left = nt_ref[at * quarter : (at + 1) * quarter, :]
        out_ref = grad_refs[2 + at]
        out_ref[:, :block] = dot_nn(left, dg_ref[...]).astype(BF)
        out_ref[:, block:] = dot_nn(left, du_ref[...]).astype(BF)


def d_mid_kernel(dg_ref, du_ref, wg_ref, wu_ref, own_ref, rest_ref, sum_ref):
    step = pl.program_id(0)
    own = own_ref.shape[0]
    tile = min(512, own)
    for at in range(0, LEN, tile):
        rows = slice(at, at + tile)
        part = dot_nt(dg_ref[rows, :], wg_ref[...]) + dot_nt(du_ref[rows, :], wu_ref[...])

        @pl.when(step == 0)
        def _():
            sum_ref[rows, :] = part

        @pl.when(step > 0)
        def _():
            sum_ref[rows, :] += part

    @pl.when(step == pl.num_programs(0) - 1)
    def _():
        own_ref[...] = sum_ref[:own, :]
        rest_ref[...] = sum_ref[own:, :].astype(BF)


def d_mid_parts(d_gate, d_up, w_gate, w_up, own):
    width, units = w_gate.shape
    block = min(512, units)
    d_spec = pl.BlockSpec((LEN, block), lambda i: (0, i))
    w_spec = pl.BlockSpec((width, block), lambda i: (0, i))
    return pl.pallas_call(
        d_mid_kernel,
        grid=(units // block,),
        in_specs=[d_spec, d_spec, w_spec, w_spec],
        out_specs=[pl.BlockSpec((own, width), lambda i: (0, 0)), pl.BlockSpec((LEN - own, width), lambda i: (0, 0))],
        out_shape=[shape_of((own, width), F32), shape_of((LEN - own, width), BF)],
        scratch_shapes=[pltpu.VMEM((LEN, width), F32)],
        compiler_params=params(30),
        name="d_mid",
    )(d_gate, d_up, w_gate, w_up)


def feed_forward(index, block, n_pieces, down_order, slots, nm, nt, sg_own, sg_rest, w_gate, w_up, w_down, kept):
    width, units = w_gate.shape
    cols = pl.BlockSpec((width, block), lambda i, s: (0, index))
    kept_spec = pl.BlockSpec((LEN, block), lambda i, s: (0, index))
    grads = [(block // 2, width)] * 2 + [(width // 4, 2 * block)] * 4
    previous = list(kept) if kept is not None else []
    in_vmem = pl.BlockSpec(memory_space=pltpu.VMEM)
    return pl.pallas_call(
        functools.partial(ff_kernel, n_pieces, down_order),
        grid_spec=pltpu.PrefetchScalarGridSpec(
            num_scalar_prefetch=1,
            grid=(1,),
            in_specs=[in_vmem] * 4
            + [cols, cols, pl.BlockSpec((block, width), lambda i, s: (index, 0))]
            + [pl.BlockSpec(memory_space=pl.ANY)] * len(previous),
            out_specs=[kept_spec] * 3 + [pl.BlockSpec(dims, lambda i, s: (0, 0)) for dims in grads],
            scratch_shapes=[pltpu.VMEM((block, LEN), BF)],
        ),
        out_shape=[shape_of((LEN, units), BF)] * 3 + [shape_of(dims, BF) for dims in grads],
        input_output_aliases={8 + i: i for i in range(len(previous))},
        compiler_params=params(34),
        name="feed_forward",
    )(slots, nm, nt, sg_own, sg_rest, w_gate, w_up, w_down, *previous)


def orders_of(n_dp):
    bits = [1 << i for i in range(n_dp.bit_length() - 1)]
    if len(bits) < 4:
        return [bits] * 6
    x, y, z = bits[:3]
    return [o + bits[3:] for o in ([x, y, z], [x, z, y], [y, x, z], [y, z, x], [z, x, y], [z, y, x])]


def masks_of(order):
    size = 1 << len(order)
    masks = []
    for slot in range(size):
        mask = 0
        for level, bit in enumerate(order):
            if slot >> (len(order) - 1 - level) & 1:
                mask |= bit
        masks.append(mask)
    return masks


def slots_of(orders, me):
    table = []
    for order in orders:
        inverse = [0] * (1 << len(order))
        for slot, mask in enumerate(masks_of(order)):
            inverse[mask] = slot
        table.append(inverse)
    size = len(table[0])
    here = jnp.arange(size, dtype=jnp.int32) ^ me
    match = here[:, None] == jnp.arange(size, dtype=jnp.int32)[None, :]
    pieces = jnp.array([masks_of(order) for order in orders], jnp.int32) ^ me
    slots = jnp.stack([jnp.sum(jnp.where(match, jnp.array(t, jnp.int32)[None, :], 0), axis=1) for t in table])
    return (slots, pieces)


def swap_dp(values, bit, n_dp):
    return lax.ppermute(values, "dp", [(i, i ^ bit) for i in range(n_dp)])


class Part:
    def __init__(self, buffer, first, rows):
        self.buffer, self.first, self.rows = buffer, first, rows

    def value(self):
        if self.rows == self.buffer.shape[0]:
            return self.buffer
        return self.buffer[self.first : self.first + self.rows]


def phases_of(order):
    return [("halve", b) for b in order[:-1]] + [("swap", order[-1])] + [("double", b) for b in order[-2::-1]]


class Chunk:
    def __init__(self, keep, send, order, target):
        self.phases, self.target = phases_of(order), target
        self.keep, self.send = keep, send
        self.at, self.parts = 0, []

    @property
    def open(self):
        return self.at < len(self.phases)

    @property
    def left(self):
        return len(self.phases) - self.at

    @property
    def bit(self):
        return self.phases[self.at][1]

    def outgoing(self):
        if self.phases[self.at][0] == "double":
            return [part.value() for part in self.parts]
        return [self.send]

    def next_rows(self):
        if self.phases[self.at][0] == "double":
            return sum(part.rows for part in self.parts)
        return self.send.shape[0]

    def incoming(self, buffer, first):
        rows = self.next_rows()
        kind = self.phases[self.at][0]
        self.at += 1
        got = Part(buffer, first, rows)
        if kind == "double":
            self.parts = self.parts + [got]
            return
        total = self.keep + got.value()
        following = self.phases[self.at][0]
        if following == "halve":
            self.keep, self.send = total[: rows // 2], total[rows // 2 :]
        elif following == "swap":
            self.keep = self.send = total
        else:
            self.parts = [Part(total, 0, rows)]


def in_rounds(work, chunks, n_dp, found, place):
    placing, recent = [], set()
    wanted = next(work)
    before = ({}, {})
    now = 1

    def finish(picks, got):
        for bit, members in picks.items():
            at = 0
            for chunk in members:
                rows = chunk.next_rows()
                chunk.incoming(got[bit], at)
                at += rows
                if not chunk.open:
                    placing.append(chunk)

    while wanted is not None or before[0] or placing or any(c.open for c in chunks):
        early, limit, rank = (row[min(now, len(row) - 1)] for row in (EARLY, LIMITS, RANKS))
        if early and before[0]:
            got, wanted = lax.optimization_barrier((before[1], wanted))
            finish(before[0], got)
            before = ({}, {})
        picks, loads = {}, {}
        busy = [chunk for members in before[0].values() for chunk in members]
        free = [chunk for chunk in chunks if chunk.open and chunk not in busy]
        free.sort(key=lambda c: (0, -c.left, -c.next_rows(), c.next_rows())[rank])
        for chunk in free:
            bit, rows = chunk.bit, chunk.next_rows()
            cost = rows * (2 if bit == n_dp // 2 else 1)
            if loads.get(bit, 0) and loads[bit] + cost > limit:
                continue
            loads[bit] = loads.get(bit, 0) + cost
            picks.setdefault(bit, []).append(chunk)
        sends = {}
        for bit in sorted(picks):
            picks[bit].sort(key=lambda c: -c.next_rows())
            parts = [part for chunk in picks[bit] for part in chunk.outgoing()]
            sends[bit] = parts[0] if len(parts) == 1 else jnp.concatenate(parts, axis=0)
        buffers = [c.parts[-1].buffer for c in placing]
        placed = {name: found[name] for name in recent}
        held = (before[1], sends, buffers, placed, wanted)
        got, _, buffers, placed, wanted = lax.optimization_barrier(held)
        found.update(placed)
        recent = set()
        taken = {bit: swap_dp(values, bit, n_dp) for bit, values in sends.items()}
        finished, placing = placing, []
        finish(before[0], got)
        for chunk, buffer in zip(finished, buffers):
            chunk.parts[-1].buffer = buffer
        while finished:
            recent.update(place(finished[:4]))
            finished = finished[4:]
        if wanted is not None:
            try:
                wanted = work.send(wanted)
            except StopIteration:
                wanted = None
        before = (picks, taken)
        now += 1


def place_kernel(plans, n_outs, n_given, slots_ref, scale_ref, *refs):
    outs, wide_ref, sems = refs[-n_outs - 2 : -2], refs[-2], refs[-1]
    scale = scale_ref[0]
    copies = []
    at_ref = done_rows = 0
    for which, counts, folds in plans:
        slot = 0
        for count in counts:
            part_ref = refs[at_ref]
            at_ref += 1
            piece = part_ref.shape[0] // count
            for j in range(count):
                here = slice(done_rows, done_rows + piece)
                done_rows += piece
                wide_ref[here, :] = part_ref[j * piece : (j + 1) * piece, :].astype(F32) * scale
                place_at = slots_ref[which, slot]
                for lane, end, out, row, col in folds:
                    to = pl.multiple_of(row + place_at * piece, piece)
                    copy = pltpu.make_async_copy(
                        wide_ref.at[here, lane:end],
                        outs[out].at[pl.ds(to, piece), col : col + end - lane],
                        sems.at[len(copies)],
                    )
                    copy.start()
                    copies.append(copy)
                slot += 1
    for copy in copies:
        copy.wait()


def place(chunks, pieces, scale, found):
    names, plans, parts = {}, [], []
    n_pieces = pieces.shape[1]
    for chunk in chunks:
        which, folds, shapes = chunk.target
        for name, dims in shapes:
            names.setdefault(name, dims)
        order = list(names)
        mine = [order.index(name) for name, _ in shapes]
        piece = sum(part.rows for part in chunk.parts) // n_pieces
        counts = tuple(part.rows // piece for part in chunk.parts)
        plans.append((which, counts, tuple((l, e, mine[o], r, c) for l, e, o, r, c in folds)))
        parts += chunk.parts
    given = [name for name in names if name in found]
    at = {name: i for i, name in enumerate(names)}
    index_map = lambda block: (lambda i, *_: block)
    anywhere = pl.BlockSpec(memory_space=pl.ANY)
    rows_all = sum(part.rows for part in parts)
    results = pl.pallas_call(
        lambda s, k, *refs: place_kernel(plans, len(names), len(given), s, k, *refs),
        grid_spec=pltpu.PrefetchScalarGridSpec(
            num_scalar_prefetch=2,
            grid=(1,),
            in_specs=[pl.BlockSpec((p.rows, 1024), index_map((p.first // p.rows, 0))) for p in parts]
            + [anywhere] * len(given),
            out_specs=[anywhere] * len(names),
            scratch_shapes=[
                pltpu.VMEM((rows_all, 1024), F32),
                pltpu.SemaphoreType.DMA((n_pieces * sum(len(plan[2]) for plan in plans),)),
            ],
        ),
        out_shape=[shape_of(dims, F32) for dims in names.values()],
        input_output_aliases={2 + len(parts) + i: at[name] for i, name in enumerate(given)},
        compiler_params=params(4 + 8 * rows_all * 1024 // MIB),
        name="place",
    )(pieces, scale, *[part.buffer for part in parts], *[found[name] for name in given])
    found.update(zip(names, results))
    return list(names)


def late_kernel(n_pieces, table, slots_ref, own_ref, rest_ref, dq_ref, dk_ref, dv_ref, *refs):
    out_refs, all_ref = refs[:-1], refs[-1]
    own, width = own_ref.shape
    cols = dq_ref.shape[1]
    rows = all_ref.shape[0]
    piece = rows // n_pieces
    for which, d_ref in enumerate((dq_ref, dk_ref, dv_ref)):
        for i in range(width // rows):
            lanes = slice(i * rows, (i + 1) * rows)
            grads = dot_tn(own_ref[:, lanes], d_ref[:own, :]) + dot_tn(rest_ref[:, lanes], d_ref[own:, :])
            all_ref[:, i * cols : (i + 1) * cols] = grads.astype(BF)
        to_slots(n_pieces, slots_ref, table[which], piece, all_ref, out_refs[2 * which], out_refs[2 * which + 1])


def to_slots(n_pieces, pieces_ref, which, piece, all_ref, keep_ref, send_ref):
    for slot in range(n_pieces):
        at = pl.multiple_of(pieces_ref[which, slot] * piece, piece)
        out_ref = keep_ref if slot < n_pieces // 2 else send_ref
        to = slot % (n_pieces // 2) * piece
        out_ref[to : to + piece, :] = all_ref[pl.ds(at, piece), :]


def late_grads(pieces, n_pieces, table, own, rest, backs, at, cols):
    width = own.shape[1]
    rows = width * cols // 1024
    strip = pl.BlockSpec((LEN, cols), lambda i, s: (0, at))
    return pl.pallas_call(
        functools.partial(late_kernel, n_pieces, table),
        grid_spec=pltpu.PrefetchScalarGridSpec(
            num_scalar_prefetch=1,
            grid=(1,),
            in_specs=[whole_of(own), whole_of(rest)] + [strip] * 3,
            out_specs=[pl.BlockSpec((rows // 2, 1024), lambda i, s: (0, 0))] * 6,
            scratch_shapes=[pltpu.VMEM((rows, 1024), BF)],
        ),
        out_shape=[shape_of((rows // 2, 1024), BF)] * 6,
        compiler_params=params(24),
        name="late_grads",
    )(pieces, own, rest, *backs)


def out_back_kernel(n_pieces, pieces_ref, do_ref, dr_ref, co_ref, cr_ref, w_ref, dc_ref, delta_ref, keep_ref, send_ref, all_ref):
    own = do_ref.shape[0]
    at = 0
    for d_ref, c_ref in ((do_ref, co_ref), (dr_ref, cr_ref)):
        count = d_ref.shape[0]
        d_context = dot_nt(d_ref[...], w_ref[...]).astype(BF)
        dc_ref[at : at + count, :] = d_context
        both = (d_context.astype(F32) * c_ref[...].astype(F32)).T
        for head in range(both.shape[0] // HD):
            sums = jnp.sum(both[head * HD : (head + 1) * HD, :], axis=0, keepdims=True)
            delta_ref[head // 2, head % 2 : head % 2 + 1, at : at + count] = sums
        at += count
    rows = all_ref.shape[0]
    step = min(256, rows)
    for first in range(0, rows, step):
        lanes = slice(first, first + step)
        grads = dot_tn(co_ref[:, lanes], do_ref[...]) + dot_tn(cr_ref[:, lanes], dr_ref[...])
        all_ref[lanes, :] = grads.astype(BF)
    if rows % (16 * n_pieces) == 0:
        to_slots(n_pieces, pieces_ref, OUT_ORDER, rows // n_pieces, all_ref, keep_ref, send_ref)
    else:
        keep_ref[...] = all_ref[: rows // 2, :]
        send_ref[...] = all_ref[rows // 2 :, :]


def out_back(pieces, n_pieces, d_own, d_rest, ctx_own, ctx_rest, w_out):
    cols, width = w_out.shape
    pairs = cols // LANES
    outs = [shape_of((LEN, cols), BF), shape_of((pairs, 2, LEN), F32)] + [shape_of((cols // 2, width), BF)] * 2
    arrays = (d_own, d_rest, ctx_own, ctx_rest, w_out)
    return pl.pallas_call(
        functools.partial(out_back_kernel, n_pieces),
        grid_spec=pltpu.PrefetchScalarGridSpec(
            num_scalar_prefetch=1,
            grid=(1,),
            in_specs=[whole_of(a) for a in arrays],
            out_specs=[whole_of(o) for o in outs],
            scratch_shapes=[pltpu.VMEM((cols, width), BF)],
        ),
        out_shape=outs,
        compiler_params=params(32),
        name="out_back",
    )(pieces, *arrays)


def per_device(
    tokens,
    cotangent,
    species_ids,
    species_counts,
    norm1_gain,
    norm1_bias,
    w_query,
    w_key,
    w_value,
    w_out,
    norm2_gain,
    norm2_bias,
    w_gate,
    w_up,
    w_down,
):
    own, width = tokens.shape
    group = lax.axis_size("tensor")
    member = lax.axis_index("tensor")
    n_dp = lax.axis_size("dp")
    me = lax.axis_index("dp")
    rest = LEN - own
    units = w_gate.shape[1]
    block = min(512, units)
    head_cols = w_query.shape[1]
    pairs = head_cols // LANES
    orders = orders_of(n_dp)
    n_pieces = n_dp // 2
    slots, pieces = slots_of([order[:-1] for order in orders], me % n_pieces)

    def from_member(values, step):
        return lax.ppermute(values, "tensor", [((i + step) % group, i) for i in range(group)])

    def rest_rows(values):
        parts = [from_member(values, step) for step in range(1, group)]
        return parts[0] if group == 2 else jnp.concatenate(parts, axis=0)

    def from_others(others):
        got = []
        for step in range(1, group):
            perm = [(i, (i + step) % group) for i in range(group)]
            got.append(lax.ppermute(others[(step - 1) * own : step * own], "tensor", perm))
        return got

    picked = species_ids[:, None] == jnp.arange(SPECIES, dtype=jnp.int32)[None, :]
    count = jnp.sum(jnp.where(picked, species_counts[None, :], 0), axis=1)
    inverse = 1000.0 / count.astype(F32)[0]
    sg_own = (cotangent.astype(F32) * inverse).astype(BF)

    in_own = norm_in(tokens, norm1_gain, norm1_bias)
    in_rest = rest_rows(in_own)
    sg_rest = rest_rows(sg_own)
    cos_tab, sin_tab = rope_tables(member * own)

    share = jnp.broadcast_to(inverse, (1, LANES))
    levels = [1 << level for level in range(n_dp.bit_length() - 1)]

    def hop(values):
        nonlocal share
        if levels:
            share = share + swap_dp(share, levels.pop(0), n_dp)
        values, share = lax.optimization_barrier((values, share))
        return values

    query, key, value = project(in_own, in_rest, cos_tab, sin_tab, w_query, w_key, w_value)
    query = hop(query)
    ctx_rest, lse_rest = attend(query, key, value, own, rest, own)
    branch_rest = hop(dot_nn(ctx_rest, w_out).astype(BF))
    got_branch = from_others(branch_rest)
    ctx_own, lse_own = attend(query, key, value, 0, own, own)
    ctx_own = hop(ctx_own)
    mixed, mid_own = norm_mid(tokens, ctx_own, w_out, norm2_gain, norm2_bias, got_branch)
    mid_rest = rest_rows(mid_own)
    mid_turned, mid = turn(mid_own, mid_rest, slots, n_pieces)
    while levels:
        mid = hop(mid)
    scale = n_dp / share[:, :1]

    chunks, found = [], {"scale": scale[0]}
    late_cols = min(256, head_cols)
    late_fits = width * late_cols // 1024 >= 16 * n_pieces and w_out.shape[0] % (16 * n_pieces) == 0

    def send_off(keep, send, which, folds, shapes):
        chunks.append(Chunk(keep, send, orders[which], (which, folds, shapes)))

    def work():
        kept = None
        gate_slots = slots
        for index in range(units // block):
            down_order = DOWN_ORDERS[index % len(DOWN_ORDERS)]
            *kept, down_keep, down_send, a_keep, a_send, b_keep, b_send = feed_forward(
                index, block, n_pieces, down_order, gate_slots, mid, mid_turned, sg_own, sg_rest, w_gate, w_up, w_down, kept
            )
            folds = [(0, width, 0, index * block, 0)]
            send_off(down_keep, down_send, down_order, folds, [("down", w_down.shape)])
            for at, (keep, send) in enumerate(((a_keep, a_send), (b_keep, b_send))):
                row, col = at * width // 2, index * block
                folds = [(0, block, 0, row, col), (block, 2 * block, 1, row, col)]
                send_off(keep, send, WIDE_ORDERS[at], folds, [("gate", w_gate.shape), ("up", w_up.shape)])
            gate_slots, kept = yield (gate_slots, kept)
        hidden, d_gate, d_up = kept
        d_mid_part, d_mid_rest = d_mid_parts(d_gate, d_up, w_gate, w_up, own)
        d_mid_part, d_mid_rest, hidden = yield (d_mid_part, d_mid_rest, hidden)
        got = from_others(d_mid_rest)
        out_part = dot_nn(hidden, w_down)
        got_out = from_others(out_part[own:].astype(BF))
        got, out_part = lax.optimization_barrier((got, out_part))
        d_mixed, d_branch_own, sums2 = norm_backward(
            "mid", mixed, sg_own, norm2_gain, scale, d_mid_part, got
        )
        d_branch_rest = rest_rows(d_branch_own)
        lse = jnp.concatenate([lse_own, lse_rest], axis=2)
        output = mixed + out_part[:own]
        for part in got_out:
            output = output + part.astype(F32)
        output = output.astype(BF)
        d_branch_rest, found["output"] = lax.optimization_barrier((d_branch_rest, output))
        d_context, delta, out_keep, out_send = out_back(
            pieces, n_pieces, d_branch_own, d_branch_rest, ctx_own, ctx_rest, w_out
        )
        if late_fits:
            send_off(out_keep, out_send, OUT_ORDER, [(0, width, 0, 0, 0)], [("out", w_out.shape)])
        else:
            grad = jnp.concatenate([out_keep, out_send], axis=0)
            found["out"] = lax.psum(grad, "dp").astype(F32) * scale
        backs = ()
        for at in range(head_cols // late_cols):
            d_context, *backs = yield (d_context, *backs)
            per = late_cols // LANES
            backs = attend_back(
                query, key, value, d_context, delta, lse, cos_tab, sin_tab, at * per, per, backs
            )
            if late_fits:
                rows = width * late_cols // 1024
                lanes = [i * late_cols for i in range(width // rows + 1)]
                folds = [(lanes[i], lanes[i + 1], 0, i * rows, at * late_cols) for i in range(width // rows)]
                late_orders = LATE_ORDERS[at % len(LATE_ORDERS)]
                late = late_grads(pieces, n_pieces, late_orders, in_own, in_rest, backs, at, late_cols)
                for which, name in enumerate(("query", "key", "value")):
                    target = [(name, w_query.shape)]
                    send_off(late[2 * which], late[2 * which + 1], late_orders[which], folds, target)
        if not late_fits:
            for name, d in zip(("query", "key", "value"), backs):
                grad = dot_tn(in_own, d[:own]) + dot_tn(in_rest, d[own:])
                found[name] = lax.psum(grad.astype(BF), "dp").astype(F32) * scale
        backs = yield (*backs,)
        d_in_part = sum(dot_nt(d, w) for d, w in zip(backs, (w_query, w_key, w_value)))
        got = from_others(d_in_part[own:].astype(BF))
        found["input"], sums1 = norm_backward("in", tokens, d_mixed, norm1_gain, scale, d_in_part, got)
        vectors = jnp.concatenate([sums1, sums2], axis=0)
        total = vectors
        for step in range(1, group):
            total = total + from_member(vectors, step)
        for level in range(n_dp.bit_length() - 1):
            (total,) = yield (total,)
            total = total + swap_dp(total, 1 << level, n_dp)
        found["vectors"] = total * scale

    in_rounds(work(), chunks, n_dp, found, lambda done: place(done, pieces, found["scale"], found))
    vectors = found["vectors"]
    return (
        found["output"],
        found["input"],
        vectors[0],
        vectors[1],
        found["query"],
        found["key"],
        found["value"],
        found["out"],
        vectors[2],
        vectors[3],
        found["gate"],
        found["up"],
        found["down"],
    )


def solution(mesh):
    split = P(("dp", "tensor"), None)
    cols = P(None, "tensor")
    rows = P("tensor", None)
    return jax.shard_map(
        per_device,
        mesh=mesh,
        in_specs=(split, split, P("dp"), P(), P(), P(), cols, cols, cols, rows, P(), P(), cols, cols, rows),
        out_specs=(split, split, P(), P(), cols, cols, cols, rows, P(), P(), cols, cols, rows),
        check_vma=False,
    )
```

```python
import functools
import math

import jax
import jax.numpy as jnp
from jax import lax
from jax.experimental import pallas as pl
from jax.experimental.pallas import tpu as pltpu
from jax.sharding import PartitionSpec as P

HD = 64
LEN = 1024
SPECIES = 850
LANES = 128

eps_norm = 1e-05
BF = jnp.bfloat16
F32 = jnp.float32
EXP_SCALE = HD ** (-0.5) * math.log2(math.e)
MIB = 1024 * 1024
BACK_TILE = 512
WIDE_ORDERS = (2, 4)
DOWN_ORDERS = (0, 0, 0, 0)
OUT_ORDER = 2
LATE_ORDERS = ((0, 2, 4), (0, 2, 4))
EARLY = (1, 1, 1, 1, 1, 1, 1, 1, 1, 1, 1, 0, 0, 0, 0, 0, 0, 0, 0, 0, 0, 0, 0, 0, 0, 0, 0, 0, 0, 0)
LIMITS = (384, 384, 384, 384, 384, 384, 384, 384, 384, 384, 384, 384, 384, 384, 384, 384, 384, 384, 384, 384, 384, 384, 384, 384, 384, 384, 384, 384, 384, 384)
RANKS = (0, 0, 0, 0, 0, 0, 0, 1, 1, 1, 1, 1, 1, 1, 1, 1, 1, 1, 1, 1, 1, 1, 1, 1, 1, 1, 1, 1, 1, 1)


def shape_of(dims, dtype):
    return jax.ShapeDtypeStruct(dims, dtype)


def dot_nn(left, right):
    return lax.dot_general(left, right, (((1,), (0,)), ((), ())), preferred_element_type=F32)


def dot_nt(left, right):
    return lax.dot_general(left, right, (((1,), (1,)), ((), ())), preferred_element_type=F32)


def dot_tn(left, right):
    return lax.dot_general(left, right, (((0,), (0,)), ((), ())), preferred_element_type=F32)


def row_norm(values):
    center = values - jnp.mean(values, axis=-1, keepdims=True)
    inv_std = lax.rsqrt(jnp.mean(center * center, axis=-1, keepdims=True) + eps_norm)
    return (center * inv_std, inv_std)


def norm_back(upstream, normed, inv_std, gain_vec):
    scaled_up = upstream * gain_vec
    mean_one = jnp.mean(scaled_up, axis=-1, keepdims=True)
    mean_two = jnp.mean(scaled_up * normed, axis=-1, keepdims=True)
    return inv_std * (scaled_up - mean_one - normed * mean_two)


def params(mib):
    return pltpu.CompilerParams(vmem_limit_bytes=mib * MIB)


def swap_halves(values):
    width = values.shape[1]
    lane = lax.broadcasted_iota(jnp.int32, values.shape, 1) % HD
    ahead = pltpu.roll(values, width - HD // 2, 1)
    behind = pltpu.roll(values, HD // 2, 1)
    return jnp.where(lane < HD // 2, ahead, behind)


def rope_tables(start):
    half_dim = HD // 2
    inv_freq = 1.0 / 10000.0 ** (jnp.arange(half_dim, dtype=F32) * 2.0 / HD)
    position = (start + jnp.arange(LEN, dtype=jnp.int32)) % LEN
    angles = position.astype(F32)[:, None] * inv_freq[None, :]
    cos_tab, sin_tab = jnp.cos(angles), jnp.sin(angles)
    return (
        jnp.concatenate([cos_tab] * 4, axis=1),
        jnp.concatenate([-sin_tab, sin_tab] * 2, axis=1),
    )


def project_kernel(own_ref, rest_ref, cos_ref, sin_ref, wq_ref, wk_ref, wv_ref, q_ref, k_ref, v_ref):
    own = own_ref.shape[0]
    for rows, x_ref in ((slice(0, own), own_ref), (slice(own, LEN), rest_ref)):
        x = x_ref[...]
        cos_tab, sin_tab = cos_ref[rows, :], sin_ref[rows, :]
        for w_ref, out_ref, factor in ((wq_ref, q_ref, EXP_SCALE), (wk_ref, k_ref, 1.0)):
            lin = dot_nn(x, w_ref[...]) * factor
            for at in range(0, lin.shape[1], LANES):
                part = lin[:, at : at + LANES]
                turned = part * cos_tab + swap_halves(part) * sin_tab
                out_ref[rows, at : at + LANES] = turned.astype(BF)
        v_ref[rows, :] = dot_nn(x, wv_ref[...]).astype(BF)


def project(own, rest, cos_tab, sin_tab, w_query, w_key, w_value):
    cols = w_query.shape[1]
    block = min(256, cols)
    width = own.shape[1]
    whole = lambda a: pl.BlockSpec(a.shape, lambda i: (0, 0))
    w_spec = pl.BlockSpec((width, block), lambda i: (0, i))
    o_spec = pl.BlockSpec((LEN, block), lambda i: (0, i))
    return pl.pallas_call(
        project_kernel,
        grid=(cols // block,),
        in_specs=[whole(own), whole(rest), whole(cos_tab), whole(sin_tab), w_spec, w_spec, w_spec],
        out_specs=[o_spec] * 3,
        out_shape=[shape_of((LEN, cols), BF)] * 3,
        compiler_params=params(28),
        name="project",
    )(own, rest, cos_tab, sin_tab, w_query, w_key, w_value)


def head_only(values, head):
    lane = lax.broadcasted_iota(jnp.int32, values.shape, 1)
    return jnp.where(lane // HD == head, values, jnp.zeros_like(values))


def attend_kernel(q_ref, k_ref, v_ref, ctx_ref, lse_ref):
    k = k_ref[...]
    v_turned = v_ref[...].T
    parts = []
    for head in range(2):
        scores = dot_nt(k, head_only(q_ref[...], head))
        top = jnp.max(scores, axis=0, keepdims=True)
        exps = jnp.exp2(scores - top)
        total = jnp.sum(exps, axis=0, keepdims=True)
        mix = dot_nn(v_turned[head * HD : (head + 1) * HD, :], exps.astype(BF))
        parts.append(mix * (1.0 / total))
        lse_ref[0, head : head + 1, :] = top + jnp.log2(total)
    ctx_ref[...] = jnp.concatenate(parts, axis=0).T.astype(BF)


def attend(query, key, value, first, count, tile):
    cols = query.shape[1]
    pairs = cols // LANES
    whole = pl.BlockSpec((LEN, LANES), lambda p, i: (0, p))
    return pl.pallas_call(
        attend_kernel,
        grid=(pairs, count // tile),
        in_specs=[pl.BlockSpec((tile, LANES), lambda p, i: (first // tile + i, p)), whole, whole],
        out_specs=[
            pl.BlockSpec((tile, LANES), lambda p, i: (i, p)),
            pl.BlockSpec((1, 2, tile), lambda p, i: (p, 0, i)),
        ],
        out_shape=[shape_of((count, cols), BF), shape_of((pairs, 2, count), F32)],
        compiler_params=params(24),
        name="attend",
    )(query, key, value)


def attend_back_kernel(
    tile, q_ref, k_ref, v_ref, d_ref, delta_ref, lse_ref, cos_ref, sin_ref, *refs,
):
    dq_ref, dk_ref, dv_ref, dk_sum, dv_sum = refs[-5:]
    k, v = k_ref[...], v_ref[...]
    k_turned = k.T

    def unrotate(grads, rows, scale):
        grads = grads * scale
        return (grads * cos_ref[rows, :] - swap_halves(grads) * sin_ref[rows, :]).astype(BF)

    dk_sum[...] = jnp.zeros_like(dk_sum)
    dv_sum[...] = jnp.zeros_like(dv_sum)

    def step(i, carry):
        at = pl.multiple_of(i * tile, tile)
        rows = pl.ds(at, tile)
        q, d = q_ref[rows, :], d_ref[rows, :]
        parts = []
        for head in range(2):
            q_head, d_head = head_only(q, head), head_only(d, head)
            scores = dot_nt(k, q_head)
            probs = jnp.exp2(scores - lse_ref[0, head : head + 1, rows])
            d_probs = dot_nt(v, d_head)
            d_scores = (probs * (d_probs - delta_ref[0, head : head + 1, rows])).astype(BF)
            dv_sum[...] += dot_nn(probs.astype(BF), d_head)
            dk_sum[...] += dot_nn(d_scores, q_head)
            parts.append(dot_nn(k_turned[head * HD : (head + 1) * HD, :], d_scores))
        dq_ref[rows, :] = unrotate(jnp.concatenate(parts, axis=0).T, rows, HD ** (-0.5))
        return carry

    lax.fori_loop(0, LEN // tile, step, 0)
    everything = slice(0, LEN)
    dk_ref[...] = unrotate(dk_sum[...], everything, HD ** (-0.5) / EXP_SCALE)
    dv_ref[...] = dv_sum[...].astype(BF)


def attend_back(query, key, value, d_context, delta, lse, cos_tab, sin_tab, first, pairs, given):
    cols = query.shape[1]
    strip = pl.BlockSpec((LEN, LANES), lambda p: (0, first + p))
    table = pl.BlockSpec((LEN, LANES), lambda p: (0, 0))
    sums = pl.BlockSpec((1, 2, LEN), lambda p: (first + p, 0, 0))
    given = list(given)
    return pl.pallas_call(
        functools.partial(attend_back_kernel, BACK_TILE),
        grid=(pairs,),
        in_specs=[strip] * 4 + [sums, sums, table, table] + [pl.BlockSpec(memory_space=pl.ANY)] * len(given),
        out_specs=[strip] * 3,
        out_shape=[shape_of((LEN, cols), BF)] * 3,
        scratch_shapes=[pltpu.VMEM((LEN, LANES), F32)] * 2,
        input_output_aliases={8 + i: i for i in range(len(given))},
        compiler_params=params(24),
        name="attend_back",
    )(query, key, value, d_context, delta, lse, cos_tab, sin_tab, *given)


def whole_of(array):
    return pl.BlockSpec(array.shape, lambda *_: (0,) * array.ndim)


def norm_in_kernel(tok_ref, gain_ref, bias_ref, out_ref):
    normed, _ = row_norm(tok_ref[...].astype(F32))
    out_ref[...] = (normed * gain_ref[...] + bias_ref[...]).astype(BF)


def norm_in(tokens, gain, bias):
    return pl.pallas_call(
        norm_in_kernel,
        out_shape=shape_of(tokens.shape, BF),
        compiler_params=params(16),
        name="norm_in",
    )(tokens, gain[None, :], bias[None, :])


def norm_mid_kernel(n_got, tok_ref, ctx_ref, w_ref, gain_ref, bias_ref, *refs):
    mixed_ref, mid_ref = refs[n_got:]
    mixed = tok_ref[...].astype(F32) + dot_nn(ctx_ref[...], w_ref[...])
    for got_ref in refs[:n_got]:
        mixed = mixed + got_ref[...].astype(F32)
    mixed_ref[...] = mixed
    normed, _ = row_norm(mixed)
    mid_ref[...] = (normed * gain_ref[...] + bias_ref[...]).astype(BF)


def norm_mid(tokens, ctx, w_out, gain, bias, got):
    return pl.pallas_call(
        functools.partial(norm_mid_kernel, len(got)),
        out_shape=[shape_of(tokens.shape, F32), shape_of(tokens.shape, BF)],
        compiler_params=params(24),
        name="norm_mid",
    )(tokens, ctx, w_out, gain[None, :], bias[None, :], *got)


def norm_back_kernel(n_got, kind, x_ref, base_ref, gain_ref, scale_ref, part_ref, *refs):
    upstream = part_ref[...]
    for got_ref in refs[:n_got]:
        upstream = upstream + got_ref[...].astype(F32)
    normed, inv_std = row_norm(x_ref[...].astype(F32))
    result = base_ref[...].astype(F32) + norm_back(upstream, normed, inv_std, gain_ref[...])
    sums_ref = refs[-1]
    sums_ref[0:1, :] = jnp.sum(upstream * normed, axis=0, keepdims=True)
    sums_ref[1:2, :] = jnp.sum(upstream, axis=0, keepdims=True)
    if kind == "mid":
        refs[n_got][...] = result
        refs[n_got + 1][...] = result.astype(BF)
    else:
        refs[n_got][...] = result * scale_ref[...]


def norm_backward(kind, values, base, gain, scale, part, got):
    rows, width = values.shape
    outs = [shape_of((rows, width), F32)]
    if kind == "mid":
        outs.append(shape_of((rows, width), BF))
    outs.append(shape_of((2, width), F32))
    own = pl.BlockSpec((rows, width), lambda i: (0, 0))
    vector = pl.BlockSpec((1, width), lambda i: (0, 0))
    return pl.pallas_call(
        functools.partial(norm_back_kernel, len(got), kind),
        grid=(1,),
        in_specs=[own, own, vector, pl.BlockSpec((1, 1), lambda i: (0, 0)), own] + [own] * len(got),
        out_specs=[pl.BlockSpec(o.shape, lambda i: (0, 0)) for o in outs],
        out_shape=outs,
        compiler_params=params(32),
        name="norm_back",
    )(values, base, gain[None, :], scale, part, *got)


def turn_kernel(n_pieces, slots_ref, own_ref, rest_ref, turned_ref, both_ref):
    at = 0
    for x_ref in (own_ref, rest_ref):
        count = x_ref.shape[0]
        both_ref[at : at + count, :] = x_ref[...]
        turned = x_ref[...].T
        half = turned.shape[0] // 2
        piece = half // n_pieces
        for first, which in zip((0, half), WIDE_ORDERS):
            for p in range(n_pieces):
                to = pl.multiple_of(first + slots_ref[which, p] * piece, piece)
                turned_ref[pl.ds(to, piece), at : at + count] = turned[
                    first + p * piece : first + (p + 1) * piece, :
                ]
        at += count


def turn(own, rest, slots, n_pieces):
    width = own.shape[1]
    return pl.pallas_call(
        functools.partial(turn_kernel, n_pieces),
        grid_spec=pltpu.PrefetchScalarGridSpec(
            num_scalar_prefetch=1,
            grid=(1,),
            in_specs=[whole_of(own), whole_of(rest)],
            out_specs=[pl.BlockSpec((width, LEN), lambda i, s: (0, 0)), pl.BlockSpec((LEN, width), lambda i, s: (0, 0))],
        ),
        out_shape=[shape_of((width, LEN), BF), shape_of((LEN, width), BF)],
        compiler_params=params(24),
        name="turn",
    )(slots, own, rest)


def ff_kernel(n_pieces, down_order, slots_ref, nm_ref, nt_ref, so_ref, sr_ref, wg_ref, wu_ref, wd_ref, *refs):
    hid_ref, dg_ref, du_ref, *grad_refs, ht_ref = refs[-10:]
    block = wg_ref.shape[1]
    own = so_ref.shape[0]
    tile = min(512, own)
    piece = block // n_pieces

    def forward(first, s_ref):
        def body(i, carry):
            here = pl.ds(pl.multiple_of(i * tile, tile), tile)
            rows = pl.ds(pl.multiple_of(first + i * tile, tile), tile)
            x = nm_ref[rows, :]
            gate = dot_nn(x, wg_ref[...])
            up = dot_nn(x, wu_ref[...])
            d_hidden = dot_nt(s_ref[here, :], wd_ref[...])
            sig = 1.0 / (1.0 + jnp.exp(-gate))
            silu = gate * sig
            hidden = (silu * up).astype(BF)
            hid_ref[rows, :] = hidden
            turned = hidden.T
            for p in range(n_pieces):
                to = pl.multiple_of(slots_ref[down_order, p] * piece, piece)
                ht_ref[pl.ds(to, piece), rows] = turned[p * piece : (p + 1) * piece, :]
            dg_ref[rows, :] = (d_hidden * up * (sig * (1.0 + gate * (1.0 - sig)))).astype(BF)
            du_ref[rows, :] = (d_hidden * silu).astype(BF)
            return carry

        lax.fori_loop(0, s_ref.shape[0] // tile, body, 0)

    forward(0, so_ref)
    forward(own, sr_ref)
    step = min(256, block // 2)
    for half in range(2):
        out_ref = grad_refs[half]
        for at in range(0, block // 2, step):
            rows = slice(half * block // 2 + at, half * block // 2 + at + step)
            down = dot_nn(ht_ref[rows, :own], so_ref[...]) + dot_nn(ht_ref[rows, own:], sr_ref[...])
            out_ref[at : at + step, :] = down.astype(BF)
    quarter = nt_ref.shape[0] // 4
    for at in range(4):
        left = nt_ref[at * quarter : (at + 1) * quarter, :]
        out_ref = grad_refs[2 + at]
        out_ref[:, :block] = dot_nn(left, dg_ref[...]).astype(BF)
        out_ref[:, block:] = dot_nn(left, du_ref[...]).astype(BF)


def d_mid_kernel(dg_ref, du_ref, wg_ref, wu_ref, own_ref, rest_ref, sum_ref):
    step = pl.program_id(0)
    own = own_ref.shape[0]
    tile = min(512, own)
    for at in range(0, LEN, tile):
        rows = slice(at, at + tile)
        part = dot_nt(dg_ref[rows, :], wg_ref[...]) + dot_nt(du_ref[rows, :], wu_ref[...])

        @pl.when(step == 0)
        def _():
            sum_ref[rows, :] = part

        @pl.when(step > 0)
        def _():
            sum_ref[rows, :] += part

    @pl.when(step == pl.num_programs(0) - 1)
    def _():
        own_ref[...] = sum_ref[:own, :]
        rest_ref[...] = sum_ref[own:, :].astype(BF)


def d_mid_parts(d_gate, d_up, w_gate, w_up, own):
    width, units = w_gate.shape
    block = min(512, units)
    d_spec = pl.BlockSpec((LEN, block), lambda i: (0, i))
    w_spec = pl.BlockSpec((width, block), lambda i: (0, i))
    return pl.pallas_call(
        d_mid_kernel,
        grid=(units // block,),
        in_specs=[d_spec, d_spec, w_spec, w_spec],
        out_specs=[pl.BlockSpec((own, width), lambda i: (0, 0)), pl.BlockSpec((LEN - own, width), lambda i: (0, 0))],
        out_shape=[shape_of((own, width), F32), shape_of((LEN - own, width), BF)],
        scratch_shapes=[pltpu.VMEM((LEN, width), F32)],
        compiler_params=params(56),
        name="d_mid",
    )(d_gate, d_up, w_gate, w_up)


def feed_forward(index, block, n_pieces, down_order, slots, nm, nt, sg_own, sg_rest, w_gate, w_up, w_down, kept):
    width, units = w_gate.shape
    cols = pl.BlockSpec((width, block), lambda i, s: (0, index))
    kept_spec = pl.BlockSpec((LEN, block), lambda i, s: (0, index))
    grads = [(block // 2, width)] * 2 + [(width // 4, 2 * block)] * 4
    previous = list(kept) if kept is not None else []
    in_vmem = pl.BlockSpec(memory_space=pltpu.VMEM)
    return pl.pallas_call(
        functools.partial(ff_kernel, n_pieces, down_order),
        grid_spec=pltpu.PrefetchScalarGridSpec(
            num_scalar_prefetch=1,
            grid=(1,),
            in_specs=[in_vmem] * 4
            + [cols, cols, pl.BlockSpec((block, width), lambda i, s: (index, 0))]
            + [pl.BlockSpec(memory_space=pl.ANY)] * len(previous),
            out_specs=[kept_spec] * 3 + [pl.BlockSpec(dims, lambda i, s: (0, 0)) for dims in grads],
            scratch_shapes=[pltpu.VMEM((block, LEN), BF)],
        ),
        out_shape=[shape_of((LEN, units), BF)] * 3 + [shape_of(dims, BF) for dims in grads],
        input_output_aliases={8 + i: i for i in range(len(previous))},
        compiler_params=params(34),
        name="feed_forward",
    )(slots, nm, nt, sg_own, sg_rest, w_gate, w_up, w_down, *previous)


def orders_of(n_dp):
    bits = [1 << i for i in range(n_dp.bit_length() - 1)]
    if len(bits) < 4:
        return [bits] * 6
    x, y, z = bits[:3]
    return [o + bits[3:] for o in ([x, y, z], [x, z, y], [y, x, z], [y, z, x], [z, x, y], [z, y, x])]


def masks_of(order):
    size = 1 << len(order)
    masks = []
    for slot in range(size):
        mask = 0
        for level, bit in enumerate(order):
            if slot >> (len(order) - 1 - level) & 1:
                mask |= bit
        masks.append(mask)
    return masks


def slots_of(orders, me):
    table = []
    for order in orders:
        inverse = [0] * (1 << len(order))
        for slot, mask in enumerate(masks_of(order)):
            inverse[mask] = slot
        table.append(inverse)
    size = len(table[0])
    here = jnp.arange(size, dtype=jnp.int32) ^ me
    match = here[:, None] == jnp.arange(size, dtype=jnp.int32)[None, :]
    pieces = jnp.array([masks_of(order) for order in orders], jnp.int32) ^ me
    slots = jnp.stack([jnp.sum(jnp.where(match, jnp.array(t, jnp.int32)[None, :], 0), axis=1) for t in table])
    return (slots, pieces)


def swap_dp(values, bit, n_dp):
    return lax.ppermute(values, "dp", [(i, i ^ bit) for i in range(n_dp)])


class Part:
    def __init__(self, buffer, first, rows):
        self.buffer, self.first, self.rows = buffer, first, rows

    def value(self):
        if self.rows == self.buffer.shape[0]:
            return self.buffer
        return self.buffer[self.first : self.first + self.rows]


def phases_of(order):
    return [("halve", b) for b in order[:-1]] + [("swap", order[-1])] + [("double", b) for b in order[-2::-1]]


class Chunk:
    def __init__(self, keep, send, order, target):
        self.phases, self.target = phases_of(order), target
        self.keep, self.send = keep, send
        self.at, self.parts = 0, []

    @property
    def open(self):
        return self.at < len(self.phases)

    @property
    def left(self):
        return len(self.phases) - self.at

    @property
    def bit(self):
        return self.phases[self.at][1]

    def outgoing(self):
        if self.phases[self.at][0] == "double":
            return [part.value() for part in self.parts]
        return [self.send]

    def next_rows(self):
        if self.phases[self.at][0] == "double":
            return sum(part.rows for part in self.parts)
        return self.send.shape[0]

    def incoming(self, buffer, first):
        rows = self.next_rows()
        kind = self.phases[self.at][0]
        self.at += 1
        got = Part(buffer, first, rows)
        if kind == "double":
            self.parts = self.parts + [got]
            return
        total = self.keep + got.value()
        following = self.phases[self.at][0]
        if following == "halve":
            self.keep, self.send = total[: rows // 2], total[rows // 2 :]
        elif following == "swap":
            self.keep = self.send = total
        else:
            self.parts = [Part(total, 0, rows)]


def in_rounds(work, chunks, n_dp, found, place):
    placing, recent = [], set()
    wanted = next(work)
    before = ({}, {})
    now = 1

    def finish(picks, got):
        for bit, members in picks.items():
            at = 0
            for chunk in members:
                rows = chunk.next_rows()
                chunk.incoming(got[bit], at)
                at += rows
                if not chunk.open:
                    placing.append(chunk)

    while wanted is not None or before[0] or placing or any(c.open for c in chunks):
        early, limit, rank = (row[min(now, len(row) - 1)] for row in (EARLY, LIMITS, RANKS))
        if early and before[0]:
            got, wanted = lax.optimization_barrier((before[1], wanted))
            finish(before[0], got)
            before = ({}, {})
        picks, loads = {}, {}
        busy = [chunk for members in before[0].values() for chunk in members]
        free = [chunk for chunk in chunks if chunk.open and chunk not in busy]
        free.sort(key=lambda c: (0, -c.left, -c.next_rows(), c.next_rows())[rank])
        for chunk in free:
            bit, rows = chunk.bit, chunk.next_rows()
            cost = rows * (2 if bit == n_dp // 2 else 1)
            if loads.get(bit, 0) and loads[bit] + cost > limit:
                continue
            loads[bit] = loads.get(bit, 0) + cost
            picks.setdefault(bit, []).append(chunk)
        sends = {}
        for bit in sorted(picks):
            picks[bit].sort(key=lambda c: -c.next_rows())
            parts = [part for chunk in picks[bit] for part in chunk.outgoing()]
            sends[bit] = parts[0] if len(parts) == 1 else jnp.concatenate(parts, axis=0)
        buffers = [c.parts[-1].buffer for c in placing]
        placed = {name: found[name] for name in recent}
        held = (before[1], sends, buffers, placed, wanted)
        got, _, buffers, placed, wanted = lax.optimization_barrier(held)
        found.update(placed)
        recent = set()
        taken = {bit: swap_dp(values, bit, n_dp) for bit, values in sends.items()}
        finished, placing = placing, []
        finish(before[0], got)
        for chunk, buffer in zip(finished, buffers):
            chunk.parts[-1].buffer = buffer
        while finished:
            recent.update(place(finished[:4]))
            finished = finished[4:]
        if wanted is not None:
            try:
                wanted = work.send(wanted)
            except StopIteration:
                wanted = None
        before = (picks, taken)
        now += 1


def place_kernel(plans, n_outs, n_given, slots_ref, scale_ref, *refs):
    outs, wide_ref, sems = refs[-n_outs - 2 : -2], refs[-2], refs[-1]
    scale = scale_ref[0]
    copies = []
    at_ref = done_rows = 0
    for which, counts, folds in plans:
        slot = 0
        for count in counts:
            part_ref = refs[at_ref]
            at_ref += 1
            piece = part_ref.shape[0] // count
            for j in range(count):
                here = slice(done_rows, done_rows + piece)
                done_rows += piece
                wide_ref[here, :] = part_ref[j * piece : (j + 1) * piece, :].astype(F32) * scale
                place_at = slots_ref[which, slot]
                for lane, end, out, row, col in folds:
                    to = pl.multiple_of(row + place_at * piece, piece)
                    copy = pltpu.make_async_copy(
                        wide_ref.at[here, lane:end],
                        outs[out].at[pl.ds(to, piece), col : col + end - lane],
                        sems.at[len(copies)],
                    )
                    copy.start()
                    copies.append(copy)
                slot += 1
    for copy in copies:
        copy.wait()


def place(chunks, pieces, scale, found):
    names, plans, parts = {}, [], []
    n_pieces = pieces.shape[1]
    for chunk in chunks:
        which, folds, shapes = chunk.target
        for name, dims in shapes:
            names.setdefault(name, dims)
        order = list(names)
        mine = [order.index(name) for name, _ in shapes]
        piece = sum(part.rows for part in chunk.parts) // n_pieces
        counts = tuple(part.rows // piece for part in chunk.parts)
        plans.append((which, counts, tuple((l, e, mine[o], r, c) for l, e, o, r, c in folds)))
        parts += chunk.parts
    given = [name for name in names if name in found]
    at = {name: i for i, name in enumerate(names)}
    index_map = lambda block: (lambda i, *_: block)
    anywhere = pl.BlockSpec(memory_space=pl.ANY)
    rows_all = sum(part.rows for part in parts)
    results = pl.pallas_call(
        lambda s, k, *refs: place_kernel(plans, len(names), len(given), s, k, *refs),
        grid_spec=pltpu.PrefetchScalarGridSpec(
            num_scalar_prefetch=2,
            grid=(1,),
            in_specs=[pl.BlockSpec((p.rows, 1024), index_map((p.first // p.rows, 0))) for p in parts]
            + [anywhere] * len(given),
            out_specs=[anywhere] * len(names),
            scratch_shapes=[
                pltpu.VMEM((rows_all, 1024), F32),
                pltpu.SemaphoreType.DMA((n_pieces * sum(len(plan[2]) for plan in plans),)),
            ],
        ),
        out_shape=[shape_of(dims, F32) for dims in names.values()],
        input_output_aliases={2 + len(parts) + i: at[name] for i, name in enumerate(given)},
        compiler_params=params(4 + 8 * rows_all * 1024 // MIB),
        name="place",
    )(pieces, scale, *[part.buffer for part in parts], *[found[name] for name in given])
    found.update(zip(names, results))
    return list(names)


def late_kernel(n_pieces, table, slots_ref, own_ref, rest_ref, dq_ref, dk_ref, dv_ref, *refs):
    out_refs, all_ref = refs[:-1], refs[-1]
    own, width = own_ref.shape
    cols = dq_ref.shape[1]
    rows = all_ref.shape[0]
    piece = rows // n_pieces
    for which, d_ref in enumerate((dq_ref, dk_ref, dv_ref)):
        for i in range(width // rows):
            lanes = slice(i * rows, (i + 1) * rows)
            grads = dot_tn(own_ref[:, lanes], d_ref[:own, :]) + dot_tn(rest_ref[:, lanes], d_ref[own:, :])
            all_ref[:, i * cols : (i + 1) * cols] = grads.astype(BF)
        to_slots(n_pieces, slots_ref, table[which], piece, all_ref, out_refs[2 * which], out_refs[2 * which + 1])


def to_slots(n_pieces, pieces_ref, which, piece, all_ref, keep_ref, send_ref):
    for slot in range(n_pieces):
        at = pl.multiple_of(pieces_ref[which, slot] * piece, piece)
        out_ref = keep_ref if slot < n_pieces // 2 else send_ref
        to = slot % (n_pieces // 2) * piece
        out_ref[to : to + piece, :] = all_ref[pl.ds(at, piece), :]


def late_grads(pieces, n_pieces, table, own, rest, backs, at, cols):
    width = own.shape[1]
    rows = width * cols // 1024
    strip = pl.BlockSpec((LEN, cols), lambda i, s: (0, at))
    return pl.pallas_call(
        functools.partial(late_kernel, n_pieces, table),
        grid_spec=pltpu.PrefetchScalarGridSpec(
            num_scalar_prefetch=1,
            grid=(1,),
            in_specs=[whole_of(own), whole_of(rest)] + [strip] * 3,
            out_specs=[pl.BlockSpec((rows // 2, 1024), lambda i, s: (0, 0))] * 6,
            scratch_shapes=[pltpu.VMEM((rows, 1024), BF)],
        ),
        out_shape=[shape_of((rows // 2, 1024), BF)] * 6,
        compiler_params=params(24),
        name="late_grads",
    )(pieces, own, rest, *backs)


def out_back_kernel(n_pieces, pieces_ref, do_ref, dr_ref, co_ref, cr_ref, w_ref, dc_ref, delta_ref, keep_ref, send_ref, all_ref):
    own = do_ref.shape[0]
    at = 0
    for d_ref, c_ref in ((do_ref, co_ref), (dr_ref, cr_ref)):
        count = d_ref.shape[0]
        d_context = dot_nt(d_ref[...], w_ref[...]).astype(BF)
        dc_ref[at : at + count, :] = d_context
        both = (d_context.astype(F32) * c_ref[...].astype(F32)).T
        for head in range(both.shape[0] // HD):
            sums = jnp.sum(both[head * HD : (head + 1) * HD, :], axis=0, keepdims=True)
            delta_ref[head // 2, head % 2 : head % 2 + 1, at : at + count] = sums
        at += count
    rows = all_ref.shape[0]
    step = min(256, rows)
    for first in range(0, rows, step):
        lanes = slice(first, first + step)
        grads = dot_tn(co_ref[:, lanes], do_ref[...]) + dot_tn(cr_ref[:, lanes], dr_ref[...])
        all_ref[lanes, :] = grads.astype(BF)
    if rows % (16 * n_pieces) == 0:
        to_slots(n_pieces, pieces_ref, OUT_ORDER, rows // n_pieces, all_ref, keep_ref, send_ref)
    else:
        keep_ref[...] = all_ref[: rows // 2, :]
        send_ref[...] = all_ref[rows // 2 :, :]


def out_back(pieces, n_pieces, d_own, d_rest, ctx_own, ctx_rest, w_out):
    cols, width = w_out.shape
    pairs = cols // LANES
    outs = [shape_of((LEN, cols), BF), shape_of((pairs, 2, LEN), F32)] + [shape_of((cols // 2, width), BF)] * 2
    arrays = (d_own, d_rest, ctx_own, ctx_rest, w_out)
    return pl.pallas_call(
        functools.partial(out_back_kernel, n_pieces),
        grid_spec=pltpu.PrefetchScalarGridSpec(
            num_scalar_prefetch=1,
            grid=(1,),
            in_specs=[whole_of(a) for a in arrays],
            out_specs=[whole_of(o) for o in outs],
            scratch_shapes=[pltpu.VMEM((cols, width), BF)],
        ),
        out_shape=outs,
        compiler_params=params(32),
        name="out_back",
    )(pieces, *arrays)


def per_device(
    tokens,
    cotangent,
    species_ids,
    species_counts,
    norm1_gain,
    norm1_bias,
    w_query,
    w_key,
    w_value,
    w_out,
    norm2_gain,
    norm2_bias,
    w_gate,
    w_up,
    w_down,
):
    own, width = tokens.shape
    group = lax.axis_size("tensor")
    member = lax.axis_index("tensor")
    n_dp = lax.axis_size("dp")
    me = lax.axis_index("dp")
    rest = LEN - own
    units = w_gate.shape[1]
    block = min(512, units)
    head_cols = w_query.shape[1]
    pairs = head_cols // LANES
    orders = orders_of(n_dp)
    n_pieces = n_dp // 2
    slots, pieces = slots_of([order[:-1] for order in orders], me % n_pieces)

    def from_member(values, step):
        return lax.ppermute(values, "tensor", [((i + step) % group, i) for i in range(group)])

    def rest_rows(values):
        parts = [from_member(values, step) for step in range(1, group)]
        return parts[0] if group == 2 else jnp.concatenate(parts, axis=0)

    def from_others(others):
        got = []
        for step in range(1, group):
            perm = [(i, (i + step) % group) for i in range(group)]
            got.append(lax.ppermute(others[(step - 1) * own : step * own], "tensor", perm))
        return got

    picked = species_ids[:, None] == jnp.arange(SPECIES, dtype=jnp.int32)[None, :]
    count = jnp.sum(jnp.where(picked, species_counts[None, :], 0), axis=1)
    inverse = 1000.0 / count.astype(F32)[0]
    sg_own = (cotangent.astype(F32) * inverse).astype(BF)

    in_own = norm_in(tokens, norm1_gain, norm1_bias)
    in_rest = rest_rows(in_own)
    sg_rest = rest_rows(sg_own)
    cos_tab, sin_tab = rope_tables(member * own)

    share = jnp.broadcast_to(inverse, (1, LANES))
    levels = [1 << level for level in range(n_dp.bit_length() - 1)]

    def hop(values):
        nonlocal share
        if levels:
            share = share + swap_dp(share, levels.pop(0), n_dp)
        values, share = lax.optimization_barrier((values, share))
        return values

    query, key, value = project(in_own, in_rest, cos_tab, sin_tab, w_query, w_key, w_value)
    query = hop(query)
    ctx_rest, lse_rest = attend(query, key, value, own, rest, own)
    branch_rest = hop(dot_nn(ctx_rest, w_out).astype(BF))
    got_branch = from_others(branch_rest)
    ctx_own, lse_own = attend(query, key, value, 0, own, own)
    ctx_own = hop(ctx_own)
    mixed, mid_own = norm_mid(tokens, ctx_own, w_out, norm2_gain, norm2_bias, got_branch)
    mid_rest = rest_rows(mid_own)
    mid_turned, mid = turn(mid_own, mid_rest, slots, n_pieces)
    while levels:
        mid = hop(mid)
    scale = n_dp / share[:, :1]

    chunks, found = [], {"scale": scale[0]}
    late_cols = min(256, head_cols)
    late_fits = width * late_cols // 1024 >= 16 * n_pieces and w_out.shape[0] % (16 * n_pieces) == 0

    def send_off(keep, send, which, folds, shapes):
        chunks.append(Chunk(keep, send, orders[which], (which, folds, shapes)))

    def work():
        kept = None
        gate_slots = slots
        for index in range(units // block):
            down_order = DOWN_ORDERS[index % len(DOWN_ORDERS)]
            *kept, down_keep, down_send, a_keep, a_send, b_keep, b_send = feed_forward(
                index, block, n_pieces, down_order, gate_slots, mid, mid_turned, sg_own, sg_rest, w_gate, w_up, w_down, kept
            )
            folds = [(0, width, 0, index * block, 0)]
            send_off(down_keep, down_send, down_order, folds, [("down", w_down.shape)])
            for at, (keep, send) in enumerate(((a_keep, a_send), (b_keep, b_send))):
                row, col = at * width // 2, index * block
                folds = [(0, block, 0, row, col), (block, 2 * block, 1, row, col)]
                send_off(keep, send, WIDE_ORDERS[at], folds, [("gate", w_gate.shape), ("up", w_up.shape)])
            gate_slots, kept = yield (gate_slots, kept)
        hidden, d_gate, d_up = kept
        d_mid_part, d_mid_rest = d_mid_parts(d_gate, d_up, w_gate, w_up, own)
        d_mid_part, d_mid_rest, hidden = yield (d_mid_part, d_mid_rest, hidden)
        got = from_others(d_mid_rest)
        out_part = dot_nn(hidden, w_down)
        got_out = from_others(out_part[own:].astype(BF))
        got, out_part = lax.optimization_barrier((got, out_part))
        d_mixed, d_branch_own, sums2 = norm_backward(
            "mid", mixed, sg_own, norm2_gain, scale, d_mid_part, got
        )
        d_branch_rest = rest_rows(d_branch_own)
        lse = jnp.concatenate([lse_own, lse_rest], axis=2)
        output = mixed + out_part[:own]
        for part in got_out:
            output = output + part.astype(F32)
        output = output.astype(BF)
        d_branch_rest, found["output"] = lax.optimization_barrier((d_branch_rest, output))
        d_context, delta, out_keep, out_send = out_back(
            pieces, n_pieces, d_branch_own, d_branch_rest, ctx_own, ctx_rest, w_out
        )
        if late_fits:
            send_off(out_keep, out_send, OUT_ORDER, [(0, width, 0, 0, 0)], [("out", w_out.shape)])
        else:
            grad = jnp.concatenate([out_keep, out_send], axis=0)
            found["out"] = lax.psum(grad, "dp").astype(F32) * scale
        backs = ()
        for at in range(head_cols // late_cols):
            d_context, *backs = yield (d_context, *backs)
            per = late_cols // LANES
            backs = attend_back(
                query, key, value, d_context, delta, lse, cos_tab, sin_tab, at * per, per, backs
            )
            if late_fits:
                rows = width * late_cols // 1024
                lanes = [i * late_cols for i in range(width // rows + 1)]
                folds = [(lanes[i], lanes[i + 1], 0, i * rows, at * late_cols) for i in range(width // rows)]
                late_orders = LATE_ORDERS[at % len(LATE_ORDERS)]
                late = late_grads(pieces, n_pieces, late_orders, in_own, in_rest, backs, at, late_cols)
                for which, name in enumerate(("query", "key", "value")):
                    target = [(name, w_query.shape)]
                    send_off(late[2 * which], late[2 * which + 1], late_orders[which], folds, target)
        if not late_fits:
            for name, d in zip(("query", "key", "value"), backs):
                grad = dot_tn(in_own, d[:own]) + dot_tn(in_rest, d[own:])
                found[name] = lax.psum(grad.astype(BF), "dp").astype(F32) * scale
        backs = yield (*backs,)
        d_in_part = sum(dot_nt(d, w) for d, w in zip(backs, (w_query, w_key, w_value)))
        got = from_others(d_in_part[own:].astype(BF))
        found["input"], sums1 = norm_backward("in", tokens, d_mixed, norm1_gain, scale, d_in_part, got)
        vectors = jnp.concatenate([sums1, sums2], axis=0)
        total = vectors
        for step in range(1, group):
            total = total + from_member(vectors, step)
        for level in range(n_dp.bit_length() - 1):
            (total,) = yield (total,)
            total = total + swap_dp(total, 1 << level, n_dp)
        found["vectors"] = total * scale

    in_rounds(work(), chunks, n_dp, found, lambda done: place(done, pieces, found["scale"], found))
    vectors = found["vectors"]
    return (
        found["output"],
        found["input"],
        vectors[0],
        vectors[1],
        found["query"],
        found["key"],
        found["value"],
        found["out"],
        vectors[2],
        vectors[3],
        found["gate"],
        found["up"],
        found["down"],
    )


def solution(mesh):
    split = P(("dp", "tensor"), None)
    cols = P(None, "tensor")
    rows = P("tensor", None)
    return jax.shard_map(
        per_device,
        mesh=mesh,
        in_specs=(split, split, P("dp"), P(), P(), P(), cols, cols, cols, rows, P(), P(), cols, cols, rows),
        out_specs=(split, split, P(), P(), cols, cols, cols, rows, P(), P(), cols, cols, rows),
        check_vma=False,
    )
```
